32 devices in a mesh: dp: 4 (over x, core), seq: 8 (over z, y).
Axes of the slice: x: 2, y: 2, z: 4, core: 2. Of those that a mesh axis runs over, the one named last changes fastest.
Arguments:
- tokens: bfloat16 [4, 2048, 1536], P('dp', 'seq'), may hold values from -6 to 6
- segment_ids: int32 [4, 2048], P('dp', 'seq'), may hold values from 0 to 4, as said below
- pre_gain: bfloat16 [1536], P(('dp', 'seq')), may hold values from 0.5 to 1.5
- in_weight: bfloat16 [1536, 6448], P(('dp', 'seq')), may hold values from -0.15625 to 0.15625
- conv_weight: bfloat16 [3328, 4], P(('dp', 'seq')), may hold values from -3 to 3
- conv_bias: bfloat16 [3328], P(('dp', 'seq')), may hold values from -3 to 3
- dt_bias: float32 [48], replicated, may hold values from -5 to -1
- a_log: float32 [48], replicated, may hold values from -10 to 0
- skip_gain: float32 [48], replicated, may hold values from 0.5 to 1.5
- norm_gain: bfloat16 [3072], P(('dp', 'seq')), may hold values from 0.5 to 1.5
- out_weight: bfloat16 [3072, 1536], P(('dp', 'seq')), may hold values from -0.109375 to 0.109375
- cotangent: bfloat16 [4, 2048, 1536], P('dp', 'seq'), may hold values from -6 to 6
Outputs:
- mixed: bfloat16 [4, 2048, 1536], P('dp', 'seq')
- tokens_grad: float32 [4, 2048, 1536], P('dp', 'seq')
- pre_gain_grad: float32 [1536], P(('dp', 'seq'))
- in_weight_grad: float32 [1536, 6448], P(('dp', 'seq'))
- conv_weight_grad: float32 [3328, 4], P(('dp', 'seq'))
- conv_bias_grad: float32 [3328], P(('dp', 'seq'))
- dt_bias_grad: float32 [48], replicated
- a_log_grad: float32 [48], replicated
- skip_grad: float32 [48], replicated
- norm_gain_grad: float32 [3072], P(('dp', 'seq'))
- out_weight_grad: float32 [3072, 1536], P(('dp', 'seq'))
The draws below stay inside these ranges and needn't reach their ends.
Inputs may be any that keep to these rules, and one draw needn't show every extreme that they name: `segment_ids`: along each sequence the ids never fall, start at 0 and rise by one at each document start.
All inputs are finite; a program needn't handle non-finite values.
Results may differ from the reference program's by a relative error of at most 0.0069.
Values may be sent and summed in bfloat16 or wider, within the bound.
A program may use at most 256 MiB of HBM per device.

```python
import jax
import jax.numpy as jnp
from jax import lax

D = 1536
HEADS = 48
HEADDIM = 64
STATE = 128
CONVW = 4
GROUP = 256
INNER = 3072
XBC = 3328
PROJ = 6448
TOK_DEV = 256
LENGTH = 2048
SEQS = 4
N_SEQ = 8


def draw_segment_ids(key, part):
    key = jax.random.fold_in(key, 11)
    order_key, seq_key = jax.random.split(key)
    spanning = jax.random.permutation(order_key, SEQS) < SEQS // 2

    def one_sequence(subkey, whole_span):
        subkeys = jax.random.split(subkey, 5)
        inside_start = jax.random.randint(subkeys[0], (), 2, TOK_DEV)
        edge_start = TOK_DEV * jax.random.randint(subkeys[4], (), 1, N_SEQ)
        long_start = jnp.where(whole_span, inside_start, edge_start)
        early_cut = jax.random.randint(subkeys[1], (), 1, long_start)
        late_cut = LENGTH - TOK_DEV + jax.random.randint(subkeys[2], (), 1, TOK_DEV - 1)
        final_cut = late_cut + jax.random.randint(subkeys[3], (), 1, LENGTH - late_cut)
        places = jnp.arange(LENGTH)
        return (places >= early_cut).astype(jnp.int32) + (places >= long_start).astype(jnp.int32) + (places >= late_cut).astype(jnp.int32) + (places >= final_cut).astype(jnp.int32)
    return jax.vmap(one_sequence)(jax.random.split(seq_key, SEQS), spanning)


def steps_of(stream_key, extent, cuts, smallest, largest):
    level, own = 1.0, jax.random.fold_in(stream_key, 6)
    for axis_at, shards_of in cuts:
        heights = jnp.exp(jax.random.uniform(jax.random.fold_in(own, axis_at), (shards_of,), jnp.float32, smallest / len(cuts), largest / len(cuts)))
        level = level * jnp.repeat(heights, extent[axis_at] // shards_of).reshape([-1 if axis == axis_at else 1 for axis in range(len(extent))])
    return level


def bell_draw(key, dims, deviation, most, cuts=(), dtype=jnp.bfloat16):
    level = steps_of(key, dims, cuts, -0.22, 0.18) if cuts else 1.0
    entries = jax.random.normal(key, dims, jnp.float32) * deviation * level
    return jnp.minimum(jnp.maximum(entries, -most), most).astype(dtype)


def setup_inputs(seed: int = 0) -> dict:
    splits = jax.random.split(jax.random.key(seed), 13)
    tokens = bell_draw(splits[0], (SEQS, LENGTH, D), 1.0, 6.0, ((0, 4), (1, 8)))
    segment_ids = draw_segment_ids(jax.random.fold_in(splits[12], 71), 0)
    pre_gain = jnp.clip(1.0 + 0.1 * jax.random.normal(splits[2], (D,), jnp.float32), 0.5, 1.5).astype(jnp.bfloat16)
    in_weight = bell_draw(splits[3], (D, PROJ), D ** -0.5, 0.15625, ((0, 32),))
    conv_weight = bell_draw(splits[4], (XBC, CONVW), CONVW ** -0.5, 3.0, ((0, 32),))
    conv_bias = bell_draw(splits[5], (XBC,), 0.5, 3.0, ((0, 32),))
    dt_bias = jnp.clip(jax.random.uniform(splits[6], (HEADS,), jnp.float32, -5.0, -1.0), -5.0, -1.0)
    a_log = jnp.clip(jax.random.uniform(splits[7], (HEADS,), jnp.float32, -10.0, 0.0), -10.0, 0.0)
    skip_gain = jnp.clip(jax.random.uniform(splits[8], (HEADS,), jnp.float32, 0.5, 1.5), 0.5, 1.5)
    norm_gain = jnp.clip(1.0 + 0.1 * jax.random.normal(splits[9], (INNER,), jnp.float32), 0.5, 1.5).astype(jnp.bfloat16)
    out_weight = bell_draw(splits[10], (INNER, D), INNER ** -0.5, 0.109375, ((0, 32),))
    cotangent = bell_draw(splits[11], (SEQS, LENGTH, D), 1.0, 6.0, ((0, 4), (1, 8)))
    return dict(tokens=tokens, segment_ids=segment_ids, pre_gain=pre_gain, in_weight=in_weight, conv_weight=conv_weight, conv_bias=conv_bias, dt_bias=dt_bias, a_log=a_log, skip_gain=skip_gain, norm_gain=norm_gain, out_weight=out_weight, cotangent=cotangent)


HIGHEST = lax.Precision.HIGHEST
EPSILON = 1e-05

@jax.custom_vjp
def low(v):
    return lax.optimization_barrier(v.astype(jnp.bfloat16)).astype(jnp.float32)

@jax.custom_vjp
def low_back(v):
    return v

def low_keep(v):
    return (low(v), None)

def low_pass(kept, grad):
    return (grad,)

def back_keep(v):
    return (v, None)

def back_low(kept, grad):
    return (low(grad),)
low.defvjp(low_keep, low_pass)
low_back.defvjp(back_keep, back_low)

def rms_scale(values, gain):
    return values * lax.rsqrt(lax.optimization_barrier(jnp.mean(values * values, axis=-1, keepdims=True)) + EPSILON) * gain

def group_math(state, before, heads_x, b_rows, c_rows, steps_dt, log_decay, doc_ids):
    length = doc_ids.shape[0]
    running = jnp.cumsum(log_decay, axis=0)
    causal = jnp.arange(length)[:, None] >= jnp.arange(length)[None, :]
    linked = ((doc_ids[:, None] == doc_ids[None, :]) & causal)[:, :, None]
    gaps = running[:, None, :] - running[None, :, :]
    decays = jnp.exp(jnp.where(linked, gaps, 0.0)) * linked
    scores = jnp.dot(c_rows, b_rows.T, precision=HIGHEST)
    mixing = decays * scores[:, :, None] * steps_dt[None, :, :]
    inside = jnp.einsum('tsh,shp->thp', mixing, heads_x, precision=HIGHEST)
    alive = (doc_ids == before)[:, None]
    enter = jnp.exp(running) * alive
    carried = jnp.einsum('tn,hpn->thp', c_rows, state, precision=HIGHEST) * enter[:, :, None]
    last_id = doc_ids[length - 1]
    kept = (doc_ids == last_id)[:, None]
    weights_end = jnp.exp(running[length - 1][None, :] - running) * kept * steps_dt
    fresh = jnp.einsum('sh,shp,sn->hpn', weights_end, heads_x, b_rows, precision=HIGHEST)
    passed = jnp.exp(running[length - 1]) * (last_id == before)
    return (inside + carried, fresh + passed[:, None, None] * state)

def convolve(conv_in, doc_ids, kernel, offset_bias):
    length = doc_ids.shape[0]
    margin = CONVW - 1
    padded = jnp.concatenate([jnp.zeros((margin, XBC), jnp.float32), conv_in])
    padded_ids = jnp.concatenate([jnp.full((margin,), -1, jnp.int32), doc_ids])
    total = offset_bias
    for offset in range(CONVW):
        taps = padded[offset:offset + length]
        linked = (padded_ids[offset:offset + length] == doc_ids)[:, None]
        total = total + jnp.where(linked, taps, 0.0) * kernel[:, offset]
    return jax.nn.silu(total)

def mixer(activated, dt_raw, dt_shift, decay_log, doc_ids):
    length = doc_ids.shape[0]
    count = length // GROUP
    heads_x = activated[:, :INNER].reshape(length, HEADS, HEADDIM)
    b_rows = activated[:, INNER:INNER + STATE]
    c_rows = activated[:, INNER + STATE:]
    steps_dt = jax.nn.softplus(dt_raw + dt_shift)
    log_decay = -jnp.exp(decay_log) * steps_dt
    befores = jnp.concatenate([doc_ids[:1], doc_ids.reshape(count, GROUP)[:-1, GROUP - 1]])

    def step(state, item):
        out, new_state = group_math(state, *item)
        return (new_state, out)
    items = (befores, heads_x.reshape(count, GROUP, HEADS, HEADDIM), b_rows.reshape(count, GROUP, STATE), c_rows.reshape(count, GROUP, STATE), steps_dt.reshape(count, GROUP, HEADS), log_decay.reshape(count, GROUP, HEADS), doc_ids.reshape(count, GROUP))
    _, outs = lax.scan(jax.checkpoint(step), jnp.zeros((HEADS, HEADDIM, STATE), jnp.float32), items)
    return (outs.reshape(length, HEADS, HEADDIM), heads_x)

def block(tok_rows, doc_ids, pre_gain, in_weight, conv_weight, conv_bias, dt_bias, a_log, skip_gain, norm_gain, out_weight):
    normed = low(rms_scale(tok_rows, pre_gain))
    projected = low_back(jnp.dot(normed, in_weight, precision=HIGHEST))
    gate_z = projected[:, :INNER]
    conv_in = projected[:, INNER:INNER + XBC]
    dt_raw = projected[:, INNER + XBC:]
    activated = convolve(conv_in, doc_ids, conv_weight, conv_bias)
    local_y, heads_x = mixer(activated, dt_raw, dt_bias, a_log, doc_ids)
    mixer_out = (local_y + skip_gain[:, None] * heads_x).reshape(-1, INNER)
    gated = low(rms_scale(mixer_out * jax.nn.silu(gate_z), norm_gain))
    return tok_rows + low_back(jnp.dot(gated, out_weight, precision=HIGHEST))

def reference(tokens, segment_ids, pre_gain, in_weight, conv_weight, conv_bias, dt_bias, a_log, skip_gain, norm_gain, out_weight, cotangent):
    weights = (pre_gain.astype(jnp.float32), in_weight.astype(jnp.float32), conv_weight.astype(jnp.float32), conv_bias.astype(jnp.float32), dt_bias, a_log, skip_gain, norm_gain.astype(jnp.float32), out_weight.astype(jnp.float32))

    def one_sequence(totals, item):
        tok_seq, doc_ids, cot_seq = item

        def forward(tok_rows, *params):
            return block(tok_rows, doc_ids, *params)
        result, backward = jax.vjp(forward, tok_seq.astype(jnp.float32), *weights)
        grads = backward(cot_seq.astype(jnp.float32))
        totals = tuple((total + grad for total, grad in zip(totals, grads[1:])))
        return (totals, (result.astype(jnp.bfloat16), grads[0]))
    zeros = tuple((jnp.zeros_like(weight) for weight in weights))
    totals, (mixed, tokens_grad) = lax.scan(one_sequence, zeros, (tokens, segment_ids, cotangent))
    return (mixed, tokens_grad, totals[0], totals[1], totals[2], totals[3], totals[4], totals[5], totals[6], totals[7], totals[8])
```

```python
import functools

import jax
import jax.numpy as jnp
from jax import lax
from jax.experimental import pallas as pl
from jax.experimental.pallas import tpu as pltpu
from jax.sharding import Mesh
from jax.sharding import PartitionSpec as P

HEADS = 48
HEADDIM = 64
STATE = 128
CONVW = 4
GROUP = 256
INNER = 3072
XBC = 3328


HIGHEST = lax.Precision.HIGHEST
EPSILON = 1e-05


def passed_along(block, axis, distance):
    devices = range(lax.axis_size(axis))
    route = [(i - distance, i) for i in devices if i - distance in devices]
    return lax.ppermute(block, axis, route)


def shortened(shard):
    return jax.tree.map(lambda a: a.astype(jnp.bfloat16) if a.dtype == jnp.float32 else a, shard)


def rms_scale(values, gain):
    return values * lax.rsqrt(jnp.mean(values * values, axis=-1, keepdims=True) + EPSILON) * gain


def gating(values, gates, gain):
    return rms_scale(values * jax.nn.silu(gates), gain)


def group_math(state, before, heads_x, b_rows, c_rows, steps_dt, log_decay, doc_ids):
    length = doc_ids.shape[0]
    running = jnp.cumsum(log_decay, axis=0)
    causal = jnp.arange(length)[:, None] >= jnp.arange(length)[None, :]
    linked = ((doc_ids[:, None] == doc_ids[None, :]) & causal)[:, :, None]
    gaps = running[:, None, :] - running[None, :, :]
    decays = jnp.exp(jnp.where(linked, gaps, 0.0)) * linked
    scores = jnp.dot(c_rows, b_rows.T, precision=HIGHEST)
    mixing = decays * scores[:, :, None] * steps_dt[None, :, :]
    inside = jnp.einsum("tsh,shp->thp", mixing, heads_x, precision=HIGHEST)
    alive = (doc_ids == before)[:, None]
    enter = jnp.exp(running) * alive
    carried = jnp.einsum("tn,hpn->thp", c_rows, state, precision=HIGHEST) * enter[:, :, None]
    last_id = doc_ids[length - 1]
    kept = (doc_ids == last_id)[:, None]
    weights_end = jnp.exp(running[length - 1][None, :] - running) * kept * steps_dt
    fresh = jnp.einsum("sh,shp,sn->hpn", weights_end, heads_x, b_rows, precision=HIGHEST)
    passed = jnp.exp(running[length - 1]) * (last_id == before)
    return (inside + carried, fresh + passed[:, None, None] * state)


def contract_rows(left, right):
    return lax.dot_general(
        left, right, (((0,), (0,)), ((), ())), preferred_element_type=jnp.float32
    )


def contract_cols(left, right):
    return lax.dot_general(
        left, right, (((1,), (1,)), ((), ())), preferred_element_type=jnp.float32
    )


def whole_body(
    tokens,
    segment_ids,
    pre_gain,
    in_weight,
    conv_weight,
    conv_bias,
    dt_bias,
    a_log,
    skip_gain,
    norm_gain,
    out_weight,
    cotangent,
):
    tok_rows = tokens[0].astype(jnp.float32)
    doc_ids = segment_ids[0]
    length = doc_ids.shape[0]
    margin = CONVW - 1
    count = length // GROUP
    shards = (pre_gain, in_weight, conv_weight, conv_bias, norm_gain, out_weight)
    gathered = (
        lax.all_gather(shards[0], ("dp", "seq"), axis=0, tiled=True),
        lax.all_gather(shards[1], ("dp", "seq"), axis=0, tiled=True),
        lax.all_gather(shards[2], ("dp", "seq"), axis=0, tiled=True),
        lax.all_gather(shards[3], ("dp", "seq"), axis=0, tiled=True),
        lax.all_gather(shards[4], ("dp", "seq"), axis=0, tiled=True),
        lax.all_gather(shards[5], ("dp", "seq"), axis=0, tiled=True),
    )
    normed, pre_back = jax.vjp(rms_scale, tok_rows, gathered[0].astype(jnp.float32))
    normed_low = normed.astype(jnp.bfloat16)
    projected = jnp.dot(normed_low, gathered[1], preferred_element_type=jnp.float32)
    gate_z = projected[:, :INNER]
    conv_in = projected[:, INNER : INNER + XBC]
    dt_raw = projected[:, INNER + XBC :]
    halo_rows, halo_ids = (
        passed_along(conv_in[length - margin :].astype(jnp.bfloat16), "seq", 1).astype(jnp.float32),
        passed_along(
            doc_ids[length - margin :].astype(jnp.float32).astype(jnp.bfloat16), "seq", 1
        ).astype(jnp.float32),
    )
    ext_ids = jnp.concatenate([halo_ids.astype(jnp.int32), doc_ids])
    prior_id = ext_ids[margin - 1]

    def convolve(extended, kernel, offset_bias):
        total = offset_bias
        for offset in range(CONVW):
            taps = extended[offset : offset + length]
            linked = (ext_ids[offset : offset + length] == doc_ids)[:, None]
            total = total + jnp.where(linked, taps, 0.0) * kernel[:, offset]
        return jax.nn.silu(total)

    activated, conv_back = jax.vjp(
        convolve,
        jnp.concatenate([halo_rows, conv_in]),
        gathered[2].astype(jnp.float32),
        gathered[3].astype(jnp.float32),
    )

    def zero_state(acts_in, raw_in, shift_in, rate_in):
        heads_x = acts_in[:, :INNER].reshape(length, HEADS, HEADDIM)
        b_rows = acts_in[:, INNER : INNER + STATE]
        c_rows = acts_in[:, INNER + STATE :]
        steps_dt = jax.nn.softplus(raw_in + shift_in)
        log_decay = -jnp.exp(rate_in) * steps_dt
        befores = jnp.concatenate([prior_id[None], doc_ids.reshape(count, GROUP)[:-1, GROUP - 1]])

        def step(state, item):
            out, new_state = group_math(state, *item)
            return (new_state, out)

        items = (
            befores,
            heads_x.reshape(count, GROUP, HEADS, HEADDIM),
            b_rows.reshape(count, GROUP, STATE),
            c_rows.reshape(count, GROUP, STATE),
            steps_dt.reshape(count, GROUP, HEADS),
            log_decay.reshape(count, GROUP, HEADS),
            doc_ids.reshape(count, GROUP),
        )
        final, outs = lax.scan(step, jnp.zeros((HEADS, HEADDIM, STATE), jnp.float32), items)
        factor = jnp.exp(jnp.sum(log_decay, axis=0)) * (doc_ids[length - 1] == prior_id)
        return (outs.reshape(length, HEADS, HEADDIM), factor, final)

    def incoming(acts_in, raw_in, shift_in, rate_in, start_state):
        steps_dt = jax.nn.softplus(raw_in + shift_in)
        running = jnp.cumsum(-jnp.exp(rate_in) * steps_dt, axis=0)
        factor = jnp.exp(running) * (doc_ids == prior_id)[:, None]
        c_rows = acts_in[:, INNER + STATE :]
        return (
            jnp.einsum("tn,hpn->thp", c_rows, start_state, precision=HIGHEST) * factor[:, :, None]
        )

    (local_y, factor, local_state), zero_back = jax.vjp(
        zero_state, activated, dt_raw, dt_bias, a_log
    )
    identity = (jnp.ones((HEADS,), jnp.float32), jnp.zeros((HEADS, HEADDIM, STATE), jnp.float32))

    def forward_turn(index, carry_state):
        return passed_along(factor[:, None, None] * carry_state + local_state, "seq", 1)

    start_state = lax.fori_loop(0, lax.axis_size("seq") - 1, forward_turn, identity[1])
    carried_y, in_back = jax.vjp(incoming, activated, dt_raw, dt_bias, a_log, start_state)
    heads_x = activated[:, :INNER].reshape(length, HEADS, HEADDIM)
    mixer_out = (local_y + carried_y + skip_gain[:, None] * heads_x).reshape(length, INNER)
    gated, gate_back = jax.vjp(gating, mixer_out, gate_z, gathered[4].astype(jnp.float32))
    gated_low = gated.astype(jnp.bfloat16)
    branch = jnp.dot(gated_low, gathered[5], preferred_element_type=jnp.float32)
    mixed = (tok_rows + branch).astype(jnp.bfloat16)
    again = (
        lax.all_gather(shards[0], ("dp", "seq"), axis=0, tiled=True),
        lax.all_gather(shards[1], ("dp", "seq"), axis=0, tiled=True),
        lax.all_gather(shards[2], ("dp", "seq"), axis=0, tiled=True),
        lax.all_gather(shards[3], ("dp", "seq"), axis=0, tiled=True),
        lax.all_gather(shards[4], ("dp", "seq"), axis=0, tiled=True),
        lax.all_gather(shards[5], ("dp", "seq"), axis=0, tiled=True),
    )
    grad_out = cotangent[0]
    grad_gated = contract_cols(grad_out, again[5])
    out_weight_grad = contract_rows(gated_low, grad_out)
    grad_mixer, grad_gate_z, norm_gain_grad = gate_back(grad_gated)
    grad_heads = grad_mixer.reshape(length, HEADS, HEADDIM)
    skip_grad = jnp.sum(grad_heads * heads_x, axis=(0, 2))
    acts_one, raw_one, shift_one, rate_one, start_grad = in_back(grad_heads)

    def backward_turn(index, carry_grad):
        return passed_along(start_grad + factor[:, None, None] * carry_grad, "seq", -1)

    end_grad = lax.fori_loop(0, lax.axis_size("seq") - 1, backward_turn, identity[1])
    factor_grad = jnp.sum(end_grad * start_state, axis=(1, 2))
    acts_two, raw_two, shift_two, rate_two = zero_back((grad_heads, factor_grad, end_grad))
    skip_part = (grad_heads * skip_gain[:, None]).reshape(length, INNER)
    grad_acts = (
        acts_one
        + acts_two
        + jnp.concatenate([skip_part, jnp.zeros((length, 2 * STATE), jnp.float32)], axis=1)
    )
    grad_ext, conv_weight_grad, conv_bias_grad = conv_back(grad_acts)
    back_rows = passed_along(shortened(grad_ext[:margin]), "seq", -1)
    grad_conv_in = grad_ext[margin:] + jnp.concatenate(
        [jnp.zeros((length - margin, XBC), jnp.float32), back_rows]
    )
    grad_projected = jnp.concatenate([grad_gate_z, grad_conv_in, raw_one + raw_two], axis=1).astype(
        jnp.bfloat16
    )
    in_weight_grad = contract_rows(normed_low, grad_projected)
    grad_normed = contract_cols(grad_projected, again[1])
    grad_tokens_norm, pre_gain_grad = pre_back(grad_normed)
    tokens_grad = grad_out.astype(jnp.float32) + grad_tokens_norm
    grad_parts = (
        pre_gain_grad,
        in_weight_grad,
        conv_weight_grad,
        conv_bias_grad,
        norm_gain_grad,
        out_weight_grad,
    )
    row_sums = (
        lax.psum_scatter(grad_parts[0], "dp", scatter_dimension=0, tiled=True),
        lax.psum_scatter(grad_parts[1], "dp", scatter_dimension=0, tiled=True),
        lax.psum_scatter(grad_parts[2], "dp", scatter_dimension=0, tiled=True),
        lax.psum_scatter(grad_parts[3], "dp", scatter_dimension=0, tiled=True),
        lax.psum_scatter(grad_parts[4], "dp", scatter_dimension=0, tiled=True),
        lax.psum_scatter(grad_parts[5], "dp", scatter_dimension=0, tiled=True),
    )
    sums = (
        lax.psum_scatter(row_sums[0], "seq", scatter_dimension=0, tiled=True),
        lax.psum_scatter(row_sums[1], "seq", scatter_dimension=0, tiled=True),
        lax.psum_scatter(row_sums[2], "seq", scatter_dimension=0, tiled=True),
        lax.psum_scatter(row_sums[3], "seq", scatter_dimension=0, tiled=True),
        lax.psum_scatter(row_sums[4], "seq", scatter_dimension=0, tiled=True),
        lax.psum_scatter(row_sums[5], "seq", scatter_dimension=0, tiled=True),
    )
    head_sums = lax.psum((shift_one + shift_two, rate_one + rate_two, skip_grad), ("dp", "seq"))
    return (
        mixed[None],
        tokens_grad[None],
        sums[0],
        sums[1],
        sums[2],
        sums[3],
        head_sums[0],
        head_sums[1],
        head_sums[2],
        sums[4],
        sums[5],
    )

AXES = ("dpo", "dpi", "so", "si")
MESH = pl.DeviceIdType.MESH
XCOLS = INNER // 4
CCOLS = XCOLS + 2 * STATE + 128
VMEM = pl.BlockSpec(memory_space=pltpu.VMEM)


class Wires:
    def __init__(self, send, recv):
        self.send, self.recv, self.used, self.pending = send, recv, 0, []

    def slot(self):
        self.used += 1
        return self.used - 1

    def copy(self, src, dst, slot, device):
        return pltpu.make_async_remote_copy(
            src_ref=src, dst_ref=dst, send_sem=self.send.at[slot], recv_sem=self.recv.at[slot],
            device_id=device, device_id_type=MESH,
        )

    def start(self, src, dst, slot, device, when=None):
        copy = self.copy(src, dst, slot, device)
        guarded(when, copy.start)
        self.pending.append((copy, when))

    def arrived(self, landing, slot, device, when=None):
        guarded(when, self.copy(landing, landing, slot, device).wait_recv)

    def finish(self):
        for copy, when in self.pending:
            guarded(when, copy.wait_send)
        self.pending = []


def guarded(when, action):
    if when is None:
        action()
    else:
        pl.when(when)(action)


def greet(here, size):
    a, c, b, s = here
    barrier = pltpu.get_barrier_semaphore()
    met = 0
    for rel in range(1, 4):
        pl.semaphore_signal(barrier, inc=1, device_id=member(here, rel), device_id_type=MESH)
        met = met + 1
    for k in range(1, size["so"]):
        pl.semaphore_signal(
            barrier, inc=1, device_id=(a, c, lax.rem(b + k, size["so"]), s), device_id_type=MESH
        )
        met = met + 1
    for k in range(1, size["dpo"]):
        pl.semaphore_signal(
            barrier, inc=1, device_id=(lax.rem(a + k, size["dpo"]), c, b, s), device_id_type=MESH
        )
        met = met + 1
    pl.semaphore_wait(barrier, met)


def member(here, rel):
    a, c, b, s = here
    return (a, c ^ (rel >> 1), b, s ^ (rel & 1))


def place():
    return tuple(lax.axis_index(name) for name in AXES)


def gather_kernel(size, wc_in, wg_in, wo_in, tok, cot, wc, wg, wo, toks, cots, send, recv, local):
    here = place()
    a, c, b, s = here
    n, nx = size["so"], size["dpo"]
    wires = Wires(send, recv)
    mine = 2 * c + s
    own = []

    def keep(src, dst, when=None):
        copy = pltpu.make_async_copy(src, dst, local.at[len(own)])
        guarded(when, copy.start)
        own.append((copy, when))

    greet(here, size)
    rows = wc_in.shape[1]
    span = 2 * rows
    shard = lambda w, cc, ss: w.at[a, cc, pl.ds(pl.multiple_of(span * b + rows * ss, 16), rows)]
    unit = lambda w, aa, bb: w.at[aa, :, pl.ds(pl.multiple_of(span * bb, 16), span)]
    halves = wo_in.shape[0]
    wo_half = lambda aa, bb, ss: wo.at[aa, bb // 2, pl.ds(pl.multiple_of(halves * ss, 16), halves)]
    holder = lax.rem(b, 2) == s
    first = {}
    for name, src, dst in (("c", wc_in, wc), ("g", wg_in, wg)):
        keep(src.at[mine], shard(dst, c, s))
        for rel in range(1, 4):
            _, cc, _, ss = member(here, rel)
            first[name, rel] = wires.slot()
            wires.start(src.at[2 * cc + ss], shard(dst, c, s), first[name, rel], member(here, rel))
        if name == "c":
            for key, src2, dst2 in (("t", tok, toks), ("k", cot, cots)):
                keep(src2, dst2.at[mine])
                for rel in range(1, 4):
                    first[key, rel] = wires.slot()
                    wires.start(src2, dst2.at[mine], first[key, rel], member(here, rel))
    keep(wo_in, wo_half(a, b, s), holder)
    first["o"] = wires.slot()
    wires.start(wo_in, wo_half(a, b, s), first["o"], member(here, 1), jnp.logical_not(holder))
    for copy, when in own:
        guarded(when, copy.wait)

    def spread(get, has):
        def cross(bb, when, slots):
            for k in range(1, nx):
                wires.start(get(a, bb), get(a, bb), slots[k], (lax.rem(a + k, nx), c, b, s), when)
        crossing = {}
        def note(bb, when):
            slots = {k: wires.slot() for k in range(1, nx)}
            cross(bb, when, slots)
            crossing[len(crossing)] = (bb, when, slots)
        up = {j: wires.slot() for j in range(1, n)}
        down = {j: wires.slot() for j in range(1, n)}
        above, below = (a, c, jnp.minimum(b + 1, n - 1), s), (a, c, jnp.maximum(b - 1, 0), s)
        wires.start(get(a, b), get(a, b), up[1], above, (b + 1 < n) & has(b))
        wires.start(get(a, b), get(a, b), down[1], below, (b > 0) & has(b))
        note(b, has(b))
        for j in range(1, n):
            for slots, origin, there, target, onward in (
                (up, jnp.maximum(b - j, 0), (b - j >= 0) & has(b + j), above, b + 1 < n),
                (down, jnp.minimum(b + j, n - 1), (b + j < n) & has(b + j), below, b > 0),
            ):
                wires.arrived(get(a, origin), slots[j], below, there)
                if j + 1 < n:
                    wires.start(get(a, origin), get(a, origin), slots[j + 1], target, there & onward)
                note(origin, there)
        return crossing

    def settle(get, crossing):
        for bb, when, slots in crossing.values():
            for k in range(1, nx):
                aa = lax.rem(a + nx - k, nx)
                wires.arrived(get(aa, bb), slots[k], (aa, c, b, s), when)

    always = lambda bb: jnp.bool_(True)
    crossings = []
    for name, w in (("c", wc), ("g", wg)):
        for rel in range(1, 4):
            _, cc, _, ss = member(here, rel)
            wires.arrived(shard(w, cc, ss), first[name, rel], member(here, rel))
        get = lambda aa, bb, w=w: unit(w, aa, bb)
        crossings.append((get, spread(get, always)))
    wires.arrived(wo_half(a, b, 1 - s), first["o"], member(here, 1), holder)
    get = lambda aa, bb: wo.at[aa, bb // 2]
    crossings.append((get, spread(get, lambda bb: lax.rem(bb, 2) == s)))
    for key, dst in (("t", toks), ("k", cots)):
        for rel in range(1, 4):
            _, cc, _, ss = member(here, rel)
            wires.arrived(dst.at[2 * cc + ss], first[key, rel], member(here, rel))
    for get, crossing in crossings:
        settle(get, crossing)
    wires.finish()


def gather(size, wc_in, wg_in, wo_in, tok, cot):
    rows = size["so"] * 2 * wc_in.shape[1]
    lead = (size["dpo"], 2, rows)
    shapes = (
        jax.ShapeDtypeStruct(lead + (wc_in.shape[2],), jnp.bfloat16),
        jax.ShapeDtypeStruct(lead + (wg_in.shape[2],), jnp.bfloat16),
        jax.ShapeDtypeStruct((size["dpo"], size["so"] // 2, 2 * wo_in.shape[0], wo_in.shape[1]), jnp.bfloat16),
        jax.ShapeDtypeStruct((4,) + tok.shape, jnp.bfloat16),
        jax.ShapeDtypeStruct((4,) + cot.shape, jnp.bfloat16),
    )
    slots = 13 + 3 * (2 * (size["so"] - 1) + (size["dpo"] - 1) * (2 * size["so"] - 1))
    return pl.pallas_call(
        functools.partial(gather_kernel, size),
        out_shape=shapes,
        in_specs=[pl.BlockSpec(memory_space=pl.ANY)] * 5,
        out_specs=[pl.BlockSpec(memory_space=pl.ANY)] * 5,
        scratch_shapes=[
            pltpu.SemaphoreType.DMA((slots,)),
            pltpu.SemaphoreType.DMA((slots,)),
            pltpu.SemaphoreType.DMA((5,)),
        ],
        compiler_params=pltpu.CompilerParams(collective_id=1, has_side_effects=True),
    )(wc_in, wg_in, wo_in, tok, cot)


def reduce_kernel(size, gc, gg, go, oc, og, oo, xc, xg, xo, zc, zg, zo, send, recv):
    here = place()
    a, c, b, s = here
    n, nx = size["so"], size["dpo"]
    wires = Wires(send, recv)
    greet(here, size)
    span = gc.shape[2] // n
    rows = span // 2
    halves = go.shape[2] // 2
    block = lambda bb: pl.ds(pl.multiple_of(span * bb, 16), span)
    always = lambda bb: None
    odd = lambda bb: lax.rem(bb, 2) == s
    parts = (
        (gc, xc, zc, lambda g, aa, bb: g.at[aa, :, block(bb)], always),
        (gg, xg, zg, lambda g, aa, bb: g.at[aa, :, block(bb)], always),
        (go, xo, zo, lambda g, aa, bb: g.at[aa, bb // 2], odd),
    )
    order = [k for k in range(1, n)] + [0]
    flown = {}
    for p, (g, x, z, get, has) in enumerate(parts):
        for k in order:
            bb = lax.rem(b + k, n)
            for h in range(1, nx):
                aa = lax.rem(a + h, nx)
                flown[p, k, h] = wires.slot()
                wires.start(get(g, aa, bb), x.at[h - 1, k], flown[p, k, h], (aa, c, b, s), has(bb))
    hops = {}
    for p, (g, x, z, get, has) in enumerate(parts):
        for k in order:
            bb = lax.rem(b + k, n)
            for h in range(1, nx):
                wires.arrived(x.at[h - 1, k], flown[p, k, h], (lax.rem(a + nx - h, nx), c, b, s), has(bb))

            def add():
                total = get(g, a, bb)[...].astype(jnp.float32)
                for h in range(1, nx):
                    total = total + x[h - 1, k].astype(jnp.float32)
                x[0, k] = total.astype(jnp.bfloat16)

            guarded(has(bb), add)
            if k > 0:
                hops[p, k] = wires.slot()
                wires.start(x.at[0, k], z.at[k - 1], hops[p, k], (a, c, bb, s), has(bb))
    back = {}
    for p, (g, x, z, get, has) in enumerate(parts):
        for k in range(1, n):
            wires.arrived(z.at[k - 1], hops[p, k], (a, c, lax.rem(b + n - k, n), s), has(b))

        def total():
            t = x[0, 0].astype(jnp.float32)
            for k in range(1, n):
                t = t + z[k - 1].astype(jnp.float32)
            return t

        if p < 2:
            out = (oc, og)[p]
            t = total().astype(jnp.bfloat16)
            z[0] = t
            mine = 2 * c + s
            out[mine] = z[0, c, pl.ds(pl.multiple_of(rows * s, 16), rows)]
            for rel in range(1, 4):
                _, cc, _, ss = member(here, rel)
                back[p, rel] = wires.slot()
                wires.start(
                    z.at[0, cc, pl.ds(pl.multiple_of(rows * ss, 16), rows)], out.at[mine],
                    back[p, rel], member(here, rel),
                )
        else:
            def close():
                z[0] = total().astype(jnp.bfloat16)
                oo[...] = z[0, pl.ds(pl.multiple_of(halves * s, 16), halves)]
            guarded(odd(b), close)
            back[p] = wires.slot()
            wires.start(
                z.at[0, pl.ds(pl.multiple_of(halves * (1 - s), 16), halves)], oo, back[p], member(here, 1), odd(b)
            )
    for p, out in ((0, oc), (1, og)):
        for rel in range(1, 4):
            _, cc, _, ss = member(here, rel)
            wires.arrived(out.at[2 * cc + ss], back[p, rel], member(here, rel))
    wires.arrived(oo, back[2], member(here, 1), jnp.logical_not(odd(b)))
    wires.finish()


def reduce(size, gc, gg, go):
    n, nx = size["so"], size["dpo"]
    span = gc.shape[2] // n
    rows = span // 2
    outs = (
        jax.ShapeDtypeStruct((4, rows, gc.shape[3]), jnp.bfloat16),
        jax.ShapeDtypeStruct((4, rows, gg.shape[3]), jnp.bfloat16),
        jax.ShapeDtypeStruct((go.shape[2] // 2, go.shape[3]), jnp.bfloat16),
    )
    units = [(2, span, gc.shape[3]), (2, span, gg.shape[3]), go.shape[2:]]
    slots = 3 * n * (nx - 1) + 3 * (n - 1) + 7
    return pl.pallas_call(
        functools.partial(reduce_kernel, size),
        out_shape=outs,
        in_specs=[VMEM] * 3,
        out_specs=[VMEM] * 3,
        scratch_shapes=[pltpu.VMEM((nx - 1, n) + tuple(u), jnp.bfloat16) for u in units]
        + [pltpu.VMEM((n - 1,) + tuple(u), jnp.bfloat16) for u in units]
        + [pltpu.SemaphoreType.DMA((slots,)), pltpu.SemaphoreType.DMA((slots,))],
        compiler_params=pltpu.CompilerParams(
            collective_id=2, has_side_effects=True, vmem_limit_bytes=56 * 2**20
        ),
    )(gc, gg, go)


def split_classes(full, size):
    lead = full.shape[:-1]
    w = full.shape[-1] // (size["dpo"] * 2 * size["so"])
    cut = full.reshape(lead + (size["dpo"], 2, size["so"] // 2, 2, w))
    k = len(lead)
    order = (k + 1, k + 3) + tuple(range(k)) + (k, k + 2, k + 4)
    return cut.transpose(order).reshape((2, 2) + lead + (full.shape[-1] // 4,))


def join_classes(parts, size):
    lead = parts.shape[2:-1]
    w = parts.shape[-1] // (size["dpo"] * size["so"] // 2)
    k = len(lead)
    cut = parts.reshape((2, 2) + lead + (size["dpo"], size["so"] // 2, w))
    order = tuple(range(2, 2 + k)) + (2 + k, 0, 3 + k, 1, 4 + k)
    return cut.transpose(order).reshape(lead + (parts.shape[-1] * 4,))


def fast_body(size, tokens, segment_ids, pre_gain, in_weight, conv_weight, conv_bias, dt_bias, a_log, skip_gain, norm_gain, out_weight, cotangent):
    here = place()
    a, c, b, s = here
    group = ("dpi", "si")
    hl = HEADS // 4
    margin = CONVW - 1
    tok, cot, doc = tokens[0], cotangent[0], segment_ids[0]
    own = doc.shape[0]
    rows = in_weight.shape[0]
    wg_in = split_classes(in_weight[:, :INNER], size).reshape(4, rows, XCOLS)
    wx_in = split_classes(in_weight[:, INNER : 2 * INNER], size).reshape(4, rows, XCOLS)
    bc_in = jnp.broadcast_to(in_weight[None, :, 2 * INNER : INNER + XBC], (4, rows, 2 * STATE))
    dt_in = split_classes(in_weight[:, INNER + XBC :], size).reshape(4, rows, hl)
    wc_in = jnp.concatenate([wx_in, bc_in, dt_in, jnp.zeros((4, rows, 128 - hl), jnp.bfloat16)], axis=2)
    wc, wg, wo, toks, cots = gather(size, wc_in, wg_in, out_weight, tok, cot)
    wc = wc.reshape(-1, CCOLS)
    wg = wg.reshape(-1, XCOLS)
    wo = wo.reshape(-1, wo.shape[-1])
    everywhere = lambda v: lax.all_gather(v, AXES, axis=0, tiled=True)
    pick = lambda v: lax.dynamic_index_in_dim(
        lax.dynamic_index_in_dim(split_classes(v, size), c, 0, False), s, 0, False
    )
    gain1 = everywhere(pre_gain).astype(jnp.float32)
    gain2 = pick(everywhere(norm_gain).astype(jnp.float32))
    kern = everywhere(conv_weight).astype(jnp.float32).T
    kern = jnp.concatenate([pick(kern[:, :INNER]), kern[:, INNER:]], axis=1)
    bias = everywhere(conv_bias).astype(jnp.float32)
    bias = jnp.concatenate([pick(bias[:INNER]), bias[INNER:]])
    shift, rate, skip = pick(dt_bias), pick(a_log), pick(skip_gain)
    docs = lax.all_gather(doc, group, axis=0).reshape(2, 2 * own)
    n = size["so"]
    up = [(i, i + 1) for i in range(n - 1)]
    down = [(i + 1, i) for i in range(n - 1)]
    toks = toks.reshape(2, 2 * own, -1)
    cots = cots.reshape(2, 2 * own, -1)
    halo = lax.ppermute(toks[:, 2 * own - margin :], "so", up)
    halo_ids = jnp.where(b > 0, lax.ppermute(docs[:, 2 * own - margin :], "so", up), -1)
    rowsx = jnp.concatenate([halo, toks], axis=1).astype(jnp.float32)
    ext_ids = jnp.concatenate([halo_ids, docs], axis=1)
    normed, _ = jax.vjp(rms_scale, rowsx, gain1)
    normed_low = normed.astype(jnp.bfloat16)
    projected = jnp.einsum("qtd,dk->qtk", normed_low, wc, preferred_element_type=jnp.float32)
    gate_z = jnp.einsum("qtd,dk->qtk", normed_low[:, margin:], wg, preferred_element_type=jnp.float32)
    length = 2 * own
    count = length // GROUP
    dt_raw = projected[:, margin:, XCOLS + 2 * STATE : XCOLS + 2 * STATE + hl]

    def convolve(extended, kernel, offset_bias):
        def one(ext, ids):
            total = offset_bias
            for offset in range(CONVW):
                linked = (ids[offset : offset + length] == ids[margin:])[:, None]
                total = total + jnp.where(linked, ext[offset : offset + length], 0.0) * kernel[offset]
            return jax.nn.silu(total)
        return jax.vmap(one)(extended, ext_ids)

    activated, conv_back = jax.vjp(convolve, projected[:, :, : XCOLS + 2 * STATE], kern, bias)

    def zero_state(acts_in, raw_in, shift_in, rate_in):
        def one(acts, raw, doc_ids, prior_id):
            heads_x = acts[:, :XCOLS].reshape(length, hl, HEADDIM)
            b_rows = acts[:, XCOLS : XCOLS + STATE]
            c_rows = acts[:, XCOLS + STATE :]
            steps_dt = jax.nn.softplus(raw + shift_in)
            log_decay = -jnp.exp(rate_in) * steps_dt
            befores = jnp.concatenate([prior_id[None], doc_ids.reshape(count, GROUP)[:-1, GROUP - 1]])
            items = (
                befores,
                heads_x.reshape(count, GROUP, hl, HEADDIM),
                b_rows.reshape(count, GROUP, STATE),
                c_rows.reshape(count, GROUP, STATE),
                steps_dt.reshape(count, GROUP, hl),
                log_decay.reshape(count, GROUP, hl),
                doc_ids.reshape(count, GROUP),
            )
            final = jnp.zeros((hl, HEADDIM, STATE), jnp.float32)
            outs = []
            for i in range(count):
                out, final = group_math(final, *[v[i] for v in items])
                outs.append(out)
            factor = jnp.exp(jnp.sum(log_decay, axis=0)) * (doc_ids[length - 1] == prior_id)
            return (jnp.stack(outs).reshape(length, hl, HEADDIM), factor, final)
        return jax.vmap(one)(acts_in, raw_in, docs, ext_ids[:, margin - 1])

    def incoming(acts_in, raw_in, shift_in, rate_in, start_state):
        def one(acts, raw, doc_ids, prior_id, state):
            steps_dt = jax.nn.softplus(raw + shift_in)
            running = jnp.cumsum(-jnp.exp(rate_in) * steps_dt, axis=0)
            factor = jnp.exp(running) * (doc_ids == prior_id)[:, None]
            return jnp.einsum("tn,hpn->thp", acts[:, XCOLS + STATE :], state, precision=HIGHEST) * factor[:, :, None]
        return jax.vmap(one)(acts_in, raw_in, docs, ext_ids[:, margin - 1], start_state)

    (local_y, factor, local_state), zero_back = jax.vjp(zero_state, activated, dt_raw, shift, rate)
    all_states = lax.all_gather(local_state, "so", axis=0)
    all_factors = lax.all_gather(factor, "so", axis=0)
    start_state = jnp.zeros_like(local_state)
    for i in range(n - 1):
        step = all_factors[i][:, :, None, None] * start_state + all_states[i]
        start_state = jnp.where(i < b, step, start_state)
    carried_y, in_back = jax.vjp(incoming, activated, dt_raw, shift, rate, start_state)
    heads_x = activated[:, :, :XCOLS].reshape(2, length, hl, HEADDIM)
    mixer_out = (local_y + carried_y + skip[:, None] * heads_x).reshape(2, length, XCOLS)

    grad_gated = jnp.einsum("qtd,kd->qtk", cots, wo, preferred_element_type=jnp.float32)
    silu_z, silu_back = jax.vjp(jax.nn.silu, gate_z)
    v = mixer_out * silu_z
    u = grad_gated * gain2
    sums = lax.psum(jnp.stack([jnp.sum(v * v, axis=-1), jnp.sum(u * v, axis=-1)]), group)
    r = lax.rsqrt(sums[0] / INNER + EPSILON)[:, :, None]
    mean_uv = sums[1][:, :, None] / INNER
    gated_low = (v * r * gain2).astype(jnp.bfloat16)
    grad_v = r * u - r * r * r * v * mean_uv
    norm_gain_grad = jnp.sum(grad_gated * v * r, axis=(0, 1))
    grad_mixer = grad_v * silu_z
    (grad_gate_z,) = silu_back(grad_v * mixer_out)
    branch = jnp.einsum("qtk,kd->qtd", gated_low, wo, preferred_element_type=jnp.float32)
    out_weight_grad = jnp.einsum("qtk,qtd->kd", gated_low, cots, preferred_element_type=jnp.float32)
    branch = lax.psum_scatter(branch.reshape(4, own, -1), group, scatter_dimension=0, tiled=False)
    mixed = (tok.astype(jnp.float32) + branch).astype(jnp.bfloat16)

    grad_heads = grad_mixer.reshape(2, length, hl, HEADDIM)
    skip_grad = jnp.sum(grad_heads * heads_x, axis=(0, 1, 3))
    acts_one, raw_one, shift_one, rate_one, start_grad = in_back(grad_heads)
    all_grads = lax.all_gather(start_grad, "so", axis=0)
    end_grad = jnp.zeros_like(start_grad)
    for i in range(n - 1, 0, -1):
        step = all_grads[i] + all_factors[i][:, :, None, None] * end_grad
        end_grad = jnp.where(i > b, step, end_grad)
    factor_grad = jnp.sum(end_grad * start_state, axis=(2, 3))
    acts_two, raw_two, shift_two, rate_two = zero_back((grad_heads, factor_grad, end_grad))
    skip_part = (grad_heads * skip[:, None]).reshape(2, length, XCOLS)
    grad_acts = acts_one + acts_two + jnp.concatenate([skip_part, jnp.zeros((2, length, 2 * STATE), jnp.float32)], axis=2)
    grad_ext, kern_grad, bias_grad = conv_back(grad_acts)
    grad_dt = jnp.pad(raw_one + raw_two, ((0, 0), (margin, 0), (0, 128 - hl)))
    gpc = jnp.concatenate([grad_ext, grad_dt], axis=2).astype(jnp.bfloat16)
    gpg = grad_gate_z.astype(jnp.bfloat16)
    wc_grad = jnp.einsum("qtd,qtk->dk", normed_low, gpc, preferred_element_type=jnp.float32)
    wg_grad = jnp.einsum("qtd,qtk->dk", normed_low[:, margin:], gpg, preferred_element_type=jnp.float32)
    grad_normed = jnp.einsum("qtk,dk->qtd", gpc, wc, preferred_element_type=jnp.float32)
    late = grad_normed[:, margin:] + jnp.einsum("qtk,dk->qtd", gpg, wg, preferred_element_type=jnp.float32)
    early = lax.ppermute(grad_normed[:, :margin], "so", down)
    grad_normed = late + jnp.pad(early, ((0, 0), (length - margin, 0), (0, 0)))
    grad_normed = lax.psum_scatter(grad_normed.reshape(4, own, -1), group, scatter_dimension=0, tiled=False)
    _, pre_back = jax.vjp(rms_scale, tok.astype(jnp.float32), gain1)
    grad_tokens_norm, pre_gain_grad = pre_back(grad_normed)
    tokens_grad = cot.astype(jnp.float32) + grad_tokens_norm

    low = lambda v: v.astype(jnp.bfloat16)
    lead = (size["dpo"], 2, size["so"] * 2 * rows)
    oc, og, oo = reduce(
        size, low(wc_grad).reshape(lead + (CCOLS,)), low(wg_grad).reshape(lead + (XCOLS,)),
        low(out_weight_grad).reshape(size["dpo"], size["so"] // 2, 2 * out_weight.shape[0], -1),
    )
    oc, og = oc.astype(jnp.float32), og.astype(jnp.float32)
    by_class = lambda v: join_classes(v.reshape((2, 2) + v.shape[1:]), size)
    in_weight_grad = jnp.concatenate([
        by_class(og), by_class(oc[:, :, :XCOLS]), jnp.sum(oc[:, :, XCOLS : XCOLS + 2 * STATE], axis=0),
        by_class(oc[:, :, XCOLS + 2 * STATE : XCOLS + 2 * STATE + hl]),
    ], axis=1)
    def place_class(v):
        parts = jnp.zeros((2, 2) + v.shape, jnp.float32)
        return join_classes(lax.dynamic_update_slice(parts, v[None, None], (c, s) + (0,) * v.ndim), size)
    kern_grad = jnp.concatenate([place_class(kern_grad[:, :XCOLS]), kern_grad[:, XCOLS:]], axis=1).T
    bias_grad = jnp.concatenate([place_class(bias_grad[:XCOLS]), bias_grad[XCOLS:]])
    scattered = lambda v: lax.psum_scatter(v, AXES, scatter_dimension=0, tiled=True)
    heads = lax.psum((place_class(shift_one + shift_two), place_class(rate_one + rate_two), place_class(skip_grad)), AXES)
    return (
        mixed[None], tokens_grad[None], scattered(pre_gain_grad), in_weight_grad, scattered(kern_grad), scattered(bias_grad),
        heads[0], heads[1], heads[2], scattered(place_class(norm_gain_grad)), oo.astype(jnp.float32),
    )


def specs(dp, seq):
    both = dp + seq
    ins = (
        P(dp, seq, None), P(dp, seq), P(both), P(both, None), P(both, None), P(both),
        P(), P(), P(), P(both), P(both, None), P(dp, seq, None),
    )
    outs = (
        P(dp, seq, None), P(dp, seq, None), P(both), P(both, None), P(both, None), P(both),
        P(), P(), P(), P(both), P(both, None),
    )
    return ins, outs


def solution(mesh):
    dp, seq = mesh.shape["dp"], mesh.shape["seq"]
    fine = Mesh(mesh.devices.reshape(dp // 2, 2, seq // 2, 2), AXES)
    size = dict(fine.shape)

    def choose(*args):
        in_rows, out_rows, own = args[3].shape[0], args[10].shape[0], args[0].shape[1]
        ok = (args[0].shape[0] == 2 * size["dpo"] and own == 2 * size["so"] * GROUP and INNER % (dp * seq * HEADDIM // 2) == 0 and (in_rows // (dp * seq)) % 16 == 0 and size["so"] % 2 == 0)
        if ok:
            ins, outs = specs(AXES[:2], AXES[2:])
            return jax.shard_map(functools.partial(fast_body, size), mesh=fine, in_specs=ins, out_specs=outs, check_vma=False)(*args)
        ins, outs = specs(("dp",), ("seq",))
        return jax.shard_map(whole_body, mesh=mesh, in_specs=ins, out_specs=outs, check_vma=False)(*args)

    return choose
```

```python
import functools
import types

import jax
import jax.numpy as jnp
from jax import lax
from jax.experimental import pallas as pl
from jax.experimental.pallas import tpu as pltpu
from jax.sharding import Mesh
from jax.sharding import PartitionSpec as P

HEADS = 48
HEADDIM = 64
STATE = 128
CONVW = 4
GROUP = 256
INNER = 3072
XBC = 3328


HIGHEST = lax.Precision.HIGHEST
EPSILON = 1e-05


def passed_along(block, axis, distance):
    devices = range(lax.axis_size(axis))
    route = [(i - distance, i) for i in devices if i - distance in devices]
    return lax.ppermute(block, axis, route)


def shortened(shard):
    return jax.tree.map(lambda a: a.astype(jnp.bfloat16) if a.dtype == jnp.float32 else a, shard)


def rms_scale(values, gain):
    return values * lax.rsqrt(jnp.mean(values * values, axis=-1, keepdims=True) + EPSILON) * gain


def gating(values, gates, gain):
    return rms_scale(values * jax.nn.silu(gates), gain)


def group_math(state, before, heads_x, b_rows, c_rows, steps_dt, log_decay, doc_ids):
    length = doc_ids.shape[0]
    running = jnp.cumsum(log_decay, axis=0)
    causal = jnp.arange(length)[:, None] >= jnp.arange(length)[None, :]
    linked = ((doc_ids[:, None] == doc_ids[None, :]) & causal)[:, :, None]
    gaps = running[:, None, :] - running[None, :, :]
    decays = jnp.exp(jnp.where(linked, gaps, 0.0)) * linked
    scores = jnp.dot(c_rows, b_rows.T, precision=HIGHEST)
    mixing = decays * scores[:, :, None] * steps_dt[None, :, :]
    inside = jnp.einsum("tsh,shp->thp", mixing, heads_x, precision=HIGHEST)
    alive = (doc_ids == before)[:, None]
    enter = jnp.exp(running) * alive
    carried = jnp.einsum("tn,hpn->thp", c_rows, state, precision=HIGHEST) * enter[:, :, None]
    last_id = doc_ids[length - 1]
    kept = (doc_ids == last_id)[:, None]
    weights_end = jnp.exp(running[length - 1][None, :] - running) * kept * steps_dt
    fresh = jnp.einsum("sh,shp,sn->hpn", weights_end, heads_x, b_rows, precision=HIGHEST)
    passed = jnp.exp(running[length - 1]) * (last_id == before)
    return (inside + carried, fresh + passed[:, None, None] * state)


def contract_rows(left, right):
    return lax.dot_general(
        left, right, (((0,), (0,)), ((), ())), preferred_element_type=jnp.float32
    )


def contract_cols(left, right):
    return lax.dot_general(
        left, right, (((1,), (1,)), ((), ())), preferred_element_type=jnp.float32
    )


def whole_body(
    tokens,
    segment_ids,
    pre_gain,
    in_weight,
    conv_weight,
    conv_bias,
    dt_bias,
    a_log,
    skip_gain,
    norm_gain,
    out_weight,
    cotangent,
):
    tok_rows = tokens[0].astype(jnp.float32)
    doc_ids = segment_ids[0]
    length = doc_ids.shape[0]
    margin = CONVW - 1
    count = length // GROUP
    shards = (pre_gain, in_weight, conv_weight, conv_bias, norm_gain, out_weight)
    gathered = (
        lax.all_gather(shards[0], ("dp", "seq"), axis=0, tiled=True),
        lax.all_gather(shards[1], ("dp", "seq"), axis=0, tiled=True),
        lax.all_gather(shards[2], ("dp", "seq"), axis=0, tiled=True),
        lax.all_gather(shards[3], ("dp", "seq"), axis=0, tiled=True),
        lax.all_gather(shards[4], ("dp", "seq"), axis=0, tiled=True),
        lax.all_gather(shards[5], ("dp", "seq"), axis=0, tiled=True),
    )
    normed, pre_back = jax.vjp(rms_scale, tok_rows, gathered[0].astype(jnp.float32))
    normed_low = normed.astype(jnp.bfloat16)
    projected = jnp.dot(normed_low, gathered[1], preferred_element_type=jnp.float32)
    gate_z = projected[:, :INNER]
    conv_in = projected[:, INNER : INNER + XBC]
    dt_raw = projected[:, INNER + XBC :]
    halo_rows, halo_ids = (
        passed_along(conv_in[length - margin :].astype(jnp.bfloat16), "seq", 1).astype(jnp.float32),
        passed_along(
            doc_ids[length - margin :].astype(jnp.float32).astype(jnp.bfloat16), "seq", 1
        ).astype(jnp.float32),
    )
    ext_ids = jnp.concatenate([halo_ids.astype(jnp.int32), doc_ids])
    prior_id = ext_ids[margin - 1]

    def convolve(extended, kernel, offset_bias):
        total = offset_bias
        for offset in range(CONVW):
            taps = extended[offset : offset + length]
            linked = (ext_ids[offset : offset + length] == doc_ids)[:, None]
            total = total + jnp.where(linked, taps, 0.0) * kernel[:, offset]
        return jax.nn.silu(total)

    activated, conv_back = jax.vjp(
        convolve,
        jnp.concatenate([halo_rows, conv_in]),
        gathered[2].astype(jnp.float32),
        gathered[3].astype(jnp.float32),
    )

    def zero_state(acts_in, raw_in, shift_in, rate_in):
        heads_x = acts_in[:, :INNER].reshape(length, HEADS, HEADDIM)
        b_rows = acts_in[:, INNER : INNER + STATE]
        c_rows = acts_in[:, INNER + STATE :]
        steps_dt = jax.nn.softplus(raw_in + shift_in)
        log_decay = -jnp.exp(rate_in) * steps_dt
        befores = jnp.concatenate([prior_id[None], doc_ids.reshape(count, GROUP)[:-1, GROUP - 1]])

        def step(state, item):
            out, new_state = group_math(state, *item)
            return (new_state, out)

        items = (
            befores,
            heads_x.reshape(count, GROUP, HEADS, HEADDIM),
            b_rows.reshape(count, GROUP, STATE),
            c_rows.reshape(count, GROUP, STATE),
            steps_dt.reshape(count, GROUP, HEADS),
            log_decay.reshape(count, GROUP, HEADS),
            doc_ids.reshape(count, GROUP),
        )
        final, outs = lax.scan(step, jnp.zeros((HEADS, HEADDIM, STATE), jnp.float32), items)
        factor = jnp.exp(jnp.sum(log_decay, axis=0)) * (doc_ids[length - 1] == prior_id)
        return (outs.reshape(length, HEADS, HEADDIM), factor, final)

    def incoming(acts_in, raw_in, shift_in, rate_in, start_state):
        steps_dt = jax.nn.softplus(raw_in + shift_in)
        running = jnp.cumsum(-jnp.exp(rate_in) * steps_dt, axis=0)
        factor = jnp.exp(running) * (doc_ids == prior_id)[:, None]
        c_rows = acts_in[:, INNER + STATE :]
        return (
            jnp.einsum("tn,hpn->thp", c_rows, start_state, precision=HIGHEST) * factor[:, :, None]
        )

    (local_y, factor, local_state), zero_back = jax.vjp(
        zero_state, activated, dt_raw, dt_bias, a_log
    )
    identity = (jnp.ones((HEADS,), jnp.float32), jnp.zeros((HEADS, HEADDIM, STATE), jnp.float32))

    def forward_turn(index, carry_state):
        return passed_along(factor[:, None, None] * carry_state + local_state, "seq", 1)

    start_state = lax.fori_loop(0, lax.axis_size("seq") - 1, forward_turn, identity[1])
    carried_y, in_back = jax.vjp(incoming, activated, dt_raw, dt_bias, a_log, start_state)
    heads_x = activated[:, :INNER].reshape(length, HEADS, HEADDIM)
    mixer_out = (local_y + carried_y + skip_gain[:, None] * heads_x).reshape(length, INNER)
    gated, gate_back = jax.vjp(gating, mixer_out, gate_z, gathered[4].astype(jnp.float32))
    gated_low = gated.astype(jnp.bfloat16)
    branch = jnp.dot(gated_low, gathered[5], preferred_element_type=jnp.float32)
    mixed = (tok_rows + branch).astype(jnp.bfloat16)
    again = (
        lax.all_gather(shards[0], ("dp", "seq"), axis=0, tiled=True),
        lax.all_gather(shards[1], ("dp", "seq"), axis=0, tiled=True),
        lax.all_gather(shards[2], ("dp", "seq"), axis=0, tiled=True),
        lax.all_gather(shards[3], ("dp", "seq"), axis=0, tiled=True),
        lax.all_gather(shards[4], ("dp", "seq"), axis=0, tiled=True),
        lax.all_gather(shards[5], ("dp", "seq"), axis=0, tiled=True),
    )
    grad_out = cotangent[0]
    grad_gated = contract_cols(grad_out, again[5])
    out_weight_grad = contract_rows(gated_low, grad_out)
    grad_mixer, grad_gate_z, norm_gain_grad = gate_back(grad_gated)
    grad_heads = grad_mixer.reshape(length, HEADS, HEADDIM)
    skip_grad = jnp.sum(grad_heads * heads_x, axis=(0, 2))
    acts_one, raw_one, shift_one, rate_one, start_grad = in_back(grad_heads)

    def backward_turn(index, carry_grad):
        return passed_along(start_grad + factor[:, None, None] * carry_grad, "seq", -1)

    end_grad = lax.fori_loop(0, lax.axis_size("seq") - 1, backward_turn, identity[1])
    factor_grad = jnp.sum(end_grad * start_state, axis=(1, 2))
    acts_two, raw_two, shift_two, rate_two = zero_back((grad_heads, factor_grad, end_grad))
    skip_part = (grad_heads * skip_gain[:, None]).reshape(length, INNER)
    grad_acts = (
        acts_one
        + acts_two
        + jnp.concatenate([skip_part, jnp.zeros((length, 2 * STATE), jnp.float32)], axis=1)
    )
    grad_ext, conv_weight_grad, conv_bias_grad = conv_back(grad_acts)
    back_rows = passed_along(shortened(grad_ext[:margin]), "seq", -1)
    grad_conv_in = grad_ext[margin:] + jnp.concatenate(
        [jnp.zeros((length - margin, XBC), jnp.float32), back_rows]
    )
    grad_projected = jnp.concatenate([grad_gate_z, grad_conv_in, raw_one + raw_two], axis=1).astype(
        jnp.bfloat16
    )
    in_weight_grad = contract_rows(normed_low, grad_projected)
    grad_normed = contract_cols(grad_projected, again[1])
    grad_tokens_norm, pre_gain_grad = pre_back(grad_normed)
    tokens_grad = grad_out.astype(jnp.float32) + grad_tokens_norm
    grad_parts = (
        pre_gain_grad,
        in_weight_grad,
        conv_weight_grad,
        conv_bias_grad,
        norm_gain_grad,
        out_weight_grad,
    )
    row_sums = (
        lax.psum_scatter(grad_parts[0], "dp", scatter_dimension=0, tiled=True),
        lax.psum_scatter(grad_parts[1], "dp", scatter_dimension=0, tiled=True),
        lax.psum_scatter(grad_parts[2], "dp", scatter_dimension=0, tiled=True),
        lax.psum_scatter(grad_parts[3], "dp", scatter_dimension=0, tiled=True),
        lax.psum_scatter(grad_parts[4], "dp", scatter_dimension=0, tiled=True),
        lax.psum_scatter(grad_parts[5], "dp", scatter_dimension=0, tiled=True),
    )
    sums = (
        lax.psum_scatter(row_sums[0], "seq", scatter_dimension=0, tiled=True),
        lax.psum_scatter(row_sums[1], "seq", scatter_dimension=0, tiled=True),
        lax.psum_scatter(row_sums[2], "seq", scatter_dimension=0, tiled=True),
        lax.psum_scatter(row_sums[3], "seq", scatter_dimension=0, tiled=True),
        lax.psum_scatter(row_sums[4], "seq", scatter_dimension=0, tiled=True),
        lax.psum_scatter(row_sums[5], "seq", scatter_dimension=0, tiled=True),
    )
    head_sums = lax.psum((shift_one + shift_two, rate_one + rate_two, skip_grad), ("dp", "seq"))
    return (
        mixed[None],
        tokens_grad[None],
        sums[0],
        sums[1],
        sums[2],
        sums[3],
        head_sums[0],
        head_sums[1],
        head_sums[2],
        sums[4],
        sums[5],
    )

AXES = ("dpo", "dpi", "so", "si")
MESH = pl.DeviceIdType.MESH
XCOLS = INNER // 4
ACT = XCOLS + 2 * STATE
CCOLS = ACT + 128
CHUNK = 128
HL = HEADS // 4
PAD = 16
MARGIN = CONVW - 1
f32, bf16 = jnp.float32, jnp.bfloat16
VMEM = pl.BlockSpec(memory_space=pltpu.VMEM)
HBM = pl.BlockSpec(memory_space=pl.ANY)


def guarded(when, action):
    if when is None:
        action()
    else:
        pl.when(when)(action)


class Wires:
    def __init__(self, send, recv, local):
        self.send, self.recv, self.local = send, recv, local
        self.used, self.kept, self.pending = 0, 0, []

    def slot(self):
        self.used += 1
        return self.used - 1

    def copy(self, src, dst, slot, device, landed=None):
        return pltpu.make_async_remote_copy(
            src_ref=src, dst_ref=dst, send_sem=self.send.at[slot],
            recv_sem=self.recv.at[slot if landed is None else landed],
            device_id=device, device_id_type=MESH,
        )

    def start(self, src, dst, slot, device, when=None, landed=None):
        copy = self.copy(src, dst, slot, device, landed)
        guarded(when, copy.start)
        self.pending.append((copy, when))
        return self.pending[-1]

    def sent(self, entry):
        self.pending = [kept for kept in self.pending if kept is not entry]
        guarded(entry[1], entry[0].wait_send)

    def arrived(self, landing, slot, device, when=None):
        guarded(when, self.copy(landing, landing, slot, device).wait_recv)

    def keep(self, src, dst, when=None):
        copy = pltpu.make_async_copy(src, dst, self.local.at[self.kept])
        self.kept += 1
        guarded(when, copy.start)
        return lambda: guarded(when, copy.wait)

    def finish(self):
        for copy, when in self.pending:
            guarded(when, copy.wait_send)
        self.pending = []


def place():
    return tuple(lax.axis_index(name) for name in AXES)


def member(here, rel):
    a, c, b, s = here
    return (a, c ^ (rel >> 1), b, s ^ (rel & 1))


def greet(here, size, extra):
    a, c, b, s = here
    n, nx = size["so"], size["dpo"]
    barrier = pltpu.get_barrier_semaphore()
    known = [member(here, rel) for rel in range(1, 4)]
    known += [(a, c, lax.rem(b + k, n), s) for k in range(1, n)]
    known += [(lax.rem(a + k, nx), c, b, s) for k in range(1, nx)]
    for device in known:
        pl.semaphore_signal(barrier, inc=1, device_id=device, device_id_type=MESH)
    met = len(known)
    for devices, when in extra:
        for device in devices:
            guarded(when, lambda device=device: pl.semaphore_signal(barrier, inc=1, device_id=device, device_id_type=MESH))
        met = met + len(devices) * when.astype(jnp.int32)
    return lambda: pl.semaphore_wait(barrier, met)


def mm(x, y, dims=((1,), (0,)), exact=None):
    if exact is not None:
        whole = (x, y)[exact].astype(f32)
        high = whole.astype(bf16)
        low = (whole - high.astype(f32)).astype(bf16)
        parts = [(high, y), (low, y)] if exact == 0 else [(x, high), (x, low)]
        return mm(*parts[0], dims) + mm(*parts[1], dims)
    return lax.dot_general(x.astype(bf16), y.astype(bf16), (dims, ((), ())), preferred_element_type=f32)


def fine(x, y, dims=((1,), (0,))):
    x, y = x.astype(f32), y.astype(f32)
    xh, yh = x.astype(bf16), y.astype(bf16)
    xl, yl = (x - xh.astype(f32)).astype(bf16), (y - yh.astype(f32)).astype(bf16)
    return mm(xh, yh, dims) + (mm(xl, yh, dims) + mm(xh, yl, dims))


def iota(shape, axis):
    return lax.broadcasted_iota(jnp.int32, shape, axis)


def spread_heads():
    return (iota((128, XCOLS), 0) == iota((128, XCOLS), 1) // HEADDIM).astype(f32).astype(bf16)


def gather_heads():
    return (iota((XCOLS, 128), 1) == iota((XCOLS, 128), 0) // HEADDIM).astype(f32).astype(bf16)


def class_heads(size, cc, ss):
    per = size["so"] // 2
    run = HEADS // (size["dpo"] * 4 * per)
    lane = iota((128, 128), 1)
    group, j = lane // run, lane % run
    head = (((group // per * 2 + cc) * per + group % per) * 2 + ss) * run + j
    return ((iota((128, 128), 0) == head) & (lane < HL)).astype(f32).astype(bf16)


def pick_heads(values, chosen, dims=((1,), (0,))):
    high = values.astype(bf16)
    rest = values - high.astype(f32)
    middle = rest.astype(bf16)
    low = rest - middle.astype(f32)
    return mm(high, chosen, dims) + mm(middle, chosen, dims) + mm(low, chosen, dims)


def loop(count, body, first=0):
    lax.fori_loop(first, count, lambda i, _: (body(i), 0)[1], 0)


def chunk_rows(r, i):
    per = r.span // CHUNK
    flat = pl.multiple_of(i * CHUNK, CHUNK)
    padded = pl.multiple_of((i // per) * (r.span + PAD) + PAD + (i % per) * CHUNK, PAD)
    return flat, padded


def chunk_decays(r, i):
    flat, padded = chunk_rows(r, i)
    rows = pl.ds(flat, CHUNK)
    ids = r.idc[pl.ds(padded, CHUNK), :]
    before = r.idc[pl.ds(pl.multiple_of(padded - 8, 8), 8), :][7:8]
    last = ids[CHUNK - 1 : CHUNK]
    return flat, padded, rows, ids, before, last


def phase_norm(r, i, block):
    rows = pl.ds(pl.multiple_of(i * block, 16), block)
    t = r.toks[rows, :].astype(f32)
    scale = lax.rsqrt(jnp.mean(t * t, axis=1, keepdims=True) + EPSILON)
    r.normed[rows, :] = (t * scale * r.gain1[0:1]).astype(bf16)


def taps(window, ids, k, rows):
    first = 8 - MARGIN + k
    same = ids[first : first + rows] == ids[8 : 8 + rows]
    return jnp.where(same, window[first : first + rows], 0.0)


def phase_in(r, q, w, first):
    rows = r.span + PAD
    w = w.reshape(w.shape[0] * w.shape[1], 256)
    r.pc[q * rows : (q + 1) * rows, pl.ds(first, 256)] = mm(r.normed[q * rows : (q + 1) * rows, :], w)
    ids = r.idc[q * rows + PAD - 8 : (q + 1) * rows, :]
    for half in range(2):
        tile = pl.ds(pl.multiple_of(first + half * 128, 128), 128)
        window = r.pc[q * rows + PAD - 8 : (q + 1) * rows, tile]
        kern = r.cv[:, tile]
        pre = kern[4:5] + window[8:] * kern[3:4]
        for k in range(MARGIN):
            pre = pre + taps(window, ids, k, r.span) * kern[k : k + 1]
        gate = jax.nn.sigmoid(pre)
        act = pre * gate
        r.act[q * r.span : (q + 1) * r.span, tile] = act
        r.sp[q * r.span : (q + 1) * r.span, tile] = gate + act * (1.0 - gate)


def phase_decay(r, i):
    flat, padded, rows, ids, before, last = chunk_decays(r, i)
    raw = r.dtr[pl.ds(padded, CHUNK), :] + r.hp[0:1]
    lane = iota((CHUNK, 128), 1) < HL
    dt = jnp.where(lane, jnp.maximum(raw, 0.0) + jnp.log1p(jnp.exp(-jnp.abs(raw))), 0.0)
    la = -jnp.exp(r.hp[1:2]) * dt
    tril = (iota((CHUNK, CHUNK), 0) >= iota((CHUNK, CHUNK), 1)).astype(f32)
    run = mm(tril, la, exact=1)
    end = run[CHUNK - 1 : CHUNK]
    weight = jnp.where(ids == last, jnp.exp(end - run), 0.0)
    passed = jnp.where(last == before, jnp.exp(end), 0.0)
    e = spread_heads()
    xdt = r.act[rows, 0:XCOLS] * mm(dt, e, exact=0)
    xw = xdt * mm(weight, e, exact=0)
    r.dtm[rows, :] = dt
    r.run[rows, :] = run
    r.xdt[rows, :] = xdt.astype(bf16)
    r.st[i] = fine(r.act[rows, XCOLS : XCOLS + STATE], xw, ((0,), (0,)))
    r.pex[i] = mm(jnp.broadcast_to(passed, (8, 128)), e, exact=0)


def phase_states(r):
    per = r.span // CHUNK
    for q in range(2):
        cur = jnp.zeros((STATE, XCOLS), f32)
        fac = jnp.ones((8, XCOLS), f32)
        for j in range(per):
            i = q * per + j
            fresh = r.st[i]
            r.st[i] = cur
            r.cum[i] = fac
            cur = r.pex[i][0:1] * cur + fresh
            fac = fac * r.pex[i]
        r.end[q] = cur
        r.fac[q] = fac


def chunk_matrix(r, i):
    flat, padded, rows, ids, before, last = chunk_decays(r, i)
    mask = (ids == ids.T) & (iota((CHUNK, CHUNK), 0) >= iota((CHUNK, CHUNK), 1))
    bm = r.bc[rows, 0:STATE].astype(bf16)
    cm = r.bc[rows, STATE:].astype(bf16)
    cb = mm(cm, bm, ((1,), (1,)))
    run = r.run[rows, :]
    return rows, mask, bm, cm, cb, run, run.T


def phase_inside(r, i):
    rows, mask, bm, cm, cb, run, runt = chunk_matrix(r, i)
    for hp in range(HL // 2):
        tile = pl.ds(hp * 128, 128)
        xdt = r.xdt[rows, tile]
        outs = []
        for k in range(2):
            h = 2 * hp + k
            decay = jnp.exp(jnp.where(mask, run[:, h : h + 1] - runt[h : h + 1, :], -1e30))
            outs.append(mm(decay * cb, xdt[:, k * HEADDIM : (k + 1) * HEADDIM]))
        r.y[rows, tile] = jnp.concatenate(outs, axis=1)


def phase_carried(r, i):
    flat, padded, rows, ids, before, last = chunk_decays(r, i)
    enter = mm(jnp.where(ids == before, jnp.exp(r.run[rows, :]), 0.0), spread_heads(), exact=0)
    start = r.st[i] + r.cum[i][0:1] * r.sin[i // (r.span // CHUNK)]
    r.st[i] = start
    carried = fine(r.act[rows, XCOLS + STATE : ACT], start) * enter
    r.y[rows, :] += carried + r.hx[0:1] * r.act[rows, 0:XCOLS]


def column_pair(first, second):
    lanes = iota((first.shape[0], 128), 1)
    return jnp.where(lanes == 0, first, jnp.where(lanes == 1, second, 0.0)).T[0:8]


def phase_sums(r, i):
    rows = pl.ds(pl.multiple_of(i * CHUNK, CHUNK), CHUNK)
    z = r.z[rows, :]
    v = r.y[rows, :] * (z * jax.nn.sigmoid(z))
    u = r.gg[rows, :] * r.ng[0:1]
    r.sums[0, i] = column_pair(jnp.sum(v * v, axis=1, keepdims=True), jnp.sum(u * v, axis=1, keepdims=True))


def phase_gate(r, i):
    rows = pl.ds(pl.multiple_of(i * CHUNK, CHUNK), CHUNK)
    total = (r.sums[0, i] + r.sums[1, i]) + (r.sums[2, i] + r.sums[3, i])
    cols = jnp.concatenate([total, jnp.zeros((CHUNK - 8, 128), f32)], axis=0).T
    scale = lax.rsqrt(cols[:, 0:1] / INNER + EPSILON)
    tilt = scale * scale * scale * (cols[:, 1:2] / INNER)
    z, y, gg = r.z[rows, :], r.y[rows, :], r.gg[rows, :]
    gate = jax.nn.sigmoid(z)
    silu = z * gate
    v = y * silu
    vr = v * scale
    gv = gg * r.ng[0:1] * scale - v * tilt
    r.gated[rows, :] = (vr * r.ng[0:1]).astype(bf16)
    r.gpg[rows, :] = (gv * y * (gate + silu * (1.0 - gate))).astype(bf16)
    r.gg[rows, :] = gv * silu
    r.nggrad[0:1] += jnp.sum(gg * vr, axis=0, keepdims=True)


def phase_back_states(r, i, x):
    flat, padded, rows, ids, before, last = chunk_decays(r, i)
    enter = mm(jnp.where(ids == before, jnp.exp(r.run[rows, :]), 0.0), spread_heads(), exact=0)
    dy = r.gg[rows, :]
    own = r.y[rows, :] - r.hx[0:1] * x
    low = dy.astype(bf16).astype(f32)
    r.drun[rows, :] = mm(low * own, gather_heads(), exact=0)
    r.y[rows, :] = fine(r.bc[rows, STATE:], dy * enter, ((0,), (0,)))
    r.tally[2:3] += jnp.sum(mm(dy * x, gather_heads(), exact=0), axis=0, keepdims=True)


def phase_back_chain(r):
    per = r.span // CHUNK
    for q in range(2):
        cur = jnp.zeros((STATE, XCOLS), f32)
        fac = jnp.ones((8, XCOLS), f32)
        for j in reversed(range(per)):
            i = q * per + j
            rows = slice(i * CHUNK, (i + 1) * CHUNK)
            fresh = r.y[rows, :]
            r.y[rows, :] = cur
            r.cum[i] = fac
            cur = r.pex[i][0:1] * cur + fresh
            fac = fac * r.pex[i]
        r.end[q] = cur


def phase_back_inside(r, i):
    rows, mask, bm, cm, cb, run, runt = chunk_matrix(r, i)
    dcb = jnp.zeros((CHUNK, CHUNK), f32)
    for hp in range(HL // 2):
        tile = pl.ds(hp * 128, 128)
        xdt, dy = r.xdt[rows, tile], r.gg[rows, tile].astype(bf16)
        outs = []
        for k in range(2):
            h = 2 * hp + k
            part = slice(k * HEADDIM, (k + 1) * HEADDIM)
            decay = jnp.exp(jnp.where(mask, run[:, h : h + 1] - runt[h : h + 1, :], -1e30))
            dcb = dcb + mm(dy[:, part], xdt[:, part], ((1,), (1,))) * decay
            outs.append(mm(decay * cb, dy[:, part], ((0,), (0,))))
        r.gx[rows, tile] = jnp.concatenate(outs, axis=1)
    r.gbc[rows, 0:STATE] = mm(dcb, cm, ((0,), (0,)))
    r.gbc[rows, STATE : 2 * STATE] = mm(dcb, bm)


def phase_back_close(r, i, start, x):
    flat, padded, rows, ids, before, last = chunk_decays(r, i)
    q = i // (r.span // CHUNK)
    e, g = spread_heads(), gather_heads()
    run, dt = r.run[rows, :], r.dtm[rows, :]
    end = run[CHUNK - 1 : CHUNK]
    enter = jnp.where(ids == before, jnp.exp(run), 0.0)
    weight = jnp.where(ids == last, jnp.exp(end - run), 0.0)
    entx, wx, dtx = mm(enter, e, exact=0), mm(weight, e, exact=0), mm(dt, e, exact=0)
    bm = r.bc[rows, 0:STATE]
    dy = r.gg[rows, :]
    dend = r.y[rows, :] + r.cum[i][0:1] * r.sin[q]
    xw = x * dtx * wx
    dxw = fine(bm, dend)
    inside = r.gx[rows, :]
    via_w = dxw * xw
    through = jnp.sum(dend * start, axis=0, keepdims=True) * r.pex[i][0:1]
    through = jnp.sum(via_w, axis=0, keepdims=True) + through
    at_end = mm(jnp.broadcast_to(through, (8, XCOLS)), g, exact=0)[0:1]
    drun = r.drun[rows, :] - mm(r.xdt[rows, :].astype(f32) * inside + via_w, g, exact=0)
    drun = drun + jnp.where(iota((CHUNK, 128), 0) == CHUNK - 1, at_end, 0.0)
    triu = (iota((CHUNK, CHUNK), 0) <= iota((CHUNK, CHUNK), 1)).astype(f32)
    dla = mm(triu, drun, exact=1)
    dxdt = inside + dxw * wx
    neg = -jnp.exp(r.hp[1:2])
    ddt = dla * neg + mm(dxdt * x, g, exact=0)
    raw = r.dtr[pl.ds(padded, CHUNK), :] + r.hp[0:1]
    draw = jnp.where(iota((CHUNK, 128), 1) < HL, ddt * jax.nn.sigmoid(raw), 0.0)
    r.gx[rows, :] = dxdt * dtx + r.hx[0:1] * dy
    r.gbc[rows, 0:STATE] += fine(xw, dend, ((1,), (1,)))
    r.gbc[rows, STATE : 2 * STATE] += fine(dy * entx, start, ((1,), (1,)))
    r.gpc[pl.ds(padded, CHUNK), ACT:CCOLS] = mm(draw, r.chosen[...], ((1,), (1,))).astype(bf16)
    r.tally[0:1] += jnp.sum(draw, axis=0, keepdims=True)
    r.tally[1:2] += jnp.sum(dla * (neg * dt), axis=0, keepdims=True)


def phase_back_conv(r, q, lt, grad, window, slope):
    rows = r.span + PAD
    tile = pl.ds(pl.multiple_of(lt * 128, 128), 128)
    kern = r.cv[:, tile]
    ids = r.idc[q * rows + PAD - 8 : (q + 1) * rows, :]
    gpre = grad * slope
    sums = []
    out = jnp.zeros((rows, 128), f32)
    for k in range(CONVW):
        first = 8 - MARGIN + k
        part = gpre
        if k < MARGIN:
            part = jnp.where(ids[first : first + r.span] == ids[8:], gpre, 0.0)
        sums.append(jnp.sum(part * window[first : first + r.span], axis=0, keepdims=True))
        ahead = PAD - MARGIN + k
        pieces = [jnp.zeros((ahead, 128), f32), part * kern[k : k + 1]]
        if rows - ahead - r.span:
            pieces.append(jnp.zeros((rows - ahead - r.span, 128), f32))
        out = out + jnp.concatenate(pieces, axis=0)
    sums.append(jnp.sum(gpre, axis=0, keepdims=True))
    sums.append(jnp.zeros((3, 128), f32))
    r.cvgrad[:, tile] += jnp.concatenate(sums, axis=0)
    r.gpc[q * rows : (q + 1) * rows, tile] = out.astype(bf16)


def unit_of(w, rows, aa, bb):
    return w.at[pl.ds(2 * aa, 2), pl.ds(pl.multiple_of(2 * rows * bb, 16), 2 * rows)]


def shard_of(w, rows, aa, cc, bb, ss):
    return w.at[2 * aa + cc, pl.ds(pl.multiple_of(2 * rows * bb + rows * ss, 16), rows)]


def spread(wires, here, size, get, relay=None):
    a, c, b, s = here
    n, nx = size["so"], size["dpo"]
    crossing = []

    def cross(bb, when):
        slots = {k: wires.slot() for k in range(1, nx)}
        for k in range(1, nx):
            wires.start(get(a, bb), get(a, bb), slots[k], (lax.rem(a + k, nx), c, b, s), when)
        crossing.append((bb, when, slots))
        if relay is not None:
            relay(a, bb, when)

    up = {j: wires.slot() for j in range(1, n)}
    down = {j: wires.slot() for j in range(1, n)}
    above, below = (a, c, jnp.minimum(b + 1, n - 1), s), (a, c, jnp.maximum(b - 1, 0), s)
    wires.start(get(a, b), get(a, b), up[1], above, b + 1 < n)
    wires.start(get(a, b), get(a, b), down[1], below, b > 0)
    cross(b, None)
    yield
    for j in range(1, n):
        sides = (
            (up, jnp.maximum(b - j, 0), b - j >= 0, below, above, b + 1 < n),
            (down, jnp.minimum(b + j, n - 1), b + j < n, above, below, b > 0),
        )
        for slots, origin, there, source, target, onward in sides:
            wires.arrived(get(a, origin), slots[j], source, there)
            if j + 1 < n:
                wires.start(get(a, origin), get(a, origin), slots[j + 1], target, there & onward)
            cross(origin, there)
        yield
    for bb, when, slots in crossing:
        for k in range(1, nx):
            aa = lax.rem(a + nx - k, nx)
            wires.arrived(get(aa, bb), slots[k], (aa, c, b, s), when)
            if relay is not None:
                relay(aa, bb, when)
    yield


def collect(wires, here, size, get, x, z, close):
    a, c, b, s = here
    n, nx = size["so"], size["dpo"]
    order = [k for k in range(1, n)] + [0]
    flown, hops = {}, {}
    for k in order:
        bb = lax.rem(b + k, n)
        for h in range(1, nx):
            flown[k, h] = wires.slot()
            wires.start(get(lax.rem(a + h, nx), bb), x.at[h - 1, k], flown[k, h], (lax.rem(a + h, nx), c, b, s))
    yield
    for k in order:
        bb = lax.rem(b + k, n)
        total = get(a, bb)[...].astype(f32)
        for h in range(1, nx):
            wires.arrived(x.at[h - 1, k], flown[k, h], (lax.rem(a + nx - h, nx), c, b, s))
            total = total + x[h - 1, k].astype(f32)
        x[0, k] = total.astype(bf16)
        if k > 0:
            hops[k] = wires.slot()
            wires.start(x.at[0, k], z.at[k - 1], hops[k], (a, c, bb, s))
        yield
    for k in range(1, n):
        wires.arrived(z.at[k - 1], hops[k], (a, c, lax.rem(b + n - k, n), s))
    total = x[0, 0].astype(f32)
    for k in range(1, n):
        total = total + z[k - 1].astype(f32)
    close(total)
    yield


def collect_out(wires, here, size, get, x, y, z, out, sends):
    a, c, b, s = here
    n, nx = size["so"], size["dpo"]
    half = y.shape[2]
    order = [k for k in range(1, n)] + [0]
    flown, turned, hops = {}, {}, {}
    part = lambda bb, ss: x.at[0, bb // 2, :, pl.ds(pl.multiple_of(half * ss, 16), half)]
    for k in order:
        bb = lax.rem(b + k, n)
        for h in range(1, nx):
            flown[k, h] = wires.slot()
            to = (lax.rem(a + h, nx), c, b, s)
            sends.append(wires.start(get(lax.rem(a + h, nx), bb), x.at[h - 1, bb // 2], flown[k, h], to, lax.rem(bb, 2) == s))
    yield
    for k in order:
        bb = lax.rem(b + k, n)
        has = lax.rem(bb, 2) == s
        for h in range(1, nx):
            wires.arrived(x.at[h - 1, bb // 2], flown[k, h], (lax.rem(a + nx - h, nx), c, b, s), has)

        @pl.when(has)
        def _():
            total = get(a, bb)[...].astype(f32)
            for h in range(1, nx):
                total = total + x[h - 1, bb // 2].astype(f32)
            x[0, bb // 2] = total.astype(bf16)

        turned[k], hops[k] = wires.slot(), wires.slot()
        wires.start(part(bb, 1 - s), y.at[bb // 2], turned[k], member(here, 1), has)
        if k > 0:
            wires.start(part(bb, s), z.at[k - 1], hops[k], (a, c, bb, s), has)
        yield
    for k in order:
        bb = lax.rem(b + k, n)
        turns = lax.rem(bb, 2) != s
        wires.arrived(y.at[bb // 2], turned[k], member(here, 1), turns)
        if k > 0:
            wires.start(y.at[bb // 2], z.at[k - 1], hops[k], (a, c, bb, s), turns)
    yield
    for k in range(1, n):
        wires.arrived(z.at[k - 1], hops[k], (a, c, lax.rem(b + n - k, n), s))

    def close(own):
        for h in range(2):
            total = own[h].astype(f32)
            for k in range(1, n):
                total = total + z[k - 1, h].astype(f32)
            out[:, h * XCOLS : (h + 1) * XCOLS] = total

    pl.when(lax.rem(b, 2) == s)(lambda: close(part(b, s)[...]))
    pl.when(lax.rem(b, 2) != s)(lambda: close(y[b // 2]))
    yield


def collect_shared(wires, here, size, g, s1, s2, s3, s4, out):
    a, c, b, s = here
    n, nx = size["so"], size["dpo"]
    slots = [wires.slot() for _ in range(2 + nx + n)]
    wires.start(g.at[pl.ds(2 * (1 - c), 2)], s1, slots[0], member(here, 2))
    yield
    wires.arrived(s1, slots[0], member(here, 2))
    for k in range(2):
        s1[k] = (s1[k].astype(f32) + g[2 * c + k].astype(f32)).astype(bf16)
    wires.start(s1.at[1 - s], s2, slots[1], member(here, 1))
    yield
    wires.arrived(s2, slots[1], member(here, 1))
    for k in range(nx):
        s2[k] = (s2[k].astype(f32) + s1[s, k].astype(f32)).astype(bf16)
    for h in range(1, nx):
        to = lax.rem(a + h, nx)
        wires.start(s2.at[to], s3.at[h - 1], slots[1 + h], (to, c, b, s))
    yield
    total = s2[a].astype(f32)
    for h in range(1, nx):
        wires.arrived(s3.at[h - 1], slots[1 + h], (lax.rem(a + nx - h, nx), c, b, s))
        total = total + s3[h - 1].astype(f32)
    s3[0] = total.astype(bf16)
    for k in range(1, n):
        bb = lax.rem(b + k, n)
        wires.start(s3.at[0, bb], s4.at[k - 1], slots[1 + nx + k], (a, c, bb, s))
    yield
    total = s3[0, b].astype(f32)
    for k in range(1, n):
        wires.arrived(s4.at[k - 1], slots[1 + nx + k], (a, c, lax.rem(b + n - k, n), s))
        total = total + s4[k - 1].astype(f32)
    out[...] = total
    yield


def finish_units(wires, here, rows, z, out):
    a, c, b, s = here
    mine = 2 * c + s
    back = {}

    def close(total):
        z[0] = total.astype(bf16)
        out[mine] = z[0, c, pl.ds(pl.multiple_of(rows * s, 16), rows)]
        for rel in range(1, 4):
            _, cc, _, ss = member(here, rel)
            back[rel] = wires.slot()
            part = z.at[0, cc, pl.ds(pl.multiple_of(rows * ss, 16), rows)]
            wires.start(part, out.at[mine], back[rel], member(here, rel))

    def wait():
        for rel in range(1, 4):
            _, cc, _, ss = member(here, rel)
            wires.arrived(out.at[2 * cc + ss], back[rel], member(here, rel))

    return close, wait


def sum_all(wires, here, size, mine, z, x):
    a, c, b, s = here
    n, nx = size["so"], size["dpo"]
    slots = [wires.slot() for _ in range(n + nx)]
    z[b] = mine[...]
    for k in range(1, n):
        wires.start(mine, z.at[b], slots[k], (a, c, lax.rem(b + k, n), s))
    yield
    for k in range(1, n):
        origin = lax.rem(b + n - k, n)
        wires.arrived(z.at[origin], slots[k], (a, c, origin, s))
    total = z[0]
    for k in range(1, n):
        total = total + z[k]
    x[a] = total
    for h in range(1, nx):
        wires.start(x.at[a], x.at[a], slots[n + h], (lax.rem(a + h, nx), c, b, s))
    yield
    for h in range(1, nx):
        origin = lax.rem(a + nx - h, nx)
        wires.arrived(x.at[origin], slots[n + h], (origin, c, b, s))
    total = x[0]
    for h in range(1, nx):
        total = total + x[h]
    yield total


def run_places(size):
    per = size["so"] // 2
    width = INNER // (size["dpo"] * 4 * per)
    return [
        (2 * cc + ss, (aa * per + bb) * width)
        for aa in range(size["dpo"]) for cc in range(2) for bb in range(per) for ss in range(2)
    ], width


def class_runs(values, size, m):
    places, width = run_places(size)
    return jnp.concatenate([values[:, k * width : (k + 1) * width] for k, (cls, _) in enumerate(places) if cls == m], axis=1)


def joined_runs(of_class, size, first, count):
    places, width = run_places(size)
    return jnp.concatenate([of_class[m][:, at : at + width] for m, at in places[first // width : (first + count) // width]], axis=1)


def device_index(size, here):
    a, c, b, s = here
    return (2 * a + c) * (2 * size["so"]) + 2 * b + s


def widened(values, rows, columns):
    if columns > values.shape[1]:
        values = jnp.concatenate([values, jnp.zeros((values.shape[0], columns - values.shape[1]), f32)], axis=1)
    if rows > values.shape[0]:
        values = jnp.concatenate([values, jnp.zeros((rows - values.shape[0], columns), f32)], axis=0)
    return values


def place_smalls(size, here, r):
    count = size["dpo"] * 4 * size["so"]
    index = device_index(size, here)
    depth = r.normed.shape[1]
    sub = iota((8, 128), 0)

    def placed(tile, total):
        return pltpu.roll(widened(tile, 8, total), index * (total // count), 1)

    taps = widened(r.conv_w[...].astype(f32), 128, 128).T[0:8]
    tile = taps + jnp.where(sub == 4, widened(r.conv_b[...].astype(f32), 1, 128), 0.0)
    conv = placed(tile, XBC)
    norm = placed(widened(r.norm_in[...].astype(f32), 8, 128), INNER)
    pre = placed(widened(r.pre_in[...].astype(f32), 8, 128), depth)
    sub = iota((8, ACT), 0)
    low = widened(pre[0:1, ACT:], 1, ACT)
    common = jnp.where(sub == 6, pre[0:1, :ACT], jnp.where(sub == 7, low, 0.0))
    for m in range(4):
        own = jnp.concatenate([class_runs(conv[:, :INNER], size, m), conv[:, INNER:]], axis=1)
        gain = widened(class_runs(norm, size, m)[0:1], 1, ACT)
        r.cvs[m] = own + jnp.where(sub == 5, gain, common)


def final_smalls(size, here, r):
    count = size["dpo"] * 4 * size["so"]
    index = device_index(size, here)
    depth = 2 * XCOLS
    tiles = [r.os[m] for m in range(4)]

    def taken(values, total):
        return pltpu.roll(values, total - index * (total // count), 1)[:, 0:128]

    inner = joined_runs([t[:, :XCOLS] for t in tiles], size, 0, INNER)
    rest = (tiles[0][:, XCOLS:] + tiles[1][:, XCOLS:]) + (tiles[2][:, XCOLS:] + tiles[3][:, XCOLS:])
    conv = taken(jnp.concatenate([inner, rest], axis=1), XBC)
    r.smo[0] = conv
    r.smo[1] = taken(inner, INNER)
    r.cwo[...] = widened(conv, 128, 128).T[0 : r.cwo.shape[0], 0:CONVW]
    pre = [jnp.concatenate([t[6:7], t[7:8, : depth - ACT]], axis=1) for t in tiles]
    r.smo[2] = taken(widened((pre[0] + pre[1]) + (pre[2] + pre[3]), 8, depth), depth)
    heads = jnp.zeros((8, 128), f32)
    for m, t in enumerate(tiles):
        three = jnp.concatenate([t[5:6, XCOLS : XCOLS + 128], t[5:6, XCOLS + 128 :], t[7:8, depth - ACT : depth - ACT + 128]], axis=0)
        heads = heads + pick_heads(widened(three, 8, 128), class_heads(size, m // 2, m % 2), ((1,), (1,)))
    r.smo[3] = heads


def chain(wires, here, size, r, step):
    a, c, b, s = here
    n = size["so"]
    half = XCOLS // 2
    to = (a, c, jnp.clip(b + step, 0, n - 1), s)
    origin = (a, c, jnp.clip(b - step, 0, n - 1), s)
    place_in = b if step > 0 else n - 1 - b
    copies = []
    for m in range(4):
        slot = wires.slot()
        copies.append((wires.copy(r.cout.at[m], r.cin.at[m], slot, to), slot))
        wires.pending.append((copies[m][0], place_in + 1 < n))

    def hop(h):
        def act():
            for m in range(4):
                q, cols = m // 2, slice((m % 2) * half, (m % 2 + 1) * half)
                if h == 0:
                    value = r.end[q, :, cols]
                    r.sin[q, :, cols] = jnp.zeros((STATE, half), f32)
                else:
                    wires.arrived(r.cin.at[m], copies[m][1], origin)
                    value = r.cin[m].astype(f32)
                    r.sin[q, :, cols] = value
                    value = r.fac[q, 0:1, cols] * value + r.end[q, :, cols]
                if h + 1 < n:
                    r.cout[m] = value.astype(bf16)
                    copies[m][0].start()
        pl.when(place_in == h)(act)

    return hop


def named(names, refs):
    return types.SimpleNamespace(**dict(zip(names, refs)))


def forward_kernel(size, names, *refs):
    r = named(names, refs)
    here = place()
    a, c, b, s = here
    n, nx = size["so"], size["dpo"]
    mine = 2 * c + s
    own = r.tok.shape[0]
    r.span = span = 2 * own
    rows = r.w_in.shape[0]
    halves = r.wo_in.shape[0]
    depth = r.toks.shape[1]
    r.bc = r.act.at[:, XCOLS:ACT]
    wires = Wires(r.send, r.recv, r.local)
    follows = (s == 1) & (b + 1 < n)
    next_group = [(a, cc, jnp.minimum(b + 1, n - 1), ss) for cc in range(2) for ss in range(2)]
    prior = [(a, cc, jnp.maximum(b - 1, 0), 1) for cc in range(2)]
    met = greet(here, size, [(next_group, follows), (prior, b > 0)])

    wires.keep(r.w_in, r.wraw)()
    inner = r.wraw[:, INNER : 2 * INNER].astype(f32)
    for m in range(4):
        r.wxs[m] = class_runs(inner, size, m).astype(bf16)
    shared = widened(r.wraw[:, 2 * INNER :].astype(f32), rows, CCOLS - XCOLS)
    r.wsr[mine, a, b] = shared.astype(bf16)
    place_smalls(size, here, r)
    met()

    first = {}

    def begin(name, src, dst):
        waits = [wires.keep(src.at[mine], shard_of(dst, rows, a, c, b, s))]
        for rel in range(1, 4):
            _, cc, _, ss = member(here, rel)
            first[name, rel] = wires.slot()
            wires.start(src.at[2 * cc + ss], shard_of(dst, rows, a, c, b, s), first[name, rel], member(here, rel))
        return waits[0]

    def began(name, dst, wait):
        for rel in range(1, 4):
            _, cc, _, ss = member(here, rel)
            wires.arrived(shard_of(dst, rows, a, cc, b, ss), first[name, rel], member(here, rel))
        wait()

    wait_x = begin("x", r.wxs, r.wcx)
    spread_s = spread(wires, here, size, lambda aa, bb: r.wsr.at[mine, aa, bb])
    next(spread_s)
    for rel in range(1, 4):
        _, cc, _, ss = member(here, rel)
        first["s", rel] = wires.slot()
        wires.start(r.cvs.at[2 * cc + ss], r.cvy.at[rel - 1], first["s", rel], member(here, rel))
    gate = r.wraw[:, 0:INNER].astype(f32)
    for m in range(4):
        r.wgs[m] = class_runs(gate, size, m).astype(bf16)

    own_rows = lambda cc, ss: pl.ds(pl.multiple_of(cc * (span + PAD) + PAD + own * ss, 16), own)
    cot_rows = lambda cc, ss: pl.ds(pl.multiple_of(cc * span + own * ss, 16), own)
    pairs = {"t": (r.tok, r.toks, own_rows), "k": (r.cot, r.cots, cot_rows)}

    def begin_rows(key):
        src, dst, at = pairs[key]
        wait = wires.keep(src, dst.at[at(c, s)])
        for rel in (1, 2):
            first[key, rel] = wires.slot()
            wires.start(src, dst.at[at(c, s)], first[key, rel], member(here, rel))
        first[key, 3] = wires.slot()
        return wait

    def pass_rows(key):
        src, dst, at = pairs[key]
        wires.arrived(dst.at[at(c, 1 - s)], first[key, 1], member(here, 1))
        wires.start(dst.at[at(c, 1 - s)], dst.at[at(c, 1 - s)], first[key, 3], member(here, 2))

    def end_rows(key, wait):
        src, dst, at = pairs[key]
        for rel, ss in ((2, s), (3, 1 - s)):
            wires.arrived(dst.at[at(1 - c, ss)], first[key, rel], member(here, 2))
        wait()

    shares = []

    def share(aa):
        for rel in range(1, 4):
            shares.append((aa, rel, wires.slot()))
            wires.start(r.wsr.at[mine, aa], r.wsr.at[mine, aa], shares[-1][2], member(here, rel))

    began("x", r.wcx, wait_x)
    spread_x = spread(wires, here, size, lambda aa, bb: unit_of(r.wcx, rows, aa, bb))
    next(spread_x)
    wait_t = begin_rows("t")
    sub = iota((8, 128), 0)
    places = r.idin[...].astype(f32)
    tile = jnp.zeros((8, 128), f32)
    for j in range(own // 128):
        tile = jnp.where(sub == j, places[:, j * 128 : (j + 1) * 128], tile)
    r.ids[mine] = tile
    for rel in range(1, 4):
        first["i", rel] = wires.slot()
        wires.start(r.ids.at[mine], r.ids.at[mine], first["i", rel], member(here, rel))
    halo_rows = lambda cc: pl.ds(pl.multiple_of(cc * (span + PAD), 16), PAD)
    tail = r.tok.at[own - PAD : own]
    halo_slots, hid_slots = [wires.slot() for _ in range(4)], [wires.slot() for _ in range(4)]
    for k, device in enumerate(next_group):
        wires.start(tail, r.toks.at[halo_rows(c)], halo_slots[k], device, follows, halo_slots[0] + c)
        wires.start(r.ids.at[mine], r.hid.at[c], hid_slots[k], device, follows, hid_slots[0] + c)
    wait_g = begin("g", r.wgs, r.wg)

    @pl.when(b == 0)
    def _():
        for q in range(2):
            r.toks[q * (span + PAD) : q * (span + PAD) + PAD, :] = jnp.zeros((PAD, depth), bf16)
        r.hid[...] = jnp.zeros(r.hid.shape, f32)

    r.chosen[...] = class_heads(size, c, s)
    raw = jnp.where(sub == 0, widened(r.dtb_in[...], 1, 128), jnp.where(sub == 1, widened(r.alog_in[...], 1, 128), jnp.where(sub == 2, widened(r.skip_in[...], 1, 128), 0.0)))
    r.hp[...] = pick_heads(raw, r.chosen[...])
    r.hx[...] = pick_heads(jnp.broadcast_to(r.hp[2:3], (8, 128)), spread_heads())

    for rel in range(1, 4):
        wires.arrived(r.cvy.at[rel - 1], first["s", rel], member(here, rel))
    r.cvm[...] = (r.cvs[mine] + r.cvy[0]) + (r.cvy[1] + r.cvy[2])
    smalls = sum_all(wires, here, size, r.cvm, r.cvz, r.cvx)
    next(smalls)
    next(spread_s)
    next(spread_x)
    pass_rows("t")
    next(smalls)
    next(spread_s)
    next(spread_x)
    end_rows("t", wait_t)
    wait_k = begin_rows("k")
    for rel in range(1, 4):
        _, cc, _, ss = member(here, rel)
        wires.arrived(r.ids.at[2 * cc + ss], first["i", rel], member(here, rel))
    for sc in range(2):
        wires.arrived(r.toks.at[halo_rows(sc)], halo_slots[0] + sc, prior[sc], b > 0)
        wires.arrived(r.hid.at[sc], hid_slots[0] + sc, prior[sc], b > 0)
    per = own // CHUNK
    for q in range(2):
        top = jnp.broadcast_to(r.hid[q, per - 1 : per], (CHUNK, 128)).T[CHUNK - PAD :]
        r.idc[q * (span + PAD) : q * (span + PAD) + PAD, :] = jnp.where(b > 0, top, -1.0)
        for ss in range(2):
            for j in range(per):
                at = q * (span + PAD) + PAD + ss * own + j * CHUNK
                r.idc[at : at + CHUNK, :] = jnp.broadcast_to(r.ids[2 * q + ss, j : j + 1], (CHUNK, 128)).T
    small = next(smalls)
    r.cv[...] = small
    r.ng[...] = jnp.broadcast_to(small[5:6, :XCOLS], (8, XCOLS))
    r.gain1[...] = jnp.broadcast_to(
        jnp.concatenate([small[6:7], small[7:8, : depth - ACT]], axis=1), (8, depth)
    )
    block = (span + PAD) // 3
    for _ in range(n - 3):
        next(spread_s)
    share(a)
    began("g", r.wg, wait_g)
    spread_g = spread(wires, here, size, lambda aa, bb: unit_of(r.wg, rows, aa, bb))
    next(spread_g)
    loop(6, lambda i: phase_norm(r, i, block))
    for _ in range(n - 3):
        next(spread_x)
    next(spread_s)
    for h in range(1, nx):
        share(lax.rem(a + h, nx))
    next(spread_x)
    turns = []

    def turn(aa, bb, when):
        slot = wires.slot()
        other = lax.rem(bb, 2) != s
        here_too = lax.rem(bb, 2) == s
        if when is not None:
            other, here_too = other & when, here_too & when
        wires.start(r.wo.at[1, aa, bb // 2, s], r.wo.at[0, aa, bb // 2, s], slot, member(here, 1), other)
        turns.append((r.wo.at[0, aa, bb // 2, 1 - s], slot, member(here, 1), here_too))

    get_o = lambda aa, bb: r.wo.at[lax.rem(bb + s, 2), aa, bb // 2, s]
    wires.keep(r.wo_in, get_o(a, b))()
    spread_o = spread(wires, here, size, get_o, turn)
    next(spread_o)
    for aa, rel, slot in shares:
        _, cc, _, ss = member(here, rel)
        wires.arrived(r.wsr.at[2 * cc + ss, aa], slot, member(here, rel))
    for m in range(4):
        for aa in range(nx):
            for bb in range(n):
                at = (2 * bb + m % 2) * rows
                r.wcs[2 * aa + m // 2, at : at + rows, :] = r.wsr[m, aa, bb]
    w = r.wcs[:, :, 2 * STATE :]
    r.dtr[...] = pick_heads(mm(r.normed[...], w.reshape(w.shape[0] * w.shape[1], 128)), r.chosen[...])
    steps = list(range(1, n))
    for q in range(2):
        def columns(ct, q=q):
            at = pl.multiple_of(ct * 256, 256)
            phase_in(r, q, r.wcx[:, :, pl.ds(at, 256)], at)

        loop(XCOLS // 256, columns)
        phase_in(r, q, r.wcs[:, :, 0 : 2 * STATE], XCOLS)
        if steps:
            next(spread_g)
            steps.pop()
    chunks = 2 * span // CHUNK
    loop(chunks, lambda i: phase_decay(r, i))
    phase_states(r)
    hop = chain(wires, here, size, r, 1)
    hop(0)
    while steps:
        next(spread_g)
        steps.pop()
    pass_rows("k")
    next(spread_o)
    flushes = [wires.keep(src, dst) for src, dst in ((r.normed, r.normed_o), (r.pc, r.pc_o), (r.sp, r.sp_o), (r.act, r.act_o), (r.xdt, r.xdt_o), (r.wcx, r.wcx_o), (r.wcs, r.wcs_o), (r.dtm, r.dtm_o), (r.run, r.run_o), (r.dtr, r.dtr_o), (r.idc, r.idc_o))]

    def inner_z(q, ct):
        wide = pl.ds(pl.multiple_of(ct * 256, 256), 256)
        w = r.wg[:, :, wide]
        lines = r.normed[q * (span + PAD) + PAD : (q + 1) * (span + PAD), :]
        r.z[q * span : (q + 1) * span, wide] = mm(lines, w.reshape(w.shape[0] * w.shape[1], 256))

    def fill_a():
        loop(chunks // 2, lambda i: phase_inside(r, i))

    def fill_b():
        next(spread_g)
        for q in range(2):
            loop(XCOLS // 256, lambda ct, q=q: inner_z(q, ct))

    def fill_c():
        loop(chunks, lambda i: phase_inside(r, i), chunks // 2)

    fillers = [fill_a, fill_b, fill_c]
    for h in range(1, n):
        if fillers:
            fillers.pop(0)()
        hop(h)
        if h < n - 1:
            next(spread_o)
    for fill in fillers:
        fill()
    end_rows("k", wait_k)
    flushes += [wires.keep(src, dst) for src, dst in ((r.wg, r.wg_o), (r.z, r.z_o), (r.cots, r.cots_o))]
    next(spread_o)
    for landing, slot, device, when in turns:
        wires.arrived(landing, slot, device, when)
    flushes.append(wires.keep(r.wo.at[0], r.wo_o))
    per_x = XCOLS // nx

    def back_product(k):
        w = r.wo[0, k]
        r.gg[:, pl.ds(pl.multiple_of(k * per_x, 128), per_x)] = mm(r.cots[...], w.reshape(per_x, depth), ((1,), (1,)))

    loop(nx, back_product)
    flushes.append(wires.keep(r.gg, r.gg_o))
    loop(chunks, lambda i: phase_carried(r, i))
    flushes += [wires.keep(src, dst) for src, dst in ((r.y, r.y_o), (r.st, r.st_o))]
    wires.finish()
    for flush in flushes:
        flush()


def backward_kernel(size, names, *refs):
    r = named(names, refs)
    here = place()
    a, c, b, s = here
    n, nx = size["so"], size["dpo"]
    mine = 2 * c + s
    own, depth = r.tok.shape
    r.span = span = 2 * own
    rows = r.rest.shape[0]
    halves = r.oo.shape[0]
    lines = span + PAD
    chunks = 2 * span // CHUNK
    per_dp = r.gg_w.shape[1]
    half_cols = [slice(k * XCOLS, (k + 1) * XCOLS) for k in range(2)]
    wires = Wires(r.send, r.recv, r.local)
    fetched = {}
    for name in ("y", "z", "gg", "wo", "run", "idc", "normed", "dtm", "dtr", "wg", "wcx", "wcs"):
        fetched[name] = wires.keep(getattr(r, name + "_i"), getattr(r, name))
    fetched["bc"] = wires.keep(r.act_i.at[:, XCOLS:ACT], r.bc)
    fetched["cots"] = wires.keep(r.cots_i, r.cots.at[0 : 2 * span])
    need = lambda *keys: [fetched.pop(key)() for key in keys]
    follows = (s == 1) & (b + 1 < n)
    next_pair = [(a, c, jnp.minimum(b + 1, n - 1), ss) for ss in range(2)]
    prior = (a, c, jnp.maximum(b - 1, 0), 1)
    met = greet(here, size, [(next_pair, follows), ([prior], b > 0)])
    r.gx = r.z
    r.chosen[...] = class_heads(size, c, s)
    r.nggrad[...] = jnp.zeros(r.nggrad.shape, f32)
    r.tally[...] = jnp.zeros(r.tally.shape, f32)
    r.cvgrad[...] = jnp.zeros(r.cvgrad.shape, f32)
    for q in range(2):
        r.gpc[q * lines : q * lines + PAD, :] = jnp.zeros((PAD, CCOLS), bf16)

    need("y", "z", "gg")
    loop(chunks, lambda i: phase_sums(r, i))
    met()
    slots = {}
    for rel in range(1, 4):
        slots[rel] = wires.slot()
        wires.start(r.sums.at[0], r.sums.at[rel], slots[rel], member(here, rel))
    need("cots", "wo", "bc", "run", "idc")
    for rel in range(1, 4):
        wires.arrived(r.sums.at[rel], slots[rel], member(here, rel))
    loop(chunks, lambda i: phase_gate(r, i))

    def out_grad(k):
        left = r.gated[:, pl.ds(pl.multiple_of(k * per_dp, 128), per_dp)]
        for h, cols in enumerate(half_cols):
            r.go[2 * k + h] = mm(left, r.cots[0 : 2 * span, cols], ((0,), (0,))).astype(bf16)

    loop(nx, out_grad)
    units_o = 2 * halves
    get_o = lambda aa, bb: r.go.at[pl.ds(2 * aa, 2), pl.ds(pl.multiple_of((bb // 2) * units_o, 16), units_o)]
    sends_o = []
    collect_o = collect_out(wires, here, size, get_o, r.xo, r.yo, r.zo, r.oo, sends_o)
    next(collect_o)

    x_copy = lambda i, slot: pltpu.make_async_copy(
        r.act_i.at[pl.ds(pl.multiple_of(i * CHUNK, CHUNK), CHUNK), 0:XCOLS], r.xw.at[slot], r.stream.at[6 + slot]
    )
    x_copy(0, 0).start()

    def states_chunk(i):
        slot = lax.rem(i, 2)

        @pl.when(i + 1 < chunks)
        def _():
            x_copy(i + 1, 1 - slot).start()

        x_copy(i, slot).wait()
        phase_back_states(r, i, r.xw[slot])

    loop(chunks, states_chunk)
    phase_back_chain(r)
    hop = chain(wires, here, size, r, -1)
    hop(0)

    need("normed")

    def gate_grad(k):
        at = pl.ds(pl.multiple_of(k * per_dp, 128), per_dp)
        total = jnp.zeros((per_dp, XCOLS), f32)
        for q in range(2):
            left = r.normed[q * lines + PAD : (q + 1) * lines, at]
            total = total + mm(left, r.gpg[q * span : (q + 1) * span, :], ((0,), (0,)))
        r.gg_w[k] = total.astype(bf16)

    loop(depth // per_dp, gate_grad)
    close_g, wait_g = finish_units(wires, here, rows, r.zg, r.og)
    collect_g = collect(wires, here, size, lambda aa, bb: unit_of(r.gg_w, rows, aa, bb), r.xg, r.zg, close_g)
    next(collect_g)

    def mix(k):
        tile = pl.ds(pl.multiple_of(k * 256, 256), 256)
        w = r.wo[:, :, :, :, tile]
        r.cots[0 : 2 * span, tile] = mm(r.gated[...], w.reshape(XCOLS, 256)).astype(bf16)

    loop(depth // 256, mix)
    r.xdt = r.gated
    fetched["xdt"] = wires.keep(r.xdt_i, r.xdt)
    m_slots = [wires.slot(), wires.slot()]
    half = lambda cc: pl.ds(pl.multiple_of(cc * span, 16), span)
    m_sent = wires.start(r.cots.at[half(1 - c)], r.t1.at[0:span], m_slots[0], member(here, 2))

    entries = []
    need("xdt")

    def fill_a():
        loop(chunks // 2, lambda i: phase_back_inside(r, i))

    def fill_b():
        wires.arrived(r.t1.at[0:span], m_slots[0], member(here, 2))
        at = pl.ds(pl.multiple_of(own * (1 - s), 16), own)
        r.t1[at, :] = (r.t1[at, :].astype(f32) + r.cots[pl.ds(pl.multiple_of(c * span + own * (1 - s), 16), own), :].astype(f32)).astype(bf16)
        entries.append(wires.start(r.t1.at[at], r.t2, m_slots[1], member(here, 1)))
        loop(chunks, lambda i: phase_back_inside(r, i), chunks // 2)

    fillers = [lambda: None, fill_a, fill_b]
    for h in range(1, n):
        if fillers:
            fillers.pop(0)()
        hop(h)
    for fill in fillers:
        fill()
    for _ in range(n):
        next(collect_o)
    need("dtm", "dtr")
    state_copy = lambda i, slot: pltpu.make_async_copy(r.st_i.at[i], r.stw.at[slot], r.stream.at[4 + slot])
    state_copy(0, 0).start()
    x_copy(0, 0).start()

    def close_chunk(i):
        slot = lax.rem(i, 2)

        @pl.when(i + 1 < chunks)
        def _():
            state_copy(i + 1, 1 - slot).start()
            x_copy(i + 1, 1 - slot).start()

        state_copy(i, slot).wait()
        x_copy(i, slot).wait()
        phase_back_close(r, i, r.stw[slot], r.xw[slot])

    quarter = chunks // 4
    for k in range(4):
        loop((k + 1) * quarter, close_chunk, k * quarter)
        if k == 1:
            next(collect_o)
        if 0 < k < n - 1:
            next(collect_g)
    for k in range(2):
        fetched["tok", k] = wires.keep(r.tok.at[:, half_cols[k]], r.gated.at[k * own : (k + 1) * own])
        fetched["cot", k] = wires.keep(r.cot.at[:, half_cols[k]], r.gated.at[(2 + k) * own : (3 + k) * own])
    wide, narrow = XCOLS // 128, 2 * STATE // 128
    stream = r.stream

    def tile_place(k):
        early = k < 2 * wide
        late = k - 2 * wide
        return jnp.where(early, k // wide, late // narrow), jnp.where(early, k % wide, wide + late % narrow)

    def tile_copies(k, slot):
        q, lt = tile_place(k)
        cols = pl.ds(pl.multiple_of(lt * 128, 128), 128)
        top = pl.multiple_of(q * lines + PAD - 8, 8)
        flat = pl.multiple_of(q * span, 16)
        return (
            pltpu.make_async_copy(r.pc_i.at[pl.ds(top, span + 8), cols], r.pcw.at[slot], stream.at[2 * slot]),
            pltpu.make_async_copy(r.sp_i.at[pl.ds(flat, span), cols], r.spw.at[slot], stream.at[2 * slot + 1]),
        )

    for copy in tile_copies(jnp.int32(0), 0):
        copy.start()

    def conv_tiles(q, first, count, grads, lead):
        def conv_tile(k):
            slot = lax.rem(k, 2)

            @pl.when(k + 1 < 2 * (wide + narrow))
            def _():
                for copy in tile_copies(k + 1, 1 - slot):
                    copy.start()

            for copy in tile_copies(k, slot):
                copy.wait()
            lt = k - first
            grad = grads[q * span : (q + 1) * span, pl.ds(pl.multiple_of(lt * 128, 128), 128)]
            phase_back_conv(r, q, lt + lead, grad, r.pcw[slot], r.spw[slot])

        loop(first + count, conv_tile, first)

    conv_tiles(0, 0, wide, r.gx, 0)
    for _ in range(n - 3):
        next(collect_g)
    conv_tiles(1, wide, wide, r.gx, 0)
    for entry in sends_o:
        wires.sent(entry)
    r.gcx = r.go

    def in_grad(k):
        at = pl.ds(pl.multiple_of(k * per_dp, 128), per_dp)
        r.gcx[k] = mm(r.normed[:, at], r.gpc[:, 0:XCOLS], ((0,), (0,))).astype(bf16)

    def rest_grad(k):
        at = pl.ds(pl.multiple_of(k * per_dp, 128), per_dp)
        value = mm(r.normed[:, at], r.gpc[:, XCOLS:CCOLS], ((0,), (0,))).astype(bf16)
        for bb in range(n):
            for ss in range(2):
                first = (2 * bb + ss) * rows
                r.gs[2 * (k % 2) + ss, k // 2, bb] = value[first : first + rows]

    loop(depth // per_dp, in_grad)
    close_x, wait_x = finish_units(wires, here, rows, r.zcx, r.ocx)
    collect_x = collect(wires, here, size, lambda aa, bb: unit_of(r.gcx, rows, aa, bb), r.xcx, r.zcx, close_x)
    next(collect_x)
    next(collect_g)
    conv_tiles(0, 2 * wide, narrow, r.gbc, wide)
    conv_tiles(1, 2 * wide + narrow, narrow, r.gbc, wide)
    loop(depth // per_dp, rest_grad)
    collect_s = collect_shared(wires, here, size, r.gs, r.s1, r.s2, r.s3, r.s4, r.rest)
    next(collect_s)
    next(collect_o)

    need(("tok", 0), ("tok", 1), ("cot", 0), ("cot", 1))
    wires.arrived(r.t2, m_slots[1], member(here, 1))
    here_rows = pl.ds(pl.multiple_of(c * span + own * s, 16), own)
    for k, cols in enumerate(half_cols):
        branch = r.cots[here_rows, cols].astype(f32) + r.t1[pl.ds(pl.multiple_of(own * s, 16), own), cols].astype(f32) + r.t2[:, cols].astype(f32)
        r.t2[:, cols] = (r.gated[k * own : (k + 1) * own, :].astype(f32) + branch).astype(bf16)
    wires.keep(r.t2, r.mixed)()
    wires.sent(m_sent)
    wires.sent(entries[0])
    for k, rel in enumerate((2, 1)):
        pl.semaphore_signal(r.ack.at[k], inc=1, device_id=member(here, rel), device_id_type=MESH)

    need("wg", "wcx", "wcs")
    next(collect_s)

    def normed_grad(k):
        cols = pl.ds(pl.multiple_of(k * per_dp, 128), per_dp)
        for q in range(2):
            value = mm(r.gpc[q * lines : (q + 1) * lines, 0:XCOLS], r.wcx[k], ((1,), (1,)))
            value = value + mm(r.gpc[q * lines : (q + 1) * lines, XCOLS:CCOLS], r.wcs[k], ((1,), (1,)))
            extra = mm(r.gpg[q * span : (q + 1) * span, :], r.wg[k], ((1,), (1,)))
            value = value + jnp.concatenate([jnp.zeros((PAD, per_dp), f32), extra], axis=0)
            r.cots[q * lines : (q + 1) * lines, cols] = value.astype(bf16)

    loop(depth // per_dp, normed_grad)
    next(collect_x)
    next(collect_s)
    t_slots = [wires.slot() for _ in range(4)]
    seq_rows = lambda cc: pl.ds(pl.multiple_of(cc * lines, 16), lines)
    pl.semaphore_wait(r.ack.at[0], 1)
    wires.start(r.cots.at[seq_rows(1 - c)], r.t1, t_slots[0], member(here, 2))
    next(collect_g)
    wires.arrived(r.t1, t_slots[0], member(here, 2))

    def pair_sum(at, count, cols):
        ours = r.cots[pl.ds(pl.multiple_of(c * lines + at, 16), count), cols]
        return ours.astype(f32) + r.t1[pl.ds(pl.multiple_of(at, 16), count), cols].astype(f32)

    tg = r.y
    other = PAD + own * (1 - s)
    for k, cols in enumerate(half_cols):
        tg[k * own : (k + 1) * own, :] = pair_sum(PAD + own * s, own, cols)
        r.t1[pl.ds(pl.multiple_of(other, 16), own), cols] = pair_sum(other, own, cols).astype(bf16)
        r.t1[0:PAD, cols] = pair_sum(0, PAD, cols).astype(bf16)
    pl.semaphore_wait(r.ack.at[1], 1)
    wires.start(r.t1.at[pl.ds(pl.multiple_of(other, 16), own)], r.t2, t_slots[1], member(here, 1))
    for ss in range(2):
        wires.start(r.t1.at[0:PAD], r.th.at[ss], t_slots[2 + ss], prior, (b > 0) & (s == ss))
    next(collect_x)
    next(collect_s)
    wait_g()
    wires.arrived(r.t2, t_slots[1], member(here, 1))
    for ss in range(2):
        wires.arrived(r.th.at[ss], t_slots[2 + ss], next_pair[ss], follows)
    for k, cols in enumerate(half_cols):
        tg[k * own : (k + 1) * own, :] += r.t2[:, cols].astype(f32)

        @pl.when(follows)
        def _():
            tg[(k + 1) * own - PAD : (k + 1) * own, :] += r.th[0, :, cols].astype(f32) + r.th[1, :, cols].astype(f32)

    next(collect_x)
    r.pgrad[...] = jnp.zeros(r.pgrad.shape, f32)

    def final(i):
        at = [pl.ds(pl.multiple_of(k * own + i * 64, 64), 64) for k in range(4)]
        t = [r.gated[at[k], :].astype(f32) for k in range(2)]
        g = [tg[at[k], :] for k in range(2)]
        u = [g[k] * r.gain1[0:1, half_cols[k]] for k in range(2)]
        row = lambda left, right: jnp.sum(left[0] * right[0] + left[1] * right[1], axis=1, keepdims=True) / depth
        scale = lax.rsqrt(row(t, t) + EPSILON)
        tilt = scale * scale * scale * row(u, t)
        for k in range(2):
            tg[at[k], :] = r.gated[at[2 + k], :].astype(f32) + scale * u[k] - t[k] * tilt
            r.pgrad[0:1, half_cols[k]] += jnp.sum(g[k] * t[k] * scale, axis=0, keepdims=True)

    loop(own // 64, final)
    next(collect_x)
    next(collect_s)
    flushes = [wires.keep(tg.at[k * own : (k + 1) * own], r.tgrad.at[:, half_cols[k]]) for k in range(2)]
    sub = iota((8, ACT), 0)
    row5 = jnp.concatenate([r.nggrad[0:1], r.tally[0:1], r.tally[1:2]], axis=1)
    row7 = widened(jnp.concatenate([r.pgrad[0:1, ACT:], r.tally[2:3]], axis=1), 1, ACT)
    r.cvm[...] = r.cvgrad[...] + jnp.where(sub == 5, row5, 0.0) + jnp.where(sub == 6, r.pgrad[0:1, :ACT], 0.0) + jnp.where(sub == 7, row7, 0.0)
    smalls = sum_all(wires, here, size, r.cvm, r.cvz, r.cvx)
    next(smalls)
    pieces = INNER // XCOLS

    def assemble(classes, first):
        for p in range(pieces):
            at = (first + p) * rows
            joined = joined_runs([classes[m].astype(f32) for m in range(4)], size, p * XCOLS, XCOLS)
            r.gg[at : at + rows, :] = joined
            flushes.append(wires.keep(r.gg.at[at : at + rows], r.iw.at[:, (first + p) * XCOLS : (first + p + 1) * XCOLS]))

    assemble(r.og, 0)
    next(smalls)
    for _ in range(n - 4):
        next(collect_x)
    r.os[mine] = next(smalls)
    s_slots = {}
    for rel in range(1, 4):
        s_slots[rel] = wires.slot()
        wires.start(r.os.at[mine], r.os.at[mine], s_slots[rel], member(here, rel))
    next(collect_x)
    for rel in range(1, 4):
        _, cc, _, ss = member(here, rel)
        wires.arrived(r.os.at[2 * cc + ss], s_slots[rel], member(here, rel))
    final_smalls(size, here, r)
    wait_x()
    assemble(r.ocx, pieces)
    wires.finish()
    for flush in flushes:
        flush()


def fast_body(size, tokens, segment_ids, pre_gain, in_weight, conv_weight, conv_bias, dt_bias, a_log, skip_gain, norm_gain, out_weight, cotangent):
    n, nx = size["so"], size["dpo"]
    tok, cot = tokens[0], cotangent[0]
    own, depth = tok.shape
    span = 2 * own
    rows, halves = in_weight.shape[0], out_weight.shape[0]
    chunks = 2 * span // CHUNK
    total, lines = 2 * span, 2 * (span + PAD)
    dps = 2 * nx
    per_dp = 2 * n * rows
    rest = CCOLS - XCOLS

    hbm_state = dict(
        normed=((lines, depth), bf16), pc=((lines, ACT), f32), sp=((total, ACT), f32), act=((total, ACT), f32),
        xdt=((total, XCOLS), bf16), wcx=((dps, per_dp, XCOLS), bf16), wcs=((dps, per_dp, rest), bf16), wg=((dps, per_dp, XCOLS), bf16),
        wo=((nx, n // 2, 2, halves, depth), bf16), cots=((total, depth), bf16), z=((total, XCOLS), f32), gg=((total, XCOLS), f32),
        y=((total, XCOLS), f32), st=((chunks, STATE, XCOLS), f32), dtm=((total, 128), f32), run=((total, 128), f32),
        dtr=((lines, 128), f32), idc=((lines, 128), f32),
    )
    vmem_state = dict(
        fac=((2, 8, XCOLS), f32), pex=((chunks, 8, XCOLS), f32), cv=((8, ACT), f32), ng=((8, XCOLS), f32),
        gain1=((8, depth), f32), hp=((8, 128), f32), hx=((8, XCOLS), f32),
    )
    common = dict(
        cum=((chunks, 8, XCOLS), f32), end=((2, STATE, XCOLS), f32), sin=((2, STATE, XCOLS), f32),
        cin=((4, STATE, XCOLS // 2), bf16), cout=((4, STATE, XCOLS // 2), bf16),
        cvm=((8, ACT), f32), cvz=((n, 8, ACT), f32), cvx=((nx, 8, ACT), f32), chosen=((128, 128), bf16),
    )
    copies = 100 + 12 * n * nx
    semaphores = [pltpu.SemaphoreType.DMA((copies,)), pltpu.SemaphoreType.DMA((copies,)), pltpu.SemaphoreType.DMA((40,))]
    shape = lambda spec: jax.ShapeDtypeStruct(*spec)

    row = lambda v: v[None]
    inputs = dict(
        w_in=in_weight, wo_in=out_weight, tok=tok, cot=cot, idin=segment_ids, conv_w=conv_weight, conv_b=row(conv_bias),
        norm_in=row(norm_gain), pre_in=row(pre_gain), dtb_in=row(dt_bias), alog_in=row(a_log), skip_in=row(skip_gain),
    )
    scratch = dict(hbm_state)
    scratch.update(common)
    scratch.update(
        wo=((2, nx, n // 2, 2, halves, depth), bf16), toks=((lines, depth), bf16), ids=((4, 8, 128), f32), hid=((2, 8, 128), f32),
        cvs=((4, 8, ACT), f32), cvy=((3, 8, ACT), f32), wraw=(in_weight.shape, bf16), wxs=((4, rows, XCOLS), bf16),
        wgs=((4, rows, XCOLS), bf16), wsr=((4, nx, n, rows, rest), bf16),
    )
    names = list(inputs) + [k + "_o" for k in hbm_state] + list(vmem_state) + list(scratch) + ["send", "recv", "local"]
    outs = pl.pallas_call(
        functools.partial(forward_kernel, size, names),
        out_shape=[shape(v) for v in hbm_state.values()] + [shape(v) for v in vmem_state.values()],
        in_specs=[HBM] * 4 + [VMEM] * 8,
        out_specs=[HBM] * len(hbm_state) + [VMEM] * len(vmem_state),
        scratch_shapes=[pltpu.VMEM(*v) for v in scratch.values()] + semaphores,
        compiler_params=pltpu.CompilerParams(collective_id=1, has_side_effects=True, vmem_limit_bytes=64 * 2**20 - 2**16),
    )(*inputs.values())
    held = dict(zip(hbm_state, outs))
    small = dict(zip(vmem_state, outs[len(hbm_state) :]))

    results = dict(
        tgrad=((own, depth), f32), mixed=((own, depth), bf16), iw=((rows, 2 * INNER), f32), rest=((rows, rest), f32),
        oo=((halves, depth), f32), smo=((4, 8, 128), f32), cwo=(conv_weight.shape, f32),
    )
    scratch = {k: v for k, v in hbm_state.items() if k not in ("pc", "sp", "cots", "xdt", "st", "act")}
    scratch.update(common)
    unit, unit_o = (2, 2 * rows, XCOLS), (2, 2 * halves, XCOLS)
    scratch.update(
        cots=((lines, depth), bf16), gbc=((total, 2 * STATE), f32),
        gated=((total, XCOLS), bf16), gpg=((total, XCOLS), bf16), gpc=((lines, CCOLS), bf16), drun=((total, 128), f32),
        sums=((4, chunks, 8, 128), f32), nggrad=((8, XCOLS), f32), tally=((8, 128), f32), cvgrad=((8, ACT), f32),
        pgrad=((8, depth), f32), go=((dps, n * halves, XCOLS), bf16), gg_w=((dps, per_dp, XCOLS), bf16), gs=((4, nx, n, rows, rest), bf16),
        xcx=((nx - 1, n) + unit, bf16), xg=((nx - 1, n) + unit, bf16), xo=((nx - 1, n // 2) + unit_o, bf16),
        zcx=((n - 1,) + unit, bf16), zg=((n - 1,) + unit, bf16), zo=((n - 1, 2, halves, XCOLS), bf16), yo=((n // 2, 2, halves, XCOLS), bf16),
        s1=((2, nx, n, rows, rest), bf16), s2=((nx, n, rows, rest), bf16), s3=((nx - 1, n, rows, rest), bf16), s4=((n - 1, rows, rest), bf16),
        ocx=((4, rows, XCOLS), bf16), og=((4, rows, XCOLS), bf16), os=((4, 8, ACT), f32),
        stw=((2, STATE, XCOLS), f32), xw=((2, CHUNK, XCOLS), f32), bc=((total, 2 * STATE), f32), t1=((span + PAD, depth), bf16),
        t2=((own, depth), bf16), th=((2, PAD, depth), bf16), pcw=((2, span + 8, 128), f32), spw=((2, span, 128), f32),
    )
    names = [k + "_i" for k in hbm_state] + ["tok", "cot"] + list(vmem_state) + list(results) + list(scratch)
    names += ["send", "recv", "local", "stream", "ack"]
    outs = pl.pallas_call(
        functools.partial(backward_kernel, size, names),
        out_shape=[shape(v) for v in results.values()],
        in_specs=[HBM] * (len(hbm_state) + 2) + [VMEM] * len(vmem_state),
        out_specs=[HBM] * 3 + [VMEM] * (len(results) - 3),
        scratch_shapes=[pltpu.VMEM(*v) for v in scratch.values()] + semaphores + [pltpu.SemaphoreType.DMA((8,)), pltpu.SemaphoreType.REGULAR((2,))],
        compiler_params=pltpu.CompilerParams(collective_id=2, has_side_effects=True, vmem_limit_bytes=64 * 2**20 - 2**16),
    )(*held.values(), tok, cot, *small.values())
    out = dict(zip(results, outs))
    smo = out["smo"]
    in_weight_grad = jnp.concatenate([out["iw"], out["rest"][:, : in_weight.shape[1] - 2 * INNER]], axis=1)
    return (
        out["mixed"][None], out["tgrad"][None], smo[2, 0, : pre_gain.shape[0]], in_weight_grad, out["cwo"], smo[0, 4, : conv_bias.shape[0]],
        smo[3, 0, :HEADS], smo[3, 1, :HEADS], smo[3, 2, :HEADS], smo[1, 5, : norm_gain.shape[0]], out["oo"],
    )


def specs(dp, seq):
    both = dp + seq
    ins = (
        P(dp, seq, None), P(dp, seq), P(both), P(both, None), P(both, None), P(both),
        P(), P(), P(), P(both), P(both, None), P(dp, seq, None),
    )
    outs = (
        P(dp, seq, None), P(dp, seq, None), P(both), P(both, None), P(both, None), P(both),
        P(), P(), P(), P(both), P(both, None),
    )
    return ins, outs


def solution(mesh):
    dp, seq = mesh.shape["dp"], mesh.shape["seq"]
    fine = Mesh(mesh.devices.reshape(dp // 2, 2, seq // 2, 2), AXES)
    size = dict(fine.shape)

    def choose(*args):
        ok = args[0].shape[0] == dp and args[0].shape[1] == seq * GROUP and size["so"] % 2 == 0
        ok = ok and INNER % (dp * seq * HEADDIM // 2) == 0 and args[3].shape[0] % (dp * seq * 16) == 0 and HEADS % (dp * seq // 2) == 0 and args[3].shape[0] == 2 * XCOLS
        if ok:
            ins, outs = specs(AXES[:2], AXES[2:])
            return jax.shard_map(functools.partial(fast_body, size), mesh=fine, in_specs=ins, out_specs=outs, check_vma=False)(*args)
        ins, outs = specs(("dp",), ("seq",))
        return jax.shard_map(whole_body, mesh=mesh, in_specs=ins, out_specs=outs, check_vma=False)(*args)

    return choose
```

```python
import functools
import types

import jax
import jax.numpy as jnp
from jax import lax
from jax.experimental import pallas as pl
from jax.experimental.pallas import tpu as pltpu
from jax.sharding import Mesh
from jax.sharding import PartitionSpec as P

HEADS = 48
HEADDIM = 64
STATE = 128
CONVW = 4
GROUP = 256
INNER = 3072
XBC = 3328


HIGHEST = lax.Precision.HIGHEST
EPSILON = 1e-05


def passed_along(block, axis, distance):
    devices = range(lax.axis_size(axis))
    route = [(i - distance, i) for i in devices if i - distance in devices]
    return lax.ppermute(block, axis, route)


def shortened(shard):
    return jax.tree.map(lambda a: a.astype(jnp.bfloat16) if a.dtype == jnp.float32 else a, shard)


def rms_scale(values, gain):
    return values * lax.rsqrt(jnp.mean(values * values, axis=-1, keepdims=True) + EPSILON) * gain


def gating(values, gates, gain):
    return rms_scale(values * jax.nn.silu(gates), gain)


def group_math(state, before, heads_x, b_rows, c_rows, steps_dt, log_decay, doc_ids):
    length = doc_ids.shape[0]
    running = jnp.cumsum(log_decay, axis=0)
    causal = jnp.arange(length)[:, None] >= jnp.arange(length)[None, :]
    linked = ((doc_ids[:, None] == doc_ids[None, :]) & causal)[:, :, None]
    gaps = running[:, None, :] - running[None, :, :]
    decays = jnp.exp(jnp.where(linked, gaps, 0.0)) * linked
    scores = jnp.dot(c_rows, b_rows.T, precision=HIGHEST)
    mixing = decays * scores[:, :, None] * steps_dt[None, :, :]
    inside = jnp.einsum("tsh,shp->thp", mixing, heads_x, precision=HIGHEST)
    alive = (doc_ids == before)[:, None]
    enter = jnp.exp(running) * alive
    carried = jnp.einsum("tn,hpn->thp", c_rows, state, precision=HIGHEST) * enter[:, :, None]
    last_id = doc_ids[length - 1]
    kept = (doc_ids == last_id)[:, None]
    weights_end = jnp.exp(running[length - 1][None, :] - running) * kept * steps_dt
    fresh = jnp.einsum("sh,shp,sn->hpn", weights_end, heads_x, b_rows, precision=HIGHEST)
    passed = jnp.exp(running[length - 1]) * (last_id == before)
    return (inside + carried, fresh + passed[:, None, None] * state)


def contract_rows(left, right):
    return lax.dot_general(
        left, right, (((0,), (0,)), ((), ())), preferred_element_type=jnp.float32
    )


def contract_cols(left, right):
    return lax.dot_general(
        left, right, (((1,), (1,)), ((), ())), preferred_element_type=jnp.float32
    )


def whole_body(
    tokens,
    segment_ids,
    pre_gain,
    in_weight,
    conv_weight,
    conv_bias,
    dt_bias,
    a_log,
    skip_gain,
    norm_gain,
    out_weight,
    cotangent,
):
    tok_rows = tokens[0].astype(jnp.float32)
    doc_ids = segment_ids[0]
    length = doc_ids.shape[0]
    margin = CONVW - 1
    count = length // GROUP
    shards = (pre_gain, in_weight, conv_weight, conv_bias, norm_gain, out_weight)
    gathered = (
        lax.all_gather(shards[0], ("dp", "seq"), axis=0, tiled=True),
        lax.all_gather(shards[1], ("dp", "seq"), axis=0, tiled=True),
        lax.all_gather(shards[2], ("dp", "seq"), axis=0, tiled=True),
        lax.all_gather(shards[3], ("dp", "seq"), axis=0, tiled=True),
        lax.all_gather(shards[4], ("dp", "seq"), axis=0, tiled=True),
        lax.all_gather(shards[5], ("dp", "seq"), axis=0, tiled=True),
    )
    normed, pre_back = jax.vjp(rms_scale, tok_rows, gathered[0].astype(jnp.float32))
    normed_low = normed.astype(jnp.bfloat16)
    projected = jnp.dot(normed_low, gathered[1], preferred_element_type=jnp.float32)
    gate_z = projected[:, :INNER]
    conv_in = projected[:, INNER : INNER + XBC]
    dt_raw = projected[:, INNER + XBC :]
    halo_rows, halo_ids = (
        passed_along(conv_in[length - margin :].astype(jnp.bfloat16), "seq", 1).astype(jnp.float32),
        passed_along(
            doc_ids[length - margin :].astype(jnp.float32).astype(jnp.bfloat16), "seq", 1
        ).astype(jnp.float32),
    )
    ext_ids = jnp.concatenate([halo_ids.astype(jnp.int32), doc_ids])
    prior_id = ext_ids[margin - 1]

    def convolve(extended, kernel, offset_bias):
        total = offset_bias
        for offset in range(CONVW):
            taps = extended[offset : offset + length]
            linked = (ext_ids[offset : offset + length] == doc_ids)[:, None]
            total = total + jnp.where(linked, taps, 0.0) * kernel[:, offset]
        return jax.nn.silu(total)

    activated, conv_back = jax.vjp(
        convolve,
        jnp.concatenate([halo_rows, conv_in]),
        gathered[2].astype(jnp.float32),
        gathered[3].astype(jnp.float32),
    )

    def zero_state(acts_in, raw_in, shift_in, rate_in):
        heads_x = acts_in[:, :INNER].reshape(length, HEADS, HEADDIM)
        b_rows = acts_in[:, INNER : INNER + STATE]
        c_rows = acts_in[:, INNER + STATE :]
        steps_dt = jax.nn.softplus(raw_in + shift_in)
        log_decay = -jnp.exp(rate_in) * steps_dt
        befores = jnp.concatenate([prior_id[None], doc_ids.reshape(count, GROUP)[:-1, GROUP - 1]])

        def step(state, item):
            out, new_state = group_math(state, *item)
            return (new_state, out)

        items = (
            befores,
            heads_x.reshape(count, GROUP, HEADS, HEADDIM),
            b_rows.reshape(count, GROUP, STATE),
            c_rows.reshape(count, GROUP, STATE),
            steps_dt.reshape(count, GROUP, HEADS),
            log_decay.reshape(count, GROUP, HEADS),
            doc_ids.reshape(count, GROUP),
        )
        final, outs = lax.scan(step, jnp.zeros((HEADS, HEADDIM, STATE), jnp.float32), items)
        factor = jnp.exp(jnp.sum(log_decay, axis=0)) * (doc_ids[length - 1] == prior_id)
        return (outs.reshape(length, HEADS, HEADDIM), factor, final)

    def incoming(acts_in, raw_in, shift_in, rate_in, start_state):
        steps_dt = jax.nn.softplus(raw_in + shift_in)
        running = jnp.cumsum(-jnp.exp(rate_in) * steps_dt, axis=0)
        factor = jnp.exp(running) * (doc_ids == prior_id)[:, None]
        c_rows = acts_in[:, INNER + STATE :]
        return (
            jnp.einsum("tn,hpn->thp", c_rows, start_state, precision=HIGHEST) * factor[:, :, None]
        )

    (local_y, factor, local_state), zero_back = jax.vjp(
        zero_state, activated, dt_raw, dt_bias, a_log
    )
    identity = (jnp.ones((HEADS,), jnp.float32), jnp.zeros((HEADS, HEADDIM, STATE), jnp.float32))

    def forward_turn(index, carry_state):
        return passed_along(factor[:, None, None] * carry_state + local_state, "seq", 1)

    start_state = lax.fori_loop(0, lax.axis_size("seq") - 1, forward_turn, identity[1])
    carried_y, in_back = jax.vjp(incoming, activated, dt_raw, dt_bias, a_log, start_state)
    heads_x = activated[:, :INNER].reshape(length, HEADS, HEADDIM)
    mixer_out = (local_y + carried_y + skip_gain[:, None] * heads_x).reshape(length, INNER)
    gated, gate_back = jax.vjp(gating, mixer_out, gate_z, gathered[4].astype(jnp.float32))
    gated_low = gated.astype(jnp.bfloat16)
    branch = jnp.dot(gated_low, gathered[5], preferred_element_type=jnp.float32)
    mixed = (tok_rows + branch).astype(jnp.bfloat16)
    again = (
        lax.all_gather(shards[0], ("dp", "seq"), axis=0, tiled=True),
        lax.all_gather(shards[1], ("dp", "seq"), axis=0, tiled=True),
        lax.all_gather(shards[2], ("dp", "seq"), axis=0, tiled=True),
        lax.all_gather(shards[3], ("dp", "seq"), axis=0, tiled=True),
        lax.all_gather(shards[4], ("dp", "seq"), axis=0, tiled=True),
        lax.all_gather(shards[5], ("dp", "seq"), axis=0, tiled=True),
    )
    grad_out = cotangent[0]
    grad_gated = contract_cols(grad_out, again[5])
    out_weight_grad = contract_rows(gated_low, grad_out)
    grad_mixer, grad_gate_z, norm_gain_grad = gate_back(grad_gated)
    grad_heads = grad_mixer.reshape(length, HEADS, HEADDIM)
    skip_grad = jnp.sum(grad_heads * heads_x, axis=(0, 2))
    acts_one, raw_one, shift_one, rate_one, start_grad = in_back(grad_heads)

    def backward_turn(index, carry_grad):
        return passed_along(start_grad + factor[:, None, None] * carry_grad, "seq", -1)

    end_grad = lax.fori_loop(0, lax.axis_size("seq") - 1, backward_turn, identity[1])
    factor_grad = jnp.sum(end_grad * start_state, axis=(1, 2))
    acts_two, raw_two, shift_two, rate_two = zero_back((grad_heads, factor_grad, end_grad))
    skip_part = (grad_heads * skip_gain[:, None]).reshape(length, INNER)
    grad_acts = (
        acts_one
        + acts_two
        + jnp.concatenate([skip_part, jnp.zeros((length, 2 * STATE), jnp.float32)], axis=1)
    )
    grad_ext, conv_weight_grad, conv_bias_grad = conv_back(grad_acts)
    back_rows = passed_along(shortened(grad_ext[:margin]), "seq", -1)
    grad_conv_in = grad_ext[margin:] + jnp.concatenate(
        [jnp.zeros((length - margin, XBC), jnp.float32), back_rows]
    )
    grad_projected = jnp.concatenate([grad_gate_z, grad_conv_in, raw_one + raw_two], axis=1).astype(
        jnp.bfloat16
    )
    in_weight_grad = contract_rows(normed_low, grad_projected)
    grad_normed = contract_cols(grad_projected, again[1])
    grad_tokens_norm, pre_gain_grad = pre_back(grad_normed)
    tokens_grad = grad_out.astype(jnp.float32) + grad_tokens_norm
    grad_parts = (
        pre_gain_grad,
        in_weight_grad,
        conv_weight_grad,
        conv_bias_grad,
        norm_gain_grad,
        out_weight_grad,
    )
    row_sums = (
        lax.psum_scatter(grad_parts[0], "dp", scatter_dimension=0, tiled=True),
        lax.psum_scatter(grad_parts[1], "dp", scatter_dimension=0, tiled=True),
        lax.psum_scatter(grad_parts[2], "dp", scatter_dimension=0, tiled=True),
        lax.psum_scatter(grad_parts[3], "dp", scatter_dimension=0, tiled=True),
        lax.psum_scatter(grad_parts[4], "dp", scatter_dimension=0, tiled=True),
        lax.psum_scatter(grad_parts[5], "dp", scatter_dimension=0, tiled=True),
    )
    sums = (
        lax.psum_scatter(row_sums[0], "seq", scatter_dimension=0, tiled=True),
        lax.psum_scatter(row_sums[1], "seq", scatter_dimension=0, tiled=True),
        lax.psum_scatter(row_sums[2], "seq", scatter_dimension=0, tiled=True),
        lax.psum_scatter(row_sums[3], "seq", scatter_dimension=0, tiled=True),
        lax.psum_scatter(row_sums[4], "seq", scatter_dimension=0, tiled=True),
        lax.psum_scatter(row_sums[5], "seq", scatter_dimension=0, tiled=True),
    )
    head_sums = lax.psum((shift_one + shift_two, rate_one + rate_two, skip_grad), ("dp", "seq"))
    return (
        mixed[None],
        tokens_grad[None],
        sums[0],
        sums[1],
        sums[2],
        sums[3],
        head_sums[0],
        head_sums[1],
        head_sums[2],
        sums[4],
        sums[5],
    )

AXES = ("dpo", "dpi", "so", "si")
MESH = pl.DeviceIdType.MESH
XCOLS = INNER // 4
ACT = XCOLS + 2 * STATE
CCOLS = ACT + 128
CHUNK = 128
HL = HEADS // 4
PAD = 16
MARGIN = CONVW - 1
f32, bf16 = jnp.float32, jnp.bfloat16
VMEM = pl.BlockSpec(memory_space=pltpu.VMEM)
HBM = pl.BlockSpec(memory_space=pl.ANY)


def guarded(when, action):
    if when is None:
        action()
    else:
        pl.when(when)(action)


class Wires:
    def __init__(self, send, recv, local):
        self.send, self.recv, self.local = send, recv, local
        self.used, self.kept, self.pending = 0, 0, []

    def slot(self):
        self.used += 1
        return self.used - 1

    def copy(self, src, dst, slot, device, landed=None):
        return pltpu.make_async_remote_copy(
            src_ref=src, dst_ref=dst, send_sem=self.send.at[slot],
            recv_sem=self.recv.at[slot if landed is None else landed],
            device_id=device, device_id_type=MESH,
        )

    def start(self, src, dst, slot, device, when=None, landed=None):
        copy = self.copy(src, dst, slot, device, landed)
        guarded(when, copy.start)
        self.pending.append((copy, when))
        return self.pending[-1]

    def sent(self, entry):
        self.pending = [kept for kept in self.pending if kept is not entry]
        guarded(entry[1], entry[0].wait_send)

    def arrived(self, landing, slot, device, when=None):
        guarded(when, self.copy(landing, landing, slot, device).wait_recv)

    def keep(self, src, dst, when=None):
        copy = pltpu.make_async_copy(src, dst, self.local.at[self.kept])
        self.kept += 1
        guarded(when, copy.start)
        return lambda: guarded(when, copy.wait)

    def finish(self):
        for copy, when in self.pending:
            guarded(when, copy.wait_send)
        self.pending = []


def place():
    return tuple(lax.axis_index(name) for name in AXES)


def member(here, rel):
    a, c, b, s = here
    return (a, c ^ (rel >> 1), b, s ^ (rel & 1))


def greet(here, size, extra):
    a, c, b, s = here
    n, nx = size["so"], size["dpo"]
    barrier = pltpu.get_barrier_semaphore()
    known = [member(here, rel) for rel in range(1, 4)]
    known += [(a, c, lax.rem(b + k, n), s) for k in range(1, n)]
    known += [(lax.rem(a + k, nx), c, b, s) for k in range(1, nx)]
    for device in known:
        pl.semaphore_signal(barrier, inc=1, device_id=device, device_id_type=MESH)
    met = len(known)
    for devices, when in extra:
        for device in devices:
            guarded(when, lambda device=device: pl.semaphore_signal(barrier, inc=1, device_id=device, device_id_type=MESH))
        met = met + len(devices) * when.astype(jnp.int32)
    return lambda: pl.semaphore_wait(barrier, met)


def mm(x, y, dims=((1,), (0,)), exact=None):
    if exact is not None:
        whole = (x, y)[exact].astype(f32)
        high = whole.astype(bf16)
        low = (whole - high.astype(f32)).astype(bf16)
        parts = [(high, y), (low, y)] if exact == 0 else [(x, high), (x, low)]
        return mm(*parts[0], dims) + mm(*parts[1], dims)
    return lax.dot_general(x.astype(bf16), y.astype(bf16), (dims, ((), ())), preferred_element_type=f32)


def fine(x, y, dims=((1,), (0,))):
    x, y = x.astype(f32), y.astype(f32)
    xh, yh = x.astype(bf16), y.astype(bf16)
    xl, yl = (x - xh.astype(f32)).astype(bf16), (y - yh.astype(f32)).astype(bf16)
    return mm(xh, yh, dims) + (mm(xl, yh, dims) + mm(xh, yl, dims))


def iota(shape, axis):
    return lax.broadcasted_iota(jnp.int32, shape, axis)


def spread_heads():
    return (iota((128, XCOLS), 0) == iota((128, XCOLS), 1) // HEADDIM).astype(f32).astype(bf16)


def gather_heads():
    return (iota((XCOLS, 128), 1) == iota((XCOLS, 128), 0) // HEADDIM).astype(f32).astype(bf16)


def class_heads(size, cc, ss):
    per = size["so"] // 2
    run = HEADS // (size["dpo"] * 4 * per)
    lane = iota((128, 128), 1)
    group, j = lane // run, lane % run
    head = (((group // per * 2 + cc) * per + group % per) * 2 + ss) * run + j
    return ((iota((128, 128), 0) == head) & (lane < HL)).astype(f32).astype(bf16)


def pick_heads(values, chosen, dims=((1,), (0,))):
    high = values.astype(bf16)
    rest = values - high.astype(f32)
    middle = rest.astype(bf16)
    low = rest - middle.astype(f32)
    return mm(high, chosen, dims) + mm(middle, chosen, dims) + mm(low, chosen, dims)


def loop(count, body, first=0):
    lax.fori_loop(first, count, lambda i, _: (body(i), 0)[1], 0)


def chunk_rows(r, i):
    per = r.span // CHUNK
    flat = pl.multiple_of(i * CHUNK, CHUNK)
    padded = pl.multiple_of((i // per) * (r.span + PAD) + PAD + (i % per) * CHUNK, PAD)
    return flat, padded


def chunk_decays(r, i):
    flat, padded = chunk_rows(r, i)
    rows = pl.ds(flat, CHUNK)
    ids = r.idc[pl.ds(padded, CHUNK), :]
    before = r.idc[pl.ds(pl.multiple_of(padded - 8, 8), 8), :][7:8]
    last = ids[CHUNK - 1 : CHUNK]
    return flat, padded, rows, ids, before, last


def phase_norm(r, i, block):
    rows = pl.ds(pl.multiple_of(i * block, 16), block)
    t = r.toks[rows, :].astype(f32)
    scale = lax.rsqrt(jnp.mean(t * t, axis=1, keepdims=True) + EPSILON)
    r.normed[rows, :] = (t * scale * r.gain1[0:1]).astype(bf16)


def taps(window, ids, k, rows):
    first = 8 - MARGIN + k
    same = ids[first : first + rows] == ids[8 : 8 + rows]
    return jnp.where(same, window[first : first + rows], 0.0)


def phase_in(r, q, w, first):
    rows = r.span + PAD
    w = w.reshape(w.shape[0] * w.shape[1], 256)
    r.pc[q * rows : (q + 1) * rows, pl.ds(first, 256)] = mm(r.normed[q * rows : (q + 1) * rows, :], w)
    ids = r.idc[q * rows + PAD - 8 : (q + 1) * rows, :]
    for half in range(2):
        tile = pl.ds(pl.multiple_of(first + half * 128, 128), 128)
        window = r.pc[q * rows + PAD - 8 : (q + 1) * rows, tile]
        kern = r.cv[:, tile]
        pre = kern[4:5] + window[8:] * kern[3:4]
        for k in range(MARGIN):
            pre = pre + taps(window, ids, k, r.span) * kern[k : k + 1]
        gate = jax.nn.sigmoid(pre)
        act = pre * gate
        r.act[q * r.span : (q + 1) * r.span, tile] = act
        r.sp[q * r.span : (q + 1) * r.span, tile] = gate + act * (1.0 - gate)


def phase_decay(r, i):
    flat, padded, rows, ids, before, last = chunk_decays(r, i)
    raw = r.dtr[pl.ds(padded, CHUNK), :] + r.hp[0:1]
    lane = iota((CHUNK, 128), 1) < HL
    dt = jnp.where(lane, jnp.maximum(raw, 0.0) + jnp.log1p(jnp.exp(-jnp.abs(raw))), 0.0)
    la = -jnp.exp(r.hp[1:2]) * dt
    tril = (iota((CHUNK, CHUNK), 0) >= iota((CHUNK, CHUNK), 1)).astype(f32)
    run = mm(tril, la, exact=1)
    end = run[CHUNK - 1 : CHUNK]
    weight = jnp.where(ids == last, jnp.exp(end - run), 0.0)
    passed = jnp.where(last == before, jnp.exp(end), 0.0)
    e = spread_heads()
    xdt = r.act[rows, 0:XCOLS] * mm(dt, e, exact=0)
    xw = xdt * mm(weight, e, exact=0)
    r.dtm[rows, :] = dt
    r.run[rows, :] = run
    r.xdt[rows, :] = xdt.astype(bf16)
    r.st[i] = fine(r.act[rows, XCOLS : XCOLS + STATE], xw, ((0,), (0,)))
    r.pex[i] = mm(jnp.broadcast_to(passed, (8, 128)), e, exact=0)


def phase_states(r):
    per = r.span // CHUNK
    for q in range(2):
        cur = jnp.zeros((STATE, XCOLS), f32)
        fac = jnp.ones((8, XCOLS), f32)
        for j in range(per):
            i = q * per + j
            fresh = r.st[i]
            r.st[i] = cur
            r.cum[i] = fac
            cur = r.pex[i][0:1] * cur + fresh
            fac = fac * r.pex[i]
        r.end[q] = cur
        r.fac[q] = fac


def chunk_matrix(r, i):
    flat, padded, rows, ids, before, last = chunk_decays(r, i)
    mask = (ids == ids.T) & (iota((CHUNK, CHUNK), 0) >= iota((CHUNK, CHUNK), 1))
    bm = r.bc[rows, 0:STATE].astype(bf16)
    cm = r.bc[rows, STATE:].astype(bf16)
    cb = mm(cm, bm, ((1,), (1,)))
    run = r.run[rows, :]
    return rows, mask, bm, cm, cb, run, run.T


def phase_inside(r, i):
    rows, mask, bm, cm, cb, run, runt = chunk_matrix(r, i)
    for hp in range(HL // 2):
        tile = pl.ds(hp * 128, 128)
        xdt = r.xdt[rows, tile]
        outs = []
        for k in range(2):
            h = 2 * hp + k
            decay = jnp.exp(jnp.where(mask, run[:, h : h + 1] - runt[h : h + 1, :], -1e30))
            outs.append(mm(decay * cb, xdt[:, k * HEADDIM : (k + 1) * HEADDIM]))
        r.y[rows, tile] = jnp.concatenate(outs, axis=1)


def phase_carried(r, i):
    flat, padded, rows, ids, before, last = chunk_decays(r, i)
    enter = mm(jnp.where(ids == before, jnp.exp(r.run[rows, :]), 0.0), spread_heads(), exact=0)
    start = r.st[i] + r.cum[i][0:1] * r.sin[i // (r.span // CHUNK)]
    r.st[i] = start
    carried = fine(r.act[rows, XCOLS + STATE : ACT], start) * enter
    r.y[rows, :] += carried + r.hx[0:1] * r.act[rows, 0:XCOLS]


def column_pair(first, second):
    lanes = iota((first.shape[0], 128), 1)
    return jnp.where(lanes == 0, first, jnp.where(lanes == 1, second, 0.0)).T[0:8]


def phase_sums(r, i):
    rows = pl.ds(pl.multiple_of(i * CHUNK, CHUNK), CHUNK)
    z = r.z[rows, :]
    v = r.y[rows, :] * (z * jax.nn.sigmoid(z))
    u = r.gg[rows, :] * r.ng[0:1]
    r.sums[0, i] = column_pair(jnp.sum(v * v, axis=1, keepdims=True), jnp.sum(u * v, axis=1, keepdims=True))


def phase_gate(r, i):
    rows = pl.ds(pl.multiple_of(i * CHUNK, CHUNK), CHUNK)
    total = (r.sums[0, i] + r.sums[1, i]) + (r.sums[2, i] + r.sums[3, i])
    cols = jnp.concatenate([total, jnp.zeros((CHUNK - 8, 128), f32)], axis=0).T
    scale = lax.rsqrt(cols[:, 0:1] / INNER + EPSILON)
    tilt = scale * scale * scale * (cols[:, 1:2] / INNER)
    z, y, gg = r.z[rows, :], r.y[rows, :], r.gg[rows, :]
    gate = jax.nn.sigmoid(z)
    silu = z * gate
    v = y * silu
    vr = v * scale
    gv = gg * r.ng[0:1] * scale - v * tilt
    r.gated[rows, :] = (vr * r.ng[0:1]).astype(bf16)
    r.gpg[rows, :] = (gv * y * (gate + silu * (1.0 - gate))).astype(bf16)
    r.gg[rows, :] = gv * silu
    r.nggrad[0:1] += jnp.sum(gg * vr, axis=0, keepdims=True)


def phase_back_states(r, i, x):
    flat, padded, rows, ids, before, last = chunk_decays(r, i)
    enter = mm(jnp.where(ids == before, jnp.exp(r.run[rows, :]), 0.0), spread_heads(), exact=0)
    dy = r.gg[rows, :]
    own = r.y[rows, :] - r.hx[0:1] * x
    low = dy.astype(bf16).astype(f32)
    r.drun[rows, :] = mm(low * own, gather_heads(), exact=0)
    r.y[rows, :] = fine(r.bc[rows, STATE:], dy * enter, ((0,), (0,)))
    r.tally[2:3] += jnp.sum(mm(dy * x, gather_heads(), exact=0), axis=0, keepdims=True)


def phase_back_chain(r):
    per = r.span // CHUNK
    for q in range(2):
        cur = jnp.zeros((STATE, XCOLS), f32)
        fac = jnp.ones((8, XCOLS), f32)
        for j in reversed(range(per)):
            i = q * per + j
            rows = slice(i * CHUNK, (i + 1) * CHUNK)
            fresh = r.y[rows, :]
            r.y[rows, :] = cur
            r.cum[i] = fac
            cur = r.pex[i][0:1] * cur + fresh
            fac = fac * r.pex[i]
        r.end[q] = cur


def phase_back_inside(r, i):
    rows, mask, bm, cm, cb, run, runt = chunk_matrix(r, i)
    dcb = jnp.zeros((CHUNK, CHUNK), f32)
    for hp in range(HL // 2):
        tile = pl.ds(hp * 128, 128)
        xdt, dy = r.xdt[rows, tile], r.gg[rows, tile].astype(bf16)
        outs = []
        for k in range(2):
            h = 2 * hp + k
            part = slice(k * HEADDIM, (k + 1) * HEADDIM)
            decay = jnp.exp(jnp.where(mask, run[:, h : h + 1] - runt[h : h + 1, :], -1e30))
            dcb = dcb + mm(dy[:, part], xdt[:, part], ((1,), (1,))) * decay
            outs.append(mm(decay * cb, dy[:, part], ((0,), (0,))))
        r.gx[rows, tile] = jnp.concatenate(outs, axis=1)
    r.gbc[rows, 0:STATE] = mm(dcb, cm, ((0,), (0,)))
    r.gbc[rows, STATE : 2 * STATE] = mm(dcb, bm)


def phase_back_close(r, i, start, x):
    flat, padded, rows, ids, before, last = chunk_decays(r, i)
    q = i // (r.span // CHUNK)
    e, g = spread_heads(), gather_heads()
    run, dt = r.run[rows, :], r.dtm[rows, :]
    end = run[CHUNK - 1 : CHUNK]
    enter = jnp.where(ids == before, jnp.exp(run), 0.0)
    weight = jnp.where(ids == last, jnp.exp(end - run), 0.0)
    entx, wx, dtx = mm(enter, e, exact=0), mm(weight, e, exact=0), mm(dt, e, exact=0)
    bm = r.bc[rows, 0:STATE]
    dy = r.gg[rows, :]
    dend = r.y[rows, :] + r.cum[i][0:1] * r.sin[q]
    xw = x * dtx * wx
    dxw = fine(bm, dend)
    inside = r.gx[rows, :]
    via_w = dxw * xw
    through = jnp.sum(dend * start, axis=0, keepdims=True) * r.pex[i][0:1]
    through = jnp.sum(via_w, axis=0, keepdims=True) + through
    at_end = mm(jnp.broadcast_to(through, (8, XCOLS)), g, exact=0)[0:1]
    drun = r.drun[rows, :] - mm(r.xdt[rows, :].astype(f32) * inside + via_w, g, exact=0)
    drun = drun + jnp.where(iota((CHUNK, 128), 0) == CHUNK - 1, at_end, 0.0)
    triu = (iota((CHUNK, CHUNK), 0) <= iota((CHUNK, CHUNK), 1)).astype(f32)
    dla = mm(triu, drun, exact=1)
    dxdt = inside + dxw * wx
    neg = -jnp.exp(r.hp[1:2])
    ddt = dla * neg + mm(dxdt * x, g, exact=0)
    raw = r.dtr[pl.ds(padded, CHUNK), :] + r.hp[0:1]
    draw = jnp.where(iota((CHUNK, 128), 1) < HL, ddt * jax.nn.sigmoid(raw), 0.0)
    r.gx[rows, :] = dxdt * dtx + r.hx[0:1] * dy
    r.gbc[rows, 0:STATE] += fine(xw, dend, ((1,), (1,)))
    r.gbc[rows, STATE : 2 * STATE] += fine(dy * entx, start, ((1,), (1,)))
    r.gpc[pl.ds(padded, CHUNK), ACT:CCOLS] = mm(draw, r.chosen[...], ((1,), (1,))).astype(bf16)
    r.tally[0:1] += jnp.sum(draw, axis=0, keepdims=True)
    r.tally[1:2] += jnp.sum(dla * (neg * dt), axis=0, keepdims=True)


def phase_back_conv(r, q, lt, grad, window, slope):
    rows = r.span + PAD
    tile = pl.ds(pl.multiple_of(lt * 128, 128), 128)
    kern = r.cv[:, tile]
    ids = r.idc[q * rows + PAD - 8 : (q + 1) * rows, :]
    gpre = grad * slope
    sums = []
    out = jnp.zeros((rows, 128), f32)
    for k in range(CONVW):
        first = 8 - MARGIN + k
        part = gpre
        if k < MARGIN:
            part = jnp.where(ids[first : first + r.span] == ids[8:], gpre, 0.0)
        sums.append(jnp.sum(part * window[first : first + r.span], axis=0, keepdims=True))
        ahead = PAD - MARGIN + k
        pieces = [jnp.zeros((ahead, 128), f32), part * kern[k : k + 1]]
        if rows - ahead - r.span:
            pieces.append(jnp.zeros((rows - ahead - r.span, 128), f32))
        out = out + jnp.concatenate(pieces, axis=0)
    sums.append(jnp.sum(gpre, axis=0, keepdims=True))
    sums.append(jnp.zeros((3, 128), f32))
    r.cvgrad[:, tile] += jnp.concatenate(sums, axis=0)
    r.gpc[q * rows : (q + 1) * rows, tile] = out.astype(bf16)


def unit_of(w, rows, aa, bb):
    return w.at[pl.ds(2 * aa, 2), pl.ds(pl.multiple_of(2 * rows * bb, 16), 2 * rows)]


def shard_of(w, rows, aa, cc, bb, ss):
    return w.at[2 * aa + cc, pl.ds(pl.multiple_of(2 * rows * bb + rows * ss, 16), rows)]


def spread(wires, here, size, get, turned=None):
    a, c, b, s = here
    n, nx = size["so"], size["dpo"]
    crossing, turns = [], []
    mine = lambda bb: lax.rem(bb, 2) == s
    both = lambda when, cond: cond if when is None else when & cond

    def cross(where, bb, when):
        slots = {k: wires.slot() for k in range(1, nx)}
        for k in range(1, nx):
            wires.start(where(a, bb), where(a, bb), slots[k], (lax.rem(a + k, nx), c, b, s), when)
        crossing.append((where, bb, when, slots))

    def pass_on(bb, when):
        if turned is None:
            cross(get, bb, when)
            return
        slot = wires.slot()
        wires.start(get(a, bb), turned(a, bb, s), slot, member(here, 1), both(when, jnp.logical_not(mine(bb))))
        turns.append((bb, both(when, mine(bb)), slot))
        cross(get, bb, both(when, mine(bb)))

    def turn_back(items):
        for bb, when, slot in items:
            wires.arrived(turned(a, bb, 1 - s), slot, member(here, 1), when)
            cross(lambda aa, other: turned(aa, other, 1 - s), bb, when)

    up = {j: wires.slot() for j in range(1, n)}
    down = {j: wires.slot() for j in range(1, n)}
    above, below = (a, c, jnp.minimum(b + 1, n - 1), s), (a, c, jnp.maximum(b - 1, 0), s)
    wires.start(get(a, b), get(a, b), up[1], above, b + 1 < n)
    wires.start(get(a, b), get(a, b), down[1], below, b > 0)
    pass_on(b, None)
    yield
    for j in range(1, n):
        sides = (
            (up, jnp.maximum(b - j, 0), b - j >= 0, below, above, b + 1 < n),
            (down, jnp.minimum(b + j, n - 1), b + j < n, above, below, b > 0),
        )
        for slots, origin, there, source, target, onward in sides:
            wires.arrived(get(a, origin), slots[j], source, there)
            if j + 1 < n:
                wires.start(get(a, origin), get(a, origin), slots[j + 1], target, there & onward)
            pass_on(origin, there)
        early, late = turns[: len(turns) - 2], turns[len(turns) - 2 :]
        turn_back(early)
        turns[:] = late
        yield
    turn_back(turns)
    if turned is not None:
        yield
    for where, bb, when, slots in crossing:
        for k in range(1, nx):
            aa = lax.rem(a + nx - k, nx)
            wires.arrived(where(aa, bb), slots[k], (aa, c, b, s), when)
    yield


def collect(wires, here, size, get, x, z, close):
    a, c, b, s = here
    n, nx = size["so"], size["dpo"]
    order = [k for k in range(1, n)] + [0]
    flown, hops = {}, {}
    for k in order:
        bb = lax.rem(b + k, n)
        for h in range(1, nx):
            flown[k, h] = wires.slot()
            wires.start(get(lax.rem(a + h, nx), bb), x.at[h - 1, k], flown[k, h], (lax.rem(a + h, nx), c, b, s))
    yield
    for k in order:
        bb = lax.rem(b + k, n)
        total = get(a, bb)[...].astype(f32)
        for h in range(1, nx):
            wires.arrived(x.at[h - 1, k], flown[k, h], (lax.rem(a + nx - h, nx), c, b, s))
            total = total + x[h - 1, k].astype(f32)
        x[0, k] = total.astype(bf16)
        if k > 0:
            hops[k] = wires.slot()
            wires.start(x.at[0, k], z.at[k - 1], hops[k], (a, c, bb, s))
        yield
    for k in range(1, n):
        wires.arrived(z.at[k - 1], hops[k], (a, c, lax.rem(b + n - k, n), s))
    total = x[0, 0].astype(f32)
    for k in range(1, n):
        total = total + z[k - 1].astype(f32)
    close(total)
    yield


def collect_out(wires, here, size, get, x, y, z, out, sends):
    a, c, b, s = here
    n, nx = size["so"], size["dpo"]
    half = y.shape[2]
    order = [k for k in range(1, n)] + [0]
    flown, turned, hops = {}, {}, {}
    part = lambda bb, ss: x.at[0, bb // 2, :, pl.ds(pl.multiple_of(half * ss, 16), half)]
    for k in order:
        bb = lax.rem(b + k, n)
        for h in range(1, nx):
            flown[k, h] = wires.slot()
            to = (lax.rem(a + h, nx), c, b, s)
            sends.append(wires.start(get(lax.rem(a + h, nx), bb), x.at[h - 1, bb // 2], flown[k, h], to, lax.rem(bb, 2) == s))
    yield
    for k in order:
        bb = lax.rem(b + k, n)
        has = lax.rem(bb, 2) == s
        for h in range(1, nx):
            wires.arrived(x.at[h - 1, bb // 2], flown[k, h], (lax.rem(a + nx - h, nx), c, b, s), has)

        @pl.when(has)
        def _():
            total = get(a, bb)[...].astype(f32)
            for h in range(1, nx):
                total = total + x[h - 1, bb // 2].astype(f32)
            x[0, bb // 2] = total.astype(bf16)

        turned[k], hops[k] = wires.slot(), wires.slot()
        wires.start(part(bb, 1 - s), y.at[bb // 2], turned[k], member(here, 1), has)
        if k > 0:
            wires.start(part(bb, s), z.at[k - 1], hops[k], (a, c, bb, s), has)
        yield
    for k in order:
        bb = lax.rem(b + k, n)
        turns = lax.rem(bb, 2) != s
        wires.arrived(y.at[bb // 2], turned[k], member(here, 1), turns)
        if k > 0:
            wires.start(y.at[bb // 2], z.at[k - 1], hops[k], (a, c, bb, s), turns)
    yield
    for k in range(1, n):
        wires.arrived(z.at[k - 1], hops[k], (a, c, lax.rem(b + n - k, n), s))

    def close(own):
        for h in range(2):
            total = own[h].astype(f32)
            for k in range(1, n):
                total = total + z[k - 1, h].astype(f32)
            out[:, h * XCOLS : (h + 1) * XCOLS] = total

    pl.when(lax.rem(b, 2) == s)(lambda: close(part(b, s)[...]))
    pl.when(lax.rem(b, 2) != s)(lambda: close(y[b // 2]))
    yield


def collect_shared(wires, here, size, g, s1, s2, s3, s4, out):
    a, c, b, s = here
    n, nx = size["so"], size["dpo"]
    slots = [wires.slot() for _ in range(2 + nx + n)]
    wires.start(g.at[pl.ds(2 * (1 - c), 2)], s1, slots[0], member(here, 2))
    yield
    wires.arrived(s1, slots[0], member(here, 2))
    for k in range(2):
        s1[k] = (s1[k].astype(f32) + g[2 * c + k].astype(f32)).astype(bf16)
    wires.start(s1.at[1 - s], s2, slots[1], member(here, 1))
    yield
    wires.arrived(s2, slots[1], member(here, 1))
    for k in range(nx):
        s2[k] = (s2[k].astype(f32) + s1[s, k].astype(f32)).astype(bf16)
    for h in range(1, nx):
        to = lax.rem(a + h, nx)
        wires.start(s2.at[to], s3.at[h - 1], slots[1 + h], (to, c, b, s))
    yield
    total = s2[a].astype(f32)
    for h in range(1, nx):
        wires.arrived(s3.at[h - 1], slots[1 + h], (lax.rem(a + nx - h, nx), c, b, s))
        total = total + s3[h - 1].astype(f32)
    s3[0] = total.astype(bf16)
    for k in range(1, n):
        bb = lax.rem(b + k, n)
        wires.start(s3.at[0, bb], s4.at[k - 1], slots[1 + nx + k], (a, c, bb, s))
    yield
    total = s3[0, b].astype(f32)
    for k in range(1, n):
        wires.arrived(s4.at[k - 1], slots[1 + nx + k], (a, c, lax.rem(b + n - k, n), s))
        total = total + s4[k - 1].astype(f32)
    out[...] = total
    yield


def finish_units(wires, here, rows, z, out):
    a, c, b, s = here
    mine = 2 * c + s
    back = {}

    def close(total):
        z[0] = total.astype(bf16)
        out[mine] = z[0, c, pl.ds(pl.multiple_of(rows * s, 16), rows)]
        for rel in range(1, 4):
            _, cc, _, ss = member(here, rel)
            back[rel] = wires.slot()
            part = z.at[0, cc, pl.ds(pl.multiple_of(rows * ss, 16), rows)]
            wires.start(part, out.at[mine], back[rel], member(here, rel))

    def wait():
        for rel in range(1, 4):
            _, cc, _, ss = member(here, rel)
            wires.arrived(out.at[2 * cc + ss], back[rel], member(here, rel))

    return close, wait


def sum_all(wires, here, size, mine, z, x):
    a, c, b, s = here
    n, nx = size["so"], size["dpo"]
    slots = [wires.slot() for _ in range(n + nx)]
    z[b] = mine[...]
    for k in range(1, n):
        wires.start(mine, z.at[b], slots[k], (a, c, lax.rem(b + k, n), s))
    yield
    for k in range(1, n):
        origin = lax.rem(b + n - k, n)
        wires.arrived(z.at[origin], slots[k], (a, c, origin, s))
    total = z[0]
    for k in range(1, n):
        total = total + z[k]
    x[a] = total
    for h in range(1, nx):
        wires.start(x.at[a], x.at[a], slots[n + h], (lax.rem(a + h, nx), c, b, s))
    yield
    for h in range(1, nx):
        origin = lax.rem(a + nx - h, nx)
        wires.arrived(x.at[origin], slots[n + h], (origin, c, b, s))
    total = x[0]
    for h in range(1, nx):
        total = total + x[h]
    yield total


def run_places(size):
    per = size["so"] // 2
    width = INNER // (size["dpo"] * 4 * per)
    return [
        (2 * cc + ss, (aa * per + bb) * width)
        for aa in range(size["dpo"]) for cc in range(2) for bb in range(per) for ss in range(2)
    ], width


def class_runs(values, size, m):
    places, width = run_places(size)
    return jnp.concatenate([values[:, k * width : (k + 1) * width] for k, (cls, _) in enumerate(places) if cls == m], axis=1)


def joined_runs(of_class, size, first, count):
    places, width = run_places(size)
    return jnp.concatenate([of_class[m][:, at : at + width] for m, at in places[first // width : (first + count) // width]], axis=1)


def device_index(size, here):
    a, c, b, s = here
    return (2 * a + c) * (2 * size["so"]) + 2 * b + s


def widened(values, rows, columns):
    if columns > values.shape[1]:
        values = jnp.concatenate([values, jnp.zeros((values.shape[0], columns - values.shape[1]), f32)], axis=1)
    if rows > values.shape[0]:
        values = jnp.concatenate([values, jnp.zeros((rows - values.shape[0], columns), f32)], axis=0)
    return values


def place_smalls(size, here, r):
    count = size["dpo"] * 4 * size["so"]
    index = device_index(size, here)
    depth = r.normed.shape[1]
    sub = iota((8, 128), 0)

    def placed(tile, total):
        return pltpu.roll(widened(tile, 8, total), index * (total // count), 1)

    taps = widened(r.conv_w[...].astype(f32), 128, 128).T[0:8]
    tile = taps + jnp.where(sub == 4, widened(r.conv_b[...].astype(f32), 1, 128), 0.0)
    conv = placed(tile, XBC)
    norm = placed(widened(r.norm_in[...].astype(f32), 8, 128), INNER)
    pre = placed(widened(r.pre_in[...].astype(f32), 8, 128), depth)
    sub = iota((8, ACT), 0)
    low = widened(pre[0:1, ACT:], 1, ACT)
    common = jnp.where(sub == 6, pre[0:1, :ACT], jnp.where(sub == 7, low, 0.0))
    for m in range(4):
        own = jnp.concatenate([class_runs(conv[:, :INNER], size, m), conv[:, INNER:]], axis=1)
        gain = widened(class_runs(norm, size, m)[0:1], 1, ACT)
        r.cvs[m] = own + jnp.where(sub == 5, gain, common)


def final_smalls(size, here, r):
    count = size["dpo"] * 4 * size["so"]
    index = device_index(size, here)
    depth = 2 * XCOLS
    tiles = [r.os[m] for m in range(4)]

    def taken(values, total):
        return pltpu.roll(values, total - index * (total // count), 1)[:, 0:128]

    inner = joined_runs([t[:, :XCOLS] for t in tiles], size, 0, INNER)
    rest = (tiles[0][:, XCOLS:] + tiles[1][:, XCOLS:]) + (tiles[2][:, XCOLS:] + tiles[3][:, XCOLS:])
    conv = taken(jnp.concatenate([inner, rest], axis=1), XBC)
    r.smo[0] = conv
    r.smo[1] = taken(inner, INNER)
    r.cwo[...] = widened(conv, 128, 128).T[0 : r.cwo.shape[0], 0:CONVW]
    pre = [jnp.concatenate([t[6:7], t[7:8, : depth - ACT]], axis=1) for t in tiles]
    r.smo[2] = taken(widened((pre[0] + pre[1]) + (pre[2] + pre[3]), 8, depth), depth)
    heads = jnp.zeros((8, 128), f32)
    for m, t in enumerate(tiles):
        three = jnp.concatenate([t[5:6, XCOLS : XCOLS + 128], t[5:6, XCOLS + 128 :], t[7:8, depth - ACT : depth - ACT + 128]], axis=0)
        heads = heads + pick_heads(widened(three, 8, 128), class_heads(size, m // 2, m % 2), ((1,), (1,)))
    r.smo[3] = heads


def chain(wires, here, size, r, step):
    a, c, b, s = here
    n = size["so"]
    half = XCOLS // 2
    to = (a, c, jnp.clip(b + step, 0, n - 1), s)
    origin = (a, c, jnp.clip(b - step, 0, n - 1), s)
    place_in = b if step > 0 else n - 1 - b
    copies = []
    for m in range(4):
        slot = wires.slot()
        copies.append((wires.copy(r.cout.at[m], r.cin.at[m], slot, to), slot))
        wires.pending.append((copies[m][0], place_in + 1 < n))

    def hop(h):
        def act():
            for m in range(4):
                q, cols = m // 2, slice((m % 2) * half, (m % 2 + 1) * half)
                if h == 0:
                    value = r.end[q, :, cols]
                    r.sin[q, :, cols] = jnp.zeros((STATE, half), f32)
                else:
                    wires.arrived(r.cin.at[m], copies[m][1], origin)
                    value = r.cin[m].astype(f32)
                    r.sin[q, :, cols] = value
                    value = r.fac[q, 0:1, cols] * value + r.end[q, :, cols]
                if h + 1 < n:
                    r.cout[m] = value.astype(bf16)
                    copies[m][0].start()
        pl.when(place_in == h)(act)

    return hop


def named(names, refs):
    return types.SimpleNamespace(**dict(zip(names, refs)))


def forward_kernel(size, names, *refs):
    r = named(names, refs)
    here = place()
    a, c, b, s = here
    n, nx = size["so"], size["dpo"]
    mine = 2 * c + s
    own = r.tok.shape[0]
    r.span = span = 2 * own
    rows = r.w_in.shape[0]
    halves = r.wo_in.shape[0]
    depth = r.toks.shape[1]
    r.bc = r.act.at[:, XCOLS:ACT]
    wires = Wires(r.send, r.recv, r.local)
    follows = (s == 1) & (b + 1 < n)
    next_group = [(a, cc, jnp.minimum(b + 1, n - 1), ss) for cc in range(2) for ss in range(2)]
    prior = [(a, cc, jnp.maximum(b - 1, 0), 1) for cc in range(2)]
    met = greet(here, size, [(next_group, follows), (prior, b > 0)])

    wires.keep(r.w_in, r.wraw)()
    inner = r.wraw[:, INNER : 2 * INNER].astype(f32)
    for m in range(4):
        r.wxs[m] = class_runs(inner, size, m).astype(bf16)
    shared = widened(r.wraw[:, 2 * INNER :].astype(f32), rows, CCOLS - XCOLS)
    r.wsr[mine, a, b] = shared.astype(bf16)
    place_smalls(size, here, r)
    met()

    first = {}

    def begin(name, src, dst):
        waits = [wires.keep(src.at[mine], shard_of(dst, rows, a, c, b, s))]
        for rel in range(1, 4):
            _, cc, _, ss = member(here, rel)
            first[name, rel] = wires.slot()
            wires.start(src.at[2 * cc + ss], shard_of(dst, rows, a, c, b, s), first[name, rel], member(here, rel))
        return waits[0]

    def began(name, dst, wait):
        for rel in range(1, 4):
            _, cc, _, ss = member(here, rel)
            wires.arrived(shard_of(dst, rows, a, cc, b, ss), first[name, rel], member(here, rel))
        wait()

    wait_x = begin("x", r.wxs, r.wcx)
    spread_s = spread(wires, here, size, lambda aa, bb: r.wsr.at[mine, aa, bb])
    next(spread_s)
    for rel in range(1, 4):
        _, cc, _, ss = member(here, rel)
        first["s", rel] = wires.slot()
        wires.start(r.cvs.at[2 * cc + ss], r.cvy.at[rel - 1], first["s", rel], member(here, rel))
    gate = r.wraw[:, 0:INNER].astype(f32)
    for m in range(4):
        r.wgs[m] = class_runs(gate, size, m).astype(bf16)

    own_rows = lambda cc, ss: pl.ds(pl.multiple_of(cc * (span + PAD) + PAD + own * ss, 16), own)
    cot_rows = lambda cc, ss: pl.ds(pl.multiple_of(cc * span + own * ss, 16), own)
    pairs = {"t": (r.tok, r.toks, own_rows), "k": (r.cot, r.cots, cot_rows)}

    def begin_rows(key):
        src, dst, at = pairs[key]
        wait = wires.keep(src, dst.at[at(c, s)])
        for rel in (1, 2):
            first[key, rel] = wires.slot()
            wires.start(src, dst.at[at(c, s)], first[key, rel], member(here, rel))
        first[key, 3] = wires.slot()
        return wait

    def pass_rows(key):
        src, dst, at = pairs[key]
        wires.arrived(dst.at[at(c, 1 - s)], first[key, 1], member(here, 1))
        wires.start(dst.at[at(c, 1 - s)], dst.at[at(c, 1 - s)], first[key, 3], member(here, 2))

    def end_rows(key, wait):
        src, dst, at = pairs[key]
        for rel, ss in ((2, s), (3, 1 - s)):
            wires.arrived(dst.at[at(1 - c, ss)], first[key, rel], member(here, 2))
        wait()

    shares = []

    def share(aa):
        slots = {rel: wires.slot() for rel in range(1, 4)}
        shares.append((aa, slots))
        for rel in (1, 2):
            wires.start(r.wsr.at[mine, aa], r.wsr.at[mine, aa], slots[rel], member(here, rel))

    def share_on(aa, slots):
        theirs = 2 * c + 1 - s
        wires.arrived(r.wsr.at[theirs, aa], slots[1], member(here, 1))
        wires.start(r.wsr.at[theirs, aa], r.wsr.at[theirs, aa], slots[3], member(here, 2))

    wait_t = begin_rows("t")
    began("x", r.wcx, wait_x)
    spread_x = spread(wires, here, size, lambda aa, bb: unit_of(r.wcx, rows, aa, bb))
    next(spread_x)
    sub = iota((8, 128), 0)
    places = r.idin[...].astype(f32)
    tile = jnp.zeros((8, 128), f32)
    for j in range(own // 128):
        tile = jnp.where(sub == j, places[:, j * 128 : (j + 1) * 128], tile)
    r.ids[mine] = tile
    for rel in range(1, 4):
        first["i", rel] = wires.slot()
        wires.start(r.ids.at[mine], r.ids.at[mine], first["i", rel], member(here, rel))
    halo_rows = lambda cc: pl.ds(pl.multiple_of(cc * (span + PAD), 16), PAD)
    tail = r.tok.at[own - PAD : own]
    halo_slots, hid_slots = [wires.slot() for _ in range(4)], [wires.slot() for _ in range(4)]
    for k, device in enumerate(next_group):
        wires.start(tail, r.toks.at[halo_rows(c)], halo_slots[k], device, follows, halo_slots[0] + c)
        wires.start(r.ids.at[mine], r.hid.at[c], hid_slots[k], device, follows, hid_slots[0] + c)
    wait_g = begin("g", r.wgs, r.wg)

    @pl.when(b == 0)
    def _():
        for q in range(2):
            r.toks[q * (span + PAD) : q * (span + PAD) + PAD, :] = jnp.zeros((PAD, depth), bf16)
        r.hid[...] = jnp.zeros(r.hid.shape, f32)

    r.chosen[...] = class_heads(size, c, s)
    raw = jnp.where(sub == 0, widened(r.dtb_in[...], 1, 128), jnp.where(sub == 1, widened(r.alog_in[...], 1, 128), jnp.where(sub == 2, widened(r.skip_in[...], 1, 128), 0.0)))
    r.hp[...] = pick_heads(raw, r.chosen[...])
    r.hx[...] = pick_heads(jnp.broadcast_to(r.hp[2:3], (8, 128)), spread_heads())

    for rel in range(1, 4):
        wires.arrived(r.cvy.at[rel - 1], first["s", rel], member(here, rel))
    r.cvm[...] = (r.cvs[mine] + r.cvy[0]) + (r.cvy[1] + r.cvy[2])
    smalls = sum_all(wires, here, size, r.cvm, r.cvz, r.cvx)
    next(smalls)
    next(spread_s)
    next(spread_x)
    next(smalls)
    for _ in range(n - 2):
        next(spread_s)
        next(spread_x)
    share(a)
    began("g", r.wg, wait_g)
    spread_g = spread(wires, here, size, lambda aa, bb: unit_of(r.wg, rows, aa, bb))
    next(spread_g)
    pass_rows("t")
    end_rows("t", wait_t)
    share_on(*shares[0])
    for rel in range(1, 4):
        _, cc, _, ss = member(here, rel)
        wires.arrived(r.ids.at[2 * cc + ss], first["i", rel], member(here, rel))
    for sc in range(2):
        wires.arrived(r.toks.at[halo_rows(sc)], halo_slots[0] + sc, prior[sc], b > 0)
        wires.arrived(r.hid.at[sc], hid_slots[0] + sc, prior[sc], b > 0)
    per = own // CHUNK
    for q in range(2):
        top = jnp.broadcast_to(r.hid[q, per - 1 : per], (CHUNK, 128)).T[CHUNK - PAD :]
        r.idc[q * (span + PAD) : q * (span + PAD) + PAD, :] = jnp.where(b > 0, top, -1.0)
        for ss in range(2):
            for j in range(per):
                at = q * (span + PAD) + PAD + ss * own + j * CHUNK
                r.idc[at : at + CHUNK, :] = jnp.broadcast_to(r.ids[2 * q + ss, j : j + 1], (CHUNK, 128)).T
    small = next(smalls)
    r.cv[...] = small
    r.ng[...] = jnp.broadcast_to(small[5:6, :XCOLS], (8, XCOLS))
    r.gain1[...] = jnp.broadcast_to(
        jnp.concatenate([small[6:7], small[7:8, : depth - ACT]], axis=1), (8, depth)
    )
    block = (span + PAD) // 3
    loop(6, lambda i: phase_norm(r, i, block))
    next(spread_s)
    for h in range(1, nx):
        share(lax.rem(a + h, nx))
    next(spread_x)
    get_o = lambda aa, bb: r.wo.at[lax.rem(bb + s, 2), aa, bb // 2, s]
    wires.keep(r.wo_in, get_o(a, b))()
    spread_o = spread(wires, here, size, get_o, lambda aa, bb, ss: r.wo.at[0, aa, bb // 2, ss])
    next(spread_o)
    for aa, slots in shares[1:]:
        share_on(aa, slots)
    for aa, slots in shares:
        wires.arrived(r.wsr.at[2 * (1 - c) + s, aa], slots[2], member(here, 2))
        wires.arrived(r.wsr.at[2 * (1 - c) + 1 - s, aa], slots[3], member(here, 2))
    wait_k = begin_rows("k")
    for m in range(4):
        for aa in range(nx):
            for bb in range(n):
                at = (2 * bb + m % 2) * rows
                r.wcs[2 * aa + m // 2, at : at + rows, :] = r.wsr[m, aa, bb]
    w = r.wcs[:, :, 2 * STATE :]
    r.dtr[...] = pick_heads(mm(r.normed[...], w.reshape(w.shape[0] * w.shape[1], 128)), r.chosen[...])
    steps = list(range(1, n))
    for q in range(2):
        def columns(ct, q=q):
            at = pl.multiple_of(ct * 256, 256)
            phase_in(r, q, r.wcx[:, :, pl.ds(at, 256)], at)

        loop(XCOLS // 256, columns)
        phase_in(r, q, r.wcs[:, :, 0 : 2 * STATE], XCOLS)
        if steps:
            next(spread_g)
            steps.pop()
    chunks = 2 * span // CHUNK
    loop(chunks, lambda i: phase_decay(r, i))
    phase_states(r)
    hop = chain(wires, here, size, r, 1)
    hop(0)
    while steps:
        next(spread_g)
        steps.pop()
    next(spread_o)
    flushes = [wires.keep(src, dst) for src, dst in ((r.normed, r.normed_o), (r.pc, r.pc_o), (r.sp, r.sp_o), (r.act, r.act_o), (r.xdt, r.xdt_o), (r.wcx, r.wcx_o), (r.wcs, r.wcs_o), (r.dtm, r.dtm_o), (r.run, r.run_o), (r.dtr, r.dtr_o), (r.idc, r.idc_o))]

    def inner_z(q, ct):
        wide = pl.ds(pl.multiple_of(ct * 256, 256), 256)
        w = r.wg[:, :, wide]
        lines = r.normed[q * (span + PAD) + PAD : (q + 1) * (span + PAD), :]
        r.z[q * span : (q + 1) * span, wide] = mm(lines, w.reshape(w.shape[0] * w.shape[1], 256))

    def fill_a():
        loop(chunks // 2, lambda i: phase_inside(r, i))

    def fill_b():
        next(spread_g)
        for q in range(2):
            loop(XCOLS // 256, lambda ct, q=q: inner_z(q, ct))

    def fill_c():
        loop(chunks, lambda i: phase_inside(r, i), chunks // 2)

    fillers = [fill_a, fill_b, fill_c]
    for h in range(1, n):
        if fillers:
            fillers.pop(0)()
        if h == n - 1:
            pass_rows("k")
        hop(h)
        next(spread_o)
    for fill in fillers:
        fill()
    end_rows("k", wait_k)
    flushes += [wires.keep(src, dst) for src, dst in ((r.wg, r.wg_o), (r.z, r.z_o), (r.cots, r.cots_o))]
    next(spread_o)
    flushes.append(wires.keep(r.wo.at[0], r.wo_o))
    per_x = XCOLS // nx

    def back_product(k):
        w = r.wo[0, k]
        r.gg[:, pl.ds(pl.multiple_of(k * per_x, 128), per_x)] = mm(r.cots[...], w.reshape(per_x, depth), ((1,), (1,)))

    loop(nx, back_product)
    flushes.append(wires.keep(r.gg, r.gg_o))
    loop(chunks, lambda i: phase_carried(r, i))
    flushes += [wires.keep(src, dst) for src, dst in ((r.y, r.y_o), (r.st, r.st_o))]
    wires.finish()
    for flush in flushes:
        flush()


def backward_kernel(size, names, *refs):
    r = named(names, refs)
    here = place()
    a, c, b, s = here
    n, nx = size["so"], size["dpo"]
    mine = 2 * c + s
    own, depth = r.tok.shape
    r.span = span = 2 * own
    rows = r.rest.shape[0]
    halves = r.oo.shape[0]
    lines = span + PAD
    chunks = 2 * span // CHUNK
    per_dp = r.gg_w.shape[1]
    half_cols = [slice(k * XCOLS, (k + 1) * XCOLS) for k in range(2)]
    wires = Wires(r.send, r.recv, r.local)
    fetched = {}
    for name in ("y", "z", "gg", "wo", "run", "idc", "normed", "dtm", "dtr", "wg", "wcx", "wcs"):
        fetched[name] = wires.keep(getattr(r, name + "_i"), getattr(r, name))
    fetched["bc"] = wires.keep(r.act_i.at[:, XCOLS:ACT], r.bc)
    fetched["cots"] = wires.keep(r.cots_i, r.cots.at[0 : 2 * span])
    need = lambda *keys: [fetched.pop(key)() for key in keys]
    follows = (s == 1) & (b + 1 < n)
    next_pair = [(a, c, jnp.minimum(b + 1, n - 1), ss) for ss in range(2)]
    prior = (a, c, jnp.maximum(b - 1, 0), 1)
    met = greet(here, size, [(next_pair, follows), ([prior], b > 0)])
    r.gx = r.z
    r.chosen[...] = class_heads(size, c, s)
    r.nggrad[...] = jnp.zeros(r.nggrad.shape, f32)
    r.tally[...] = jnp.zeros(r.tally.shape, f32)
    r.cvgrad[...] = jnp.zeros(r.cvgrad.shape, f32)
    for q in range(2):
        r.gpc[q * lines : q * lines + PAD, :] = jnp.zeros((PAD, CCOLS), bf16)

    need("y", "z", "gg")
    loop(chunks, lambda i: phase_sums(r, i))
    met()
    slots = {}
    for rel in range(1, 4):
        slots[rel] = wires.slot()
        wires.start(r.sums.at[0], r.sums.at[rel], slots[rel], member(here, rel))
    need("cots", "wo", "bc", "run", "idc")
    for rel in range(1, 4):
        wires.arrived(r.sums.at[rel], slots[rel], member(here, rel))
    loop(chunks, lambda i: phase_gate(r, i))

    def out_grad(k):
        left = r.gated[:, pl.ds(pl.multiple_of(k * per_dp, 128), per_dp)]
        for h, cols in enumerate(half_cols):
            r.go[2 * k + h] = mm(left, r.cots[0 : 2 * span, cols], ((0,), (0,))).astype(bf16)

    loop(nx, out_grad)
    units_o = 2 * halves
    get_o = lambda aa, bb: r.go.at[pl.ds(2 * aa, 2), pl.ds(pl.multiple_of((bb // 2) * units_o, 16), units_o)]
    sends_o = []
    collect_o = collect_out(wires, here, size, get_o, r.xo, r.yo, r.zo, r.oo, sends_o)
    next(collect_o)

    x_copy = lambda i, slot: pltpu.make_async_copy(
        r.act_i.at[pl.ds(pl.multiple_of(i * CHUNK, CHUNK), CHUNK), 0:XCOLS], r.xw.at[slot], r.stream.at[6 + slot]
    )
    x_copy(0, 0).start()

    def states_chunk(i):
        slot = lax.rem(i, 2)

        @pl.when(i + 1 < chunks)
        def _():
            x_copy(i + 1, 1 - slot).start()

        x_copy(i, slot).wait()
        phase_back_states(r, i, r.xw[slot])

    loop(chunks, states_chunk)
    phase_back_chain(r)
    hop = chain(wires, here, size, r, -1)
    hop(0)

    def mix(k):
        tile = pl.ds(pl.multiple_of(k * 256, 256), 256)
        w = r.wo[:, :, :, :, tile]
        r.cots[0 : 2 * span, tile] = mm(r.gated[...], w.reshape(XCOLS, 256)).astype(bf16)

    loop(depth // 256, mix)
    r.xdt = r.gated
    fetched["xdt"] = wires.keep(r.xdt_i, r.xdt)
    m_slots = [wires.slot(), wires.slot()]
    half = lambda cc: pl.ds(pl.multiple_of(cc * span, 16), span)
    m_sent = wires.start(r.cots.at[half(1 - c)], r.t1.at[0:span], m_slots[0], member(here, 2))

    entries = []
    need("xdt")

    def fill_a():
        loop(chunks // 2, lambda i: phase_back_inside(r, i))

    def fill_b():
        wires.arrived(r.t1.at[0:span], m_slots[0], member(here, 2))
        at = pl.ds(pl.multiple_of(own * (1 - s), 16), own)
        r.t1[at, :] = (r.t1[at, :].astype(f32) + r.cots[pl.ds(pl.multiple_of(c * span + own * (1 - s), 16), own), :].astype(f32)).astype(bf16)
        entries.append(wires.start(r.t1.at[at], r.t2, m_slots[1], member(here, 1)))
        loop(chunks, lambda i: phase_back_inside(r, i), chunks // 2)

    fillers = [lambda: None, fill_a, fill_b]
    for h in range(1, n):
        if fillers:
            fillers.pop(0)()
        hop(h)
    for fill in fillers:
        fill()
    for _ in range(n):
        next(collect_o)
    need("normed")

    def gate_grad(k):
        at = pl.ds(pl.multiple_of(k * per_dp, 128), per_dp)
        total = jnp.zeros((per_dp, XCOLS), f32)
        for q in range(2):
            left = r.normed[q * lines + PAD : (q + 1) * lines, at]
            total = total + mm(left, r.gpg[q * span : (q + 1) * span, :], ((0,), (0,)))
        r.gg_w[k] = total.astype(bf16)

    loop(depth // per_dp, gate_grad)
    close_g, wait_g = finish_units(wires, here, rows, r.zg, r.og)
    collect_g = collect(wires, here, size, lambda aa, bb: unit_of(r.gg_w, rows, aa, bb), r.xg, r.zg, close_g)
    next(collect_g)

    need("dtm", "dtr")
    state_copy = lambda i, slot: pltpu.make_async_copy(r.st_i.at[i], r.stw.at[slot], r.stream.at[4 + slot])
    state_copy(0, 0).start()
    x_copy(0, 0).start()

    def close_chunk(i):
        slot = lax.rem(i, 2)

        @pl.when(i + 1 < chunks)
        def _():
            state_copy(i + 1, 1 - slot).start()
            x_copy(i + 1, 1 - slot).start()

        state_copy(i, slot).wait()
        x_copy(i, slot).wait()
        phase_back_close(r, i, r.stw[slot], r.xw[slot])

    quarter = chunks // 4
    for k in range(4):
        loop((k + 1) * quarter, close_chunk, k * quarter)
        if k == 2:
            next(collect_o)
        if k == 3:
            next(collect_g)
    for k in range(2):
        fetched["tok", k] = wires.keep(r.tok.at[:, half_cols[k]], r.gated.at[k * own : (k + 1) * own])
        fetched["cot", k] = wires.keep(r.cot.at[:, half_cols[k]], r.gated.at[(2 + k) * own : (3 + k) * own])
    wide, narrow = XCOLS // 128, 2 * STATE // 128
    stream = r.stream

    def tile_place(k):
        early = k < 2 * wide
        late = k - 2 * wide
        return jnp.where(early, k // wide, late // narrow), jnp.where(early, k % wide, wide + late % narrow)

    def tile_copies(k, slot):
        q, lt = tile_place(k)
        cols = pl.ds(pl.multiple_of(lt * 128, 128), 128)
        top = pl.multiple_of(q * lines + PAD - 8, 8)
        flat = pl.multiple_of(q * span, 16)
        return (
            pltpu.make_async_copy(r.pc_i.at[pl.ds(top, span + 8), cols], r.pcw.at[slot], stream.at[2 * slot]),
            pltpu.make_async_copy(r.sp_i.at[pl.ds(flat, span), cols], r.spw.at[slot], stream.at[2 * slot + 1]),
        )

    for copy in tile_copies(jnp.int32(0), 0):
        copy.start()

    def conv_tiles(q, first, count, grads, lead):
        def conv_tile(k):
            slot = lax.rem(k, 2)

            @pl.when(k + 1 < 2 * (wide + narrow))
            def _():
                for copy in tile_copies(k + 1, 1 - slot):
                    copy.start()

            for copy in tile_copies(k, slot):
                copy.wait()
            lt = k - first
            grad = grads[q * span : (q + 1) * span, pl.ds(pl.multiple_of(lt * 128, 128), 128)]
            phase_back_conv(r, q, lt + lead, grad, r.pcw[slot], r.spw[slot])

        loop(first + count, conv_tile, first)

    conv_tiles(0, 0, wide, r.gx, 0)
    conv_tiles(1, wide, wide, r.gx, 0)
    for _ in range(n - 3):
        next(collect_g)
    for entry in sends_o:
        wires.sent(entry)
    r.gcx = r.go

    def in_grad(k):
        at = pl.ds(pl.multiple_of(k * per_dp, 128), per_dp)
        r.gcx[k] = mm(r.normed[:, at], r.gpc[:, 0:XCOLS], ((0,), (0,))).astype(bf16)

    def rest_grad(k):
        at = pl.ds(pl.multiple_of(k * per_dp, 128), per_dp)
        value = mm(r.normed[:, at], r.gpc[:, XCOLS:CCOLS], ((0,), (0,))).astype(bf16)
        for bb in range(n):
            for ss in range(2):
                first = (2 * bb + ss) * rows
                r.gs[2 * (k % 2) + ss, k // 2, bb] = value[first : first + rows]

    loop(depth // per_dp, in_grad)
    close_x, wait_x = finish_units(wires, here, rows, r.zcx, r.ocx)
    collect_x = collect(wires, here, size, lambda aa, bb: unit_of(r.gcx, rows, aa, bb), r.xcx, r.zcx, close_x)
    next(collect_x)
    next(collect_g)
    conv_tiles(0, 2 * wide, narrow, r.gbc, wide)
    conv_tiles(1, 2 * wide + narrow, narrow, r.gbc, wide)
    loop(depth // per_dp, rest_grad)
    collect_s = collect_shared(wires, here, size, r.gs, r.s1, r.s2, r.s3, r.s4, r.rest)
    next(collect_s)
    next(collect_g)
    next(collect_o)

    need(("tok", 0), ("tok", 1), ("cot", 0), ("cot", 1))
    wires.arrived(r.t2, m_slots[1], member(here, 1))
    here_rows = pl.ds(pl.multiple_of(c * span + own * s, 16), own)
    for k, cols in enumerate(half_cols):
        branch = r.cots[here_rows, cols].astype(f32) + r.t1[pl.ds(pl.multiple_of(own * s, 16), own), cols].astype(f32) + r.t2[:, cols].astype(f32)
        r.t2[:, cols] = (r.gated[k * own : (k + 1) * own, :].astype(f32) + branch).astype(bf16)
    wires.keep(r.t2, r.mixed)()
    wires.sent(m_sent)
    wires.sent(entries[0])
    for k, rel in enumerate((2, 1)):
        pl.semaphore_signal(r.ack.at[k], inc=1, device_id=member(here, rel), device_id_type=MESH)

    need("wg", "wcx", "wcs")
    next(collect_s)

    def normed_grad(k):
        cols = pl.ds(pl.multiple_of(k * per_dp, 128), per_dp)
        for q in range(2):
            value = mm(r.gpc[q * lines : (q + 1) * lines, 0:XCOLS], r.wcx[k], ((1,), (1,)))
            value = value + mm(r.gpc[q * lines : (q + 1) * lines, XCOLS:CCOLS], r.wcs[k], ((1,), (1,)))
            extra = mm(r.gpg[q * span : (q + 1) * span, :], r.wg[k], ((1,), (1,)))
            value = value + jnp.concatenate([jnp.zeros((PAD, per_dp), f32), extra], axis=0)
            r.cots[q * lines : (q + 1) * lines, cols] = value.astype(bf16)

    loop(depth // per_dp, normed_grad)
    next(collect_x)
    next(collect_s)
    t_slots = [wires.slot() for _ in range(4)]
    seq_rows = lambda cc: pl.ds(pl.multiple_of(cc * lines, 16), lines)
    pl.semaphore_wait(r.ack.at[0], 1)
    wires.start(r.cots.at[seq_rows(1 - c)], r.t1, t_slots[0], member(here, 2))
    next(collect_g)
    wires.arrived(r.t1, t_slots[0], member(here, 2))

    def pair_sum(at, count, cols):
        ours = r.cots[pl.ds(pl.multiple_of(c * lines + at, 16), count), cols]
        return ours.astype(f32) + r.t1[pl.ds(pl.multiple_of(at, 16), count), cols].astype(f32)

    tg = r.y
    other = PAD + own * (1 - s)
    for k, cols in enumerate(half_cols):
        tg[k * own : (k + 1) * own, :] = pair_sum(PAD + own * s, own, cols)
        r.t1[pl.ds(pl.multiple_of(other, 16), own), cols] = pair_sum(other, own, cols).astype(bf16)
        r.t1[0:PAD, cols] = pair_sum(0, PAD, cols).astype(bf16)
    pl.semaphore_wait(r.ack.at[1], 1)
    wires.start(r.t1.at[pl.ds(pl.multiple_of(other, 16), own)], r.t2, t_slots[1], member(here, 1))
    for ss in range(2):
        wires.start(r.t1.at[0:PAD], r.th.at[ss], t_slots[2 + ss], prior, (b > 0) & (s == ss))
    next(collect_x)
    next(collect_s)
    wait_g()
    wires.arrived(r.t2, t_slots[1], member(here, 1))
    for ss in range(2):
        wires.arrived(r.th.at[ss], t_slots[2 + ss], next_pair[ss], follows)
    for k, cols in enumerate(half_cols):
        tg[k * own : (k + 1) * own, :] += r.t2[:, cols].astype(f32)

        @pl.when(follows)
        def _():
            tg[(k + 1) * own - PAD : (k + 1) * own, :] += r.th[0, :, cols].astype(f32) + r.th[1, :, cols].astype(f32)

    next(collect_x)
    r.pgrad[...] = jnp.zeros(r.pgrad.shape, f32)

    def final(i):
        at = [pl.ds(pl.multiple_of(k * own + i * 64, 64), 64) for k in range(4)]
        t = [r.gated[at[k], :].astype(f32) for k in range(2)]
        g = [tg[at[k], :] for k in range(2)]
        u = [g[k] * r.gain1[0:1, half_cols[k]] for k in range(2)]
        row = lambda left, right: jnp.sum(left[0] * right[0] + left[1] * right[1], axis=1, keepdims=True) / depth
        scale = lax.rsqrt(row(t, t) + EPSILON)
        tilt = scale * scale * scale * row(u, t)
        for k in range(2):
            tg[at[k], :] = r.gated[at[2 + k], :].astype(f32) + scale * u[k] - t[k] * tilt
            r.pgrad[0:1, half_cols[k]] += jnp.sum(g[k] * t[k] * scale, axis=0, keepdims=True)

    loop(own // 64, final)
    next(collect_x)
    next(collect_s)
    flushes = [wires.keep(tg.at[k * own : (k + 1) * own], r.tgrad.at[:, half_cols[k]]) for k in range(2)]
    sub = iota((8, ACT), 0)
    row5 = jnp.concatenate([r.nggrad[0:1], r.tally[0:1], r.tally[1:2]], axis=1)
    row7 = widened(jnp.concatenate([r.pgrad[0:1, ACT:], r.tally[2:3]], axis=1), 1, ACT)
    r.cvm[...] = r.cvgrad[...] + jnp.where(sub == 5, row5, 0.0) + jnp.where(sub == 6, r.pgrad[0:1, :ACT], 0.0) + jnp.where(sub == 7, row7, 0.0)
    smalls = sum_all(wires, here, size, r.cvm, r.cvz, r.cvx)
    next(smalls)
    pieces = INNER // XCOLS

    def assemble(classes, first):
        for p in range(pieces):
            at = (first + p) * rows
            joined = joined_runs([classes[m].astype(f32) for m in range(4)], size, p * XCOLS, XCOLS)
            r.gg[at : at + rows, :] = joined
            flushes.append(wires.keep(r.gg.at[at : at + rows], r.iw.at[:, (first + p) * XCOLS : (first + p + 1) * XCOLS]))

    assemble(r.og, 0)
    next(smalls)
    for _ in range(n - 4):
        next(collect_x)
    r.os[mine] = next(smalls)
    s_slots = {}
    for rel in range(1, 4):
        s_slots[rel] = wires.slot()
        wires.start(r.os.at[mine], r.os.at[mine], s_slots[rel], member(here, rel))
    next(collect_x)
    for rel in range(1, 4):
        _, cc, _, ss = member(here, rel)
        wires.arrived(r.os.at[2 * cc + ss], s_slots[rel], member(here, rel))
    final_smalls(size, here, r)
    wait_x()
    assemble(r.ocx, pieces)
    wires.finish()
    for flush in flushes:
        flush()


def fast_body(size, tokens, segment_ids, pre_gain, in_weight, conv_weight, conv_bias, dt_bias, a_log, skip_gain, norm_gain, out_weight, cotangent):
    n, nx = size["so"], size["dpo"]
    tok, cot = tokens[0], cotangent[0]
    own, depth = tok.shape
    span = 2 * own
    rows, halves = in_weight.shape[0], out_weight.shape[0]
    chunks = 2 * span // CHUNK
    total, lines = 2 * span, 2 * (span + PAD)
    dps = 2 * nx
    per_dp = 2 * n * rows
    rest = CCOLS - XCOLS

    hbm_state = dict(
        normed=((lines, depth), bf16), pc=((lines, ACT), f32), sp=((total, ACT), f32), act=((total, ACT), f32),
        xdt=((total, XCOLS), bf16), wcx=((dps, per_dp, XCOLS), bf16), wcs=((dps, per_dp, rest), bf16), wg=((dps, per_dp, XCOLS), bf16),
        wo=((nx, n // 2, 2, halves, depth), bf16), cots=((total, depth), bf16), z=((total, XCOLS), f32), gg=((total, XCOLS), f32),
        y=((total, XCOLS), f32), st=((chunks, STATE, XCOLS), f32), dtm=((total, 128), f32), run=((total, 128), f32),
        dtr=((lines, 128), f32), idc=((lines, 128), f32),
    )
    vmem_state = dict(
        fac=((2, 8, XCOLS), f32), pex=((chunks, 8, XCOLS), f32), cv=((8, ACT), f32), ng=((8, XCOLS), f32),
        gain1=((8, depth), f32), hp=((8, 128), f32), hx=((8, XCOLS), f32),
    )
    common = dict(
        cum=((chunks, 8, XCOLS), f32), end=((2, STATE, XCOLS), f32), sin=((2, STATE, XCOLS), f32),
        cin=((4, STATE, XCOLS // 2), bf16), cout=((4, STATE, XCOLS // 2), bf16),
        cvm=((8, ACT), f32), cvz=((n, 8, ACT), f32), cvx=((nx, 8, ACT), f32), chosen=((128, 128), bf16),
    )
    copies = 100 + 12 * n * nx
    semaphores = [pltpu.SemaphoreType.DMA((copies,)), pltpu.SemaphoreType.DMA((copies,)), pltpu.SemaphoreType.DMA((40,))]
    shape = lambda spec: jax.ShapeDtypeStruct(*spec)

    row = lambda v: v[None]
    inputs = dict(
        w_in=in_weight, wo_in=out_weight, tok=tok, cot=cot, idin=segment_ids, conv_w=conv_weight, conv_b=row(conv_bias),
        norm_in=row(norm_gain), pre_in=row(pre_gain), dtb_in=row(dt_bias), alog_in=row(a_log), skip_in=row(skip_gain),
    )
    scratch = dict(hbm_state)
    scratch.update(common)
    scratch.update(
        wo=((2, nx, n // 2, 2, halves, depth), bf16), toks=((lines, depth), bf16), ids=((4, 8, 128), f32), hid=((2, 8, 128), f32),
        cvs=((4, 8, ACT), f32), cvy=((3, 8, ACT), f32), wraw=(in_weight.shape, bf16), wxs=((4, rows, XCOLS), bf16),
        wgs=((4, rows, XCOLS), bf16), wsr=((4, nx, n, rows, rest), bf16),
    )
    names = list(inputs) + [k + "_o" for k in hbm_state] + list(vmem_state) + list(scratch) + ["send", "recv", "local"]
    outs = pl.pallas_call(
        functools.partial(forward_kernel, size, names),
        out_shape=[shape(v) for v in hbm_state.values()] + [shape(v) for v in vmem_state.values()],
        in_specs=[HBM] * 4 + [VMEM] * 8,
        out_specs=[HBM] * len(hbm_state) + [VMEM] * len(vmem_state),
        scratch_shapes=[pltpu.VMEM(*v) for v in scratch.values()] + semaphores,
        compiler_params=pltpu.CompilerParams(collective_id=1, has_side_effects=True, vmem_limit_bytes=64 * 2**20 - 2**16),
    )(*inputs.values())
    held = dict(zip(hbm_state, outs))
    small = dict(zip(vmem_state, outs[len(hbm_state) :]))

    results = dict(
        tgrad=((own, depth), f32), mixed=((own, depth), bf16), iw=((rows, 2 * INNER), f32), rest=((rows, rest), f32),
        oo=((halves, depth), f32), smo=((4, 8, 128), f32), cwo=(conv_weight.shape, f32),
    )
    scratch = {k: v for k, v in hbm_state.items() if k not in ("pc", "sp", "cots", "xdt", "st", "act")}
    scratch.update(common)
    unit, unit_o = (2, 2 * rows, XCOLS), (2, 2 * halves, XCOLS)
    scratch.update(
        cots=((lines, depth), bf16), gbc=((total, 2 * STATE), f32),
        gated=((total, XCOLS), bf16), gpg=((total, XCOLS), bf16), gpc=((lines, CCOLS), bf16), drun=((total, 128), f32),
        sums=((4, chunks, 8, 128), f32), nggrad=((8, XCOLS), f32), tally=((8, 128), f32), cvgrad=((8, ACT), f32),
        pgrad=((8, depth), f32), go=((dps, n * halves, XCOLS), bf16), gg_w=((dps, per_dp, XCOLS), bf16), gs=((4, nx, n, rows, rest), bf16),
        xcx=((nx - 1, n) + unit, bf16), xg=((nx - 1, n) + unit, bf16), xo=((nx - 1, n // 2) + unit_o, bf16),
        zcx=((n - 1,) + unit, bf16), zg=((n - 1,) + unit, bf16), zo=((n - 1, 2, halves, XCOLS), bf16), yo=((n // 2, 2, halves, XCOLS), bf16),
        s1=((2, nx, n, rows, rest), bf16), s2=((nx, n, rows, rest), bf16), s3=((nx - 1, n, rows, rest), bf16), s4=((n - 1, rows, rest), bf16),
        ocx=((4, rows, XCOLS), bf16), og=((4, rows, XCOLS), bf16), os=((4, 8, ACT), f32),
        stw=((2, STATE, XCOLS), f32), xw=((2, CHUNK, XCOLS), f32), bc=((total, 2 * STATE), f32), t1=((span + PAD, depth), bf16),
        t2=((own, depth), bf16), th=((2, PAD, depth), bf16), pcw=((2, span + 8, 128), f32), spw=((2, span, 128), f32),
    )
    names = [k + "_i" for k in hbm_state] + ["tok", "cot"] + list(vmem_state) + list(results) + list(scratch)
    names += ["send", "recv", "local", "stream", "ack"]
    outs = pl.pallas_call(
        functools.partial(backward_kernel, size, names),
        out_shape=[shape(v) for v in results.values()],
        in_specs=[HBM] * (len(hbm_state) + 2) + [VMEM] * len(vmem_state),
        out_specs=[HBM] * 3 + [VMEM] * (len(results) - 3),
        scratch_shapes=[pltpu.VMEM(*v) for v in scratch.values()] + semaphores + [pltpu.SemaphoreType.DMA((8,)), pltpu.SemaphoreType.REGULAR((2,))],
        compiler_params=pltpu.CompilerParams(collective_id=2, has_side_effects=True, vmem_limit_bytes=64 * 2**20 - 2**16),
    )(*held.values(), tok, cot, *small.values())
    out = dict(zip(results, outs))
    smo = out["smo"]
    in_weight_grad = jnp.concatenate([out["iw"], out["rest"][:, : in_weight.shape[1] - 2 * INNER]], axis=1)
    return (
        out["mixed"][None], out["tgrad"][None], smo[2, 0, : pre_gain.shape[0]], in_weight_grad, out["cwo"], smo[0, 4, : conv_bias.shape[0]],
        smo[3, 0, :HEADS], smo[3, 1, :HEADS], smo[3, 2, :HEADS], smo[1, 5, : norm_gain.shape[0]], out["oo"],
    )


def specs(dp, seq):
    both = dp + seq
    ins = (
        P(dp, seq, None), P(dp, seq), P(both), P(both, None), P(both, None), P(both),
        P(), P(), P(), P(both), P(both, None), P(dp, seq, None),
    )
    outs = (
        P(dp, seq, None), P(dp, seq, None), P(both), P(both, None), P(both, None), P(both),
        P(), P(), P(), P(both), P(both, None),
    )
    return ins, outs


def solution(mesh):
    dp, seq = mesh.shape["dp"], mesh.shape["seq"]
    fine = Mesh(mesh.devices.reshape(dp // 2, 2, seq // 2, 2), AXES)
    size = dict(fine.shape)

    def choose(*args):
        ok = args[0].shape[0] == dp and args[0].shape[1] == seq * GROUP and size["so"] % 2 == 0
        ok = ok and INNER % (dp * seq * HEADDIM // 2) == 0 and args[3].shape[0] % (dp * seq * 16) == 0 and HEADS % (dp * seq // 2) == 0 and args[3].shape[0] == 2 * XCOLS
        if ok:
            ins, outs = specs(AXES[:2], AXES[2:])
            return jax.shard_map(functools.partial(fast_body, size), mesh=fine, in_specs=ins, out_specs=outs, check_vma=False)(*args)
        ins, outs = specs(("dp",), ("seq",))
        return jax.shard_map(whole_body, mesh=mesh, in_specs=ins, out_specs=outs, check_vma=False)(*args)

    return choose
```
